32 devices in a mesh: section: 4 (over z), dp: 8 (over y, x, core).
Axes of the slice: x: 2, y: 2, z: 4, core: 2. Of those that a mesh axis runs over, the one named last changes fastest.
Arguments:
- inputs: bfloat16 [4, 8, 256, 1024], P(None, 'dp'), may hold values from -8 to 8
- cotangent: bfloat16 [4, 8, 256, 1024], P(None, 'dp'), may hold values from -6 to 6
- w_qkv: bfloat16 [3, 1024, 2048], P(None, None, 'section'), may hold values from -0.1875 to 0.1875
- w_beta: bfloat16 [1024, 16], P(None, 'section'), may hold values from -0.1875 to 0.1875
- conv_taps: float32 [3, 4, 2048], P(None, None, 'section'), may hold values from -3 to 3
- w_out: bfloat16 [2048, 1024], P('section'), may hold values from -0.1875 to 0.1875
- w_gate_up: bfloat16 [2, 1024, 5632], P(None, None, 'section'), may hold values from -0.1875 to 0.1875
- w_down: bfloat16 [5632, 1024], P('section'), may hold values from -0.109375 to 0.109375
- norm_gains: float32 [2, 2048], P(None, 'section'), may hold values from 0.1 to 1.9
- out_gains: float32 [256], P('section'), may hold values from 0.1 to 1.9
Outputs:
- outputs: bfloat16 [4, 8, 256, 1024], P(None, 'dp', None, 'section')
- input_grad: bfloat16 [4, 8, 256, 1024], P(None, 'dp', None, 'section')
- grad_qkv: float32 [3, 1024, 2048], P(None, 'dp', 'section')
- grad_beta: float32 [1024, 16], P('dp', 'section')
- grad_taps: float32 [3, 4, 2048], P(None, None, ('section', 'dp'))
- grad_out: float32 [2048, 1024], P(('section', 'dp'))
- grad_gate_up: float32 [2, 1024, 5632], P(None, 'dp', 'section')
- grad_down: float32 [5632, 1024], P(('section', 'dp'))
- grad_norm_gains: float32 [2, 2048], P(None, ('section', 'dp'))
- grad_out_gains: float32 [256], P(('section', 'dp'))
The draws below stay inside these ranges and needn't reach their ends.
All inputs are finite; a program needn't handle non-finite values.
Results may differ from the reference program's by a relative error of at most 0.024.
Values may be sent and summed in bfloat16 or wider, within the bound.
No kernel may reach another device: no remote copies, remote signals or barrier semaphores. Data moves between devices by JAX's collectives and lax.ppermute only.
A program may use at most 640 MiB of HBM per device.

```python
import math
import jax
import jax.numpy as jnp
from jax import lax

D = 1024
H = 8
HD = 128
FF = 2816
SPAN = 64
CONV = 4
LAYERS = 2
MB = 4
LEN = 256
SEQS = 8


def with_spikes(result, key, source, target, blocks, factor):
    def block_of(axis_at):
        return (jnp.arange(result.shape[axis_at]) // (result.shape[axis_at] // blocks)).reshape((-1,) + (1,) * (result.ndim - 1 - axis_at))

    near = jax.random.permutation(key, blocks)[block_of(target)]
    other_side = (block_of(target) + blocks // 2) % blocks
    return jnp.where((block_of(source) == near) | (block_of(source) == other_side), factor * result, result)


def levels(rng, shape, cuts, least, top_value):
    factor_of, own = 1.0, jax.random.fold_in(rng, 6)
    for axis_at, blocks in cuts:
        heights = jnp.exp(jax.random.uniform(jax.random.fold_in(own, axis_at), (blocks,), jnp.float32, least / len(cuts), top_value / len(cuts)))
        factor_of = factor_of * jnp.repeat(heights, shape[axis_at] // blocks).reshape([-1 if axis == axis_at else 1 for axis in range(len(shape))])
    return factor_of


def scatter_about(own_key, shape, width, most, split=(), kind=jnp.bfloat16):
    factor_of = levels(own_key, shape, split, -0.22, 0.18) if split else 1.0
    result = jax.random.normal(own_key, shape, jnp.float32) * width * factor_of
    return jnp.minimum(jnp.maximum(result, -most), most).astype(kind)


def heavy_noise(rng, dims, scale, reach, cuts, heavy, kind=jnp.bfloat16):
    entries = scale * jax.random.normal(rng, dims, jnp.float32)
    if cuts:
        entries = entries * levels(rng, dims, cuts, -0.22, 0.18)
    return jnp.clip(with_spikes(entries, jax.random.fold_in(rng, 3), *heavy), -reach, reach).astype(kind)


def setup_inputs(seed: int = 0) -> dict:
    key_of = jax.random.split(jax.random.key(seed), 11)
    inputs = heavy_noise(key_of[0], (MB, SEQS, LEN, D), 1.0, 8.0, ((1, 8),), (1, 3, 8, 2.0))
    cotangent = scatter_about(key_of[1], (MB, SEQS, LEN, D), 1.0, 6.0, ((1, 8),))
    w_qkv = scatter_about(key_of[2], (3, D, LAYERS * D), D ** -0.5, 0.1875, ((2, 4),))
    w_beta = scatter_about(key_of[3], (D, LAYERS * H), D ** -0.5, 0.1875, ((1, 4),))
    conv_taps = scatter_about(key_of[4], (3, CONV, LAYERS * D), CONV ** -0.5, 3.0, ((2, 4),), jnp.float32)
    w_out = scatter_about(key_of[5], (LAYERS * D, D), D ** -0.5, 0.1875, ((0, 4),))
    w_gate_up = scatter_about(key_of[6], (2, D, LAYERS * FF), D ** -0.5, 0.1875, ((2, 4),))
    w_down = scatter_about(key_of[7], (LAYERS * FF, D), FF ** -0.5, 0.109375, ((0, 4),))
    norm_gains = jnp.clip(1.0 + 0.18 * jax.random.normal(key_of[8], (2, LAYERS * D), jnp.float32), 0.1, 1.9)
    out_gains = jnp.clip(1.0 + 0.18 * jax.random.normal(key_of[9], (LAYERS * HD,), jnp.float32), 0.1, 1.9)
    return {"inputs": inputs, "cotangent": cotangent, "w_qkv": w_qkv, "w_beta": w_beta, "conv_taps": conv_taps, "w_out": w_out, "w_gate_up": w_gate_up, "w_down": w_down, "norm_gains": norm_gains, "out_gains": out_gains}


exact_matmul_setting = lax.Precision.HIGHEST

@jax.custom_vjp
def low(v):
    return lax.optimization_barrier(v.astype(jnp.bfloat16)).astype(jnp.float32)

@jax.custom_vjp
def low_back(v):
    return v

def low_keep(v):
    return (low(v), None)

def low_pass(kept, grad):
    return (grad,)

def back_keep(v):
    return (v, None)

def back_low(kept, grad):
    return (low(grad),)
low.defvjp(low_keep, low_pass)
low_back.defvjp(back_keep, back_low)

def product(left, right):
    return jnp.dot(left, right, precision=exact_matmul_setting)

def rms_norm(value, gain, epsilon):
    scale = lax.rsqrt(lax.optimization_barrier(jnp.mean(value * value, axis=-1, keepdims=True)) + epsilon)
    return value * scale * gain

def causal_conv(linear, taps):
    model_width = taps.shape[0]
    length = linear.shape[0]
    extended_by_zeroes = jnp.pad(linear, ((model_width - 1, 0), (0, 0)))
    total = extended_by_zeroes[0:length] * taps[0]
    for offset in range(1, model_width):
        total = total + extended_by_zeroes[offset:offset + length] * taps[offset]
    return total

def unit_rows(value, heads):
    shaped = value.reshape(value.shape[0], heads, -1)
    return shaped * lax.rsqrt(lax.optimization_barrier(jnp.sum(shaped * shaped, axis=-1, keepdims=True)) + 1e-06)

def delta_block(carried_memory_matrix, pieces):
    query_rows, lookup_vector_entries, values, betas = pieces
    size = lookup_vector_entries.shape[1]
    lower = jnp.tril(jnp.ones((size, size), jnp.float32), -1)
    identity = jnp.eye(size, dtype=jnp.float32)
    inner = jnp.einsum('hck,hdk->hcd', lookup_vector_entries, lookup_vector_entries, precision=exact_matmul_setting)
    system = identity + betas[:, :, None] * inner * lower
    right = betas[:, :, None] * jnp.concatenate([values, lookup_vector_entries], axis=-1)
    triangular_result = jax.scipy.linalg.solve_triangular(system, right, lower=True, unit_diagonal=True)
    model_width = values.shape[-1]
    latest_content_vector = triangular_result[..., :model_width] - jnp.einsum('ywj,yje->ywe', triangular_result[..., model_width:], carried_memory_matrix, precision=exact_matmul_setting)
    scores = jnp.einsum('hck,hdk->hcd', query_rows, lookup_vector_entries, precision=exact_matmul_setting) * (lower + identity)
    outputs = jnp.einsum('ywj,yje->ywe', query_rows, carried_memory_matrix, precision=exact_matmul_setting)
    outputs = outputs + jnp.einsum('hcd,hdv->hcv', scores, latest_content_vector, precision=exact_matmul_setting)
    carried_memory_matrix = carried_memory_matrix + jnp.einsum('elp,elk->epk', lookup_vector_entries, latest_content_vector, precision=exact_matmul_setting)
    return (carried_memory_matrix, outputs)

def delta_rule(query_rows, lookup_vector_entries, values, betas, block):
    length, heads, model_width = query_rows.shape
    count = length // block

    def arrange(value):
        return jnp.swapaxes(value.reshape(count, block, heads, -1), 1, 2)
    pieces = (arrange(query_rows), arrange(lookup_vector_entries), arrange(values), arrange(betas[..., None])[..., 0])
    start = jnp.zeros((heads, model_width, model_width), jnp.float32)
    final_state, outputs = lax.scan(jax.checkpoint(delta_block), start, pieces)
    return jnp.swapaxes(outputs, 1, 2).reshape(length, heads, model_width)

def mixer(stream, layer, params):
    w_qkv, w_beta, conv_taps, w_out, w_gate_up, w_down, norm_gains, out_gains = params
    part = slice(layer * D, (layer + 1) * D)
    normed = low(rms_norm(stream, norm_gains[0, part], 1e-06))
    linear = [low_back(product(normed, w_qkv[which][:, part])) for which in range(3)]
    beta_linear = low_back(product(normed, w_beta[:, layer * H:(layer + 1) * H]))
    active = [jax.nn.silu(causal_conv(linear[which], conv_taps[which][:, part])) for which in range(3)]
    query_rows = low(unit_rows(active[0], H))
    lookup_vector_entries = low(unit_rows(active[1], H))
    values = low(active[2].reshape(-1, H, HD))
    betas = jax.nn.sigmoid(beta_linear)
    outputs = delta_rule(query_rows, lookup_vector_entries, values, betas, SPAN)
    normed_out = low(rms_norm(outputs, out_gains[layer * HD:(layer + 1) * HD], 1e-05).reshape(-1, D))
    return stream + low_back(product(normed_out, w_out[part]))

def feed_forward(stream, layer, params):
    w_qkv, w_beta, conv_taps, w_out, w_gate_up, w_down, norm_gains, out_gains = params
    part = slice(layer * D, (layer + 1) * D)
    units = slice(layer * FF, (layer + 1) * FF)
    normed = low(rms_norm(stream, norm_gains[1, part], 1e-06))
    gate = low_back(product(normed, w_gate_up[0][:, units]))
    expansion_branch_output = low_back(product(normed, w_gate_up[1][:, units]))
    hidden = low(jax.nn.silu(gate) * expansion_branch_output)
    return stream + low_back(product(hidden, w_down[units]))

def two_layers(sequence, params):
    stream = sequence
    for layer in range(LAYERS):
        if layer > 0:
            stream = low_back(low(stream))
        stream = mixer(stream, layer, params)
        stream = feed_forward(stream, layer, params)
    return stream

def reference(inputs, cotangent, w_qkv, w_beta, conv_taps, w_out, w_gate_up, w_down, norm_gains, out_gains):
    params = tuple((array.astype(jnp.float32) for array in (w_qkv, w_beta, conv_taps, w_out, w_gate_up, w_down, norm_gains, out_gains)))
    total = MB * SEQS
    group = math.gcd(max(1, 4096 // LEN), total)

    def grouped(value):
        return value.astype(jnp.float32).reshape(total // group, group, LEN, D)

    def forward(streams, weights):

        def one_sequence(sequence):
            return two_layers(sequence, weights)

        def one_group(carry, block):
            return (carry, jax.vmap(one_sequence)(block))
        carried, results = lax.scan(jax.checkpoint(one_group), jnp.zeros((), jnp.float32), streams)
        return results
    results, pullback = jax.vjp(forward, grouped(inputs), params)
    stream_grad, weight_grads = pullback(grouped(cotangent))
    shape = (MB, SEQS, LEN, D)
    return (results.reshape(shape).astype(jnp.bfloat16), stream_grad.reshape(shape).astype(jnp.bfloat16), weight_grads[0], weight_grads[1], weight_grads[2], weight_grads[3], weight_grads[4], weight_grads[5], weight_grads[6], weight_grads[7])
```

```python
import jax
import jax.numpy as jnp
from jax import lax
from jax.experimental import pallas as pl
from jax.experimental.pallas import tpu as pltpu
from jax.sharding import PartitionSpec as P

SPAN = 64
PAIR = 2 * SPAN
LANES = 128
TILE = 512
UNITS = 1408
LOW = jnp.bfloat16
WIDE = jnp.float32
VMEM = 56 * 1024 * 1024


def mm(left, right):
    return lax.dot_general(left, right, (((1,), (0,)), ((), ())), preferred_element_type=WIDE)


def mm_nt(left, right):
    return lax.dot_general(left, right, (((1,), (1,)), ((), ())), preferred_element_type=WIDE)


def mm_tn(left, right):
    return lax.dot_general(left, right, (((0,), (0,)), ((), ())), preferred_element_type=WIDE)


def low(value):
    return value.astype(LOW)


def sigmoid(value):
    return 0.5 * jnp.tanh(0.5 * value) + 0.5


def shift_down(value, steps):
    rows = lax.broadcasted_iota(jnp.int32, value.shape, 0)
    return jnp.where(rows >= steps, pltpu.roll(value, steps, 0), 0.0)


def shift_up(value, steps):
    size = value.shape[0]
    rows = lax.broadcasted_iota(jnp.int32, value.shape, 0)
    return jnp.where(rows < size - steps, pltpu.roll(value, size - steps, 0), 0.0)


def pick_lane(value, lane):
    lanes = lax.broadcasted_iota(jnp.int32, value.shape, 1)
    return jnp.sum(jnp.where(lanes == lane, value, 0.0), axis=1, keepdims=True)


def norm_scale(value, epsilon):
    return lax.rsqrt(jnp.mean(value * value, axis=-1, keepdims=True) + epsilon)


def norm_back(value, gain, grad, epsilon):
    scale = norm_scale(value, epsilon)
    scaled = gain * grad
    inner = jnp.mean(value * scaled, axis=-1, keepdims=True)
    value_grad = scale * (scaled - value * (scale * scale * inner))
    gain_grad = jnp.sum(grad * value * scale, axis=0, keepdims=True)
    return value_grad, gain_grad


def pair_masks():
    rows = lax.broadcasted_iota(jnp.int32, (PAIR, PAIR), 0)
    cols = lax.broadcasted_iota(jnp.int32, (PAIR, PAIR), 1)
    apart = rows ^ cols
    near = apart < SPAN
    return rows, cols, apart, near


def inverse(systems, apart):
    one = (apart == 0).astype(WIDE)
    found = [one - jnp.where(apart == 1, system, 0.0) for system in systems]
    lows = [low(system) for system in systems]
    size = 2
    while size < SPAN:
        level = (apart >= size) & (apart < 2 * size)
        parts = [jnp.where(level, system, jnp.zeros_like(system)) for system in lows]
        heads = [low(item) for item in found]
        steps = [low(mm(head, part)) for head, part in zip(heads, parts)]
        found = [item - mm(step, head) for item, step, head in zip(found, steps, heads)]
        size *= 2
    return found


def conv_silu(linear, taps):
    count = taps.shape[0]
    total = linear * taps[count - 1 : count]
    for back in range(1, count):
        total = total + shift_down(linear, back) * taps[count - 1 - back : count - back]
    return total


def mixer_forward_kernel(
    stream_ref,
    gain_ref,
    w_qkv_ref,
    w_beta_ref,
    taps_ref,
    out_gain_ref,
    w_out_ref,
    middle_ref,
    normed_ref,
    strengths_ref,
    linear_ref,
    out_ref,
    fresh_ref,
    solve_ref,
    states_ref,
    moves_ref,
):
    step = pl.program_id(0)
    length = stream_ref.shape[0]
    spans = length // SPAN
    heads = TILE // LANES

    @pl.when(step == 0)
    def first():
        stream = stream_ref[...].astype(WIDE)
        normed_ref[...] = low(stream * norm_scale(stream, 1e-6) * gain_ref[...])
        strengths_ref[...] = mm(normed_ref[...], w_beta_ref[...])
        middle_ref[...] = stream

    normed = normed_ref[...]
    active = []
    for which in range(3):
        linear = mm(normed, w_qkv_ref[which])
        linear_ref[which] = linear
        total = conv_silu(linear, taps_ref[which])
        active.append(total * sigmoid(total))
    rows, cols, apart, near = pair_masks()
    strict = (rows > cols) & near
    lower = (rows >= cols) & near
    queries, keys, values, betas = [], [], [], []
    for head in range(heads):
        lanes = slice(head * LANES, (head + 1) * LANES)
        query, key = active[0][:, lanes], active[1][:, lanes]
        queries.append(low(query * lax.rsqrt(jnp.sum(query * query, axis=1, keepdims=True) + 1e-6)))
        keys.append(low(key * lax.rsqrt(jnp.sum(key * key, axis=1, keepdims=True) + 1e-6)))
        values.append(low(active[2][:, lanes]))
        betas.append(sigmoid(pick_lane(strengths_ref[...], step * heads + head)))
    cells = [(head, pair) for head in range(heads) for pair in range(length // PAIR)]

    def part(array, pair):
        return array[pair * PAIR : (pair + 1) * PAIR]

    systems = []
    for head, pair in cells:
        key = part(keys[head], pair)
        systems.append(jnp.where(strict, mm_nt(key, key) * part(betas[head], pair), 0.0))
    solved = [low(item) for item in inverse(systems, apart)]
    both = {}
    scores = {}
    for (head, pair), solve in zip(cells, solved):
        solve_ref[head, pair] = solve
        beta = part(betas[head], pair)
        key = part(keys[head], pair)
        right = jnp.concatenate(
            [low(beta * key.astype(WIDE)), low(beta * part(values[head], pair).astype(WIDE))], axis=1
        )
        both[head, pair] = mm(solve, right)
        scores[head, pair] = low(jnp.where(lower, mm_nt(part(queries[head], pair), key), 0.0))

    def span_of(array, span):
        return array[span * SPAN : (span + 1) * SPAN]

    def both_of(head, span):
        return span_of(both[head, span // 2], span % 2)

    states = [[None] * spans for head in range(heads)]
    turns = {}
    for head in range(heads):
        for span in range(spans - 1):
            turns[head, span] = mm_tn(span_of(keys[head], span), low(both_of(head, span)))
    for span in range(1, spans):
        for head in range(heads):
            turn = turns[head, span - 1]
            if span == 1:
                states[head][span] = turn[:, LANES:]
            else:
                before = states[head][span - 1]
                move = low(turn[:, :LANES])
                moves_ref[head, span - 2] = move
                states[head][span] = before + turn[:, LANES:] - mm(move, low(before))
    fresh = {}
    carried = {}
    for head in range(heads):
        for span in range(spans):
            item = both_of(head, span)
            if span == 0:
                fresh[head, span] = low(item[:, LANES:])
                carried[head, span] = jnp.zeros((SPAN, LANES), WIDE)
            else:
                state = low(states[head][span])
                states_ref[head, span - 1] = state
                left = jnp.concatenate([low(item[:, :LANES]), span_of(queries[head], span)], axis=0)
                seen = mm(left, state)
                fresh[head, span] = low(item[:, LANES:] - seen[:SPAN])
                carried[head, span] = seen[SPAN:]
    normed_out = []
    for head in range(heads):
        lanes = slice(head * LANES, (head + 1) * LANES)
        pieces = []
        for pair in range(length // PAIR):
            piece = jnp.concatenate([fresh[head, 2 * pair], fresh[head, 2 * pair + 1]], axis=0)
            fresh_ref[pair * PAIR : (pair + 1) * PAIR, lanes] = piece
            base = jnp.concatenate([carried[head, 2 * pair], carried[head, 2 * pair + 1]], axis=0)
            pieces.append(base + mm(scores[head, pair], piece))
        output = jnp.concatenate(pieces, axis=0)
        out_ref[:, lanes] = output
        normed_out.append(low(output * norm_scale(output, 1e-5) * out_gain_ref[...]))
    middle_ref[...] += mm(jnp.concatenate(normed_out, axis=1), w_out_ref[...])


def whole(shape):
    return pl.BlockSpec(shape, lambda step: (0,) * len(shape))


def params(**extra):
    return pltpu.CompilerParams(dimension_semantics=("arbitrary",), vmem_limit_bytes=VMEM, **extra)


def mixer_forward(stream, gain, w_qkv, w_beta, taps, out_gain, w_out):
    length, width = stream.shape
    inner = w_qkv.shape[2]
    heads = inner // LANES
    spans = length // SPAN
    pairs = length // PAIR
    here = TILE // LANES
    out = jax.ShapeDtypeStruct
    flops = 2 * length * width * inner * 4 + 2 * heads * length * (10 * 128 * 2 + 8 * 128 * 2)
    return pl.pallas_call(
        mixer_forward_kernel,
        name="mixer_forward",
        grid=(inner // TILE,),
        in_specs=[
            whole((length, width)),
            whole((1, width)),
            pl.BlockSpec((3, width, TILE), lambda step: (0, 0, step)),
            whole((width, LANES)),
            pl.BlockSpec((3, taps.shape[1], TILE), lambda step: (0, 0, step)),
            whole((1, LANES)),
            pl.BlockSpec((TILE, width), lambda step: (step, 0)),
        ],
        out_specs=[
            whole((length, width)),
            whole((length, width)),
            whole((length, LANES)),
            pl.BlockSpec((3, length, TILE), lambda step: (0, 0, step)),
            pl.BlockSpec((length, TILE), lambda step: (0, step)),
            pl.BlockSpec((length, TILE), lambda step: (0, step)),
            pl.BlockSpec((here, pairs, PAIR, PAIR), lambda step: (step, 0, 0, 0)),
            pl.BlockSpec((here, spans - 1, LANES, LANES), lambda step: (step, 0, 0, 0)),
            pl.BlockSpec((here, spans - 2, LANES, LANES), lambda step: (step, 0, 0, 0)),
        ],
        out_shape=[
            out((length, width), WIDE),
            out((length, width), LOW),
            out((length, LANES), WIDE),
            out((3, length, inner), WIDE),
            out((length, inner), WIDE),
            out((length, inner), LOW),
            out((heads, pairs, PAIR, PAIR), LOW),
            out((heads, spans - 1, LANES, LANES), LOW),
            out((heads, spans - 2, LANES, LANES), LOW),
        ],
        compiler_params=params(),
        cost_estimate=pl.CostEstimate(flops=flops * 2, bytes_accessed=18 * 2**20, transcendentals=0),
    )(stream, gain, w_qkv, w_beta, taps, out_gain, w_out)


def mixer_backward_kernel(
    stream_ref,
    branch_ref,
    strengths_ref,
    linear_ref,
    out_ref,
    fresh_ref,
    solve_ref,
    states_ref,
    moves_ref,
    gain_ref,
    w_qkv_ref,
    w_beta_ref,
    taps_ref,
    out_gain_ref,
    w_out_ref,
    stream_grad_ref,
    gain_grad_ref,
    branch_low_ref,
    linear_grad_ref,
    strengths_grad_ref,
    normed_out_ref,
    taps_grad_ref,
    out_gain_grad_ref,
    normed_grad_ref,
    strengths_sum_ref,
):
    step = pl.program_id(0)
    steps = pl.num_programs(0)
    length = stream_ref.shape[0]
    spans = length // SPAN
    pairs = length // PAIR
    heads = TILE // LANES

    @pl.when(step == 0)
    def first():
        branch_low_ref[...] = low(branch_ref[...])
        out_gain_grad_ref[...] = jnp.zeros_like(out_gain_grad_ref)
        strengths_sum_ref[...] = jnp.zeros_like(strengths_sum_ref)
        normed_grad_ref[...] = jnp.zeros_like(normed_grad_ref)

    rows, cols, apart, near = pair_masks()
    strict = (rows > cols) & near
    lower = (rows >= cols) & near
    upper_strict = (rows < cols) & near
    upper = (rows <= cols) & near
    cells = [(head, pair) for head in range(heads) for pair in range(pairs)]

    def part(array, pair):
        return array[pair * PAIR : (pair + 1) * PAIR]

    def span_of(array, span):
        return array[span * SPAN : (span + 1) * SPAN]

    normed_out_grad = mm_nt(branch_low_ref[...], w_out_ref[...])
    totals, gates, active = [], [], []
    for which in range(3):
        total = conv_silu(linear_ref[which], taps_ref[which])
        gate = sigmoid(total)
        totals.append(total)
        gates.append(gate)
        active.append(total * gate)
    query_scales, key_scales = [], []
    queries, keys, values, betas, output_grads = [], [], [], [], []
    for head in range(heads):
        lanes = slice(head * LANES, (head + 1) * LANES)
        query, key = active[0][:, lanes], active[1][:, lanes]
        query_scales.append(lax.rsqrt(jnp.sum(query * query, axis=1, keepdims=True) + 1e-6))
        key_scales.append(lax.rsqrt(jnp.sum(key * key, axis=1, keepdims=True) + 1e-6))
        queries.append(low(query * query_scales[head]))
        keys.append(low(key * key_scales[head]))
        values.append(low(active[2][:, lanes]))
        betas.append(sigmoid(pick_lane(strengths_ref[...], step * heads + head)))
        output = out_ref[:, lanes]
        scale = norm_scale(output, 1e-5)
        grad = normed_out_grad[:, lanes]
        normed_out_ref[:, lanes] = low(output * scale * out_gain_ref[...])
        scaled = out_gain_ref[...] * grad
        inner = jnp.mean(output * scaled, axis=1, keepdims=True)
        output_grads.append(low(scale * (scaled - output * (scale * scale * inner))))
        out_gain_grad_ref[...] += jnp.sum(grad * output * scale, axis=0, keepdims=True)
    fresh = [fresh_ref[:, head * LANES : (head + 1) * LANES] for head in range(heads)]

    scores_back, score_grads, score_grads_back = {}, {}, {}
    for head, pair in cells:
        query, key = part(queries[head], pair), part(keys[head], pair)
        grad, new = part(output_grads[head], pair), part(fresh[head], pair)
        scores_back[head, pair] = low(jnp.where(upper, mm_nt(key, query), 0.0))
        score_grads[head, pair] = low(jnp.where(lower, mm_nt(grad, new), 0.0))
        score_grads_back[head, pair] = low(jnp.where(upper, mm_nt(new, grad), 0.0))
    inside, early = {}, {}
    for head, pair in cells:
        inside[head, pair] = mm(scores_back[head, pair], part(output_grads[head], pair))
    for head, pair in cells:
        early[head, pair] = mm_tn(solve_ref[head, pair], low(inside[head, pair]))
    returns = {}
    for head in range(heads):
        for span in range(1, spans):
            beta = span_of(betas[head], span)
            back = low(-beta * span_of(early[head, span // 2], span % 2))
            left = jnp.concatenate([span_of(queries[head], span), span_of(keys[head], span)], axis=0)
            right = jnp.concatenate([span_of(output_grads[head], span), back], axis=0)
            returns[head, span] = mm_tn(left, right)
    state_grads = {}
    for span in range(spans - 2, -1, -1):
        for head in range(heads):
            if span == spans - 2:
                state_grads[head, span] = returns[head, span + 1]
            else:
                after = state_grads[head, span + 1]
                state_grads[head, span] = (
                    after + returns[head, span + 1] - mm_tn(moves_ref[head, span], low(after))
                )
    fresh_add = {}
    for head, pair in cells:
        pieces = []
        for span in (2 * pair, 2 * pair + 1):
            if span == spans - 1:
                pieces.append(jnp.zeros((SPAN, LANES), WIDE))
            else:
                pieces.append(mm(span_of(keys[head], span), low(state_grads[head, span])))
        fresh_add[head, pair] = low(jnp.concatenate(pieces, axis=0))
    lasts, backs = {}, {}
    for head, pair in cells:
        last = early[head, pair] + mm_tn(solve_ref[head, pair], fresh_add[head, pair])
        lasts[head, pair] = last
        backs[head, pair] = part(betas[head], pair) * last
    system_grads, system_grads_back = {}, {}
    for head, pair in cells:
        last, new = low(lasts[head, pair]), part(fresh[head], pair)
        system_grads[head, pair] = low(jnp.where(strict, -mm_nt(last, new), 0.0))
        system_grads_back[head, pair] = low(jnp.where(upper_strict, -mm_nt(new, last), 0.0))
    query_grads, key_grads, beta_grads = [], [], []
    for head in range(heads):
        query_pieces, key_pieces, beta_pieces = [], [], []
        for pair in range(pairs):
            query, key = part(queries[head], pair), part(keys[head], pair)
            beta, new = part(betas[head], pair), part(fresh[head], pair)
            grad = part(output_grads[head], pair)
            stacked = jnp.concatenate(
                [score_grads[head, pair], system_grads[head, pair]], axis=0
            )
            through = mm(stacked, key)
            query_grad = through[:PAIR]
            key_grad = beta * through[PAIR:]
            wide = jnp.concatenate(
                [score_grads_back[head, pair], system_grads_back[head, pair]], axis=1
            )
            tall = jnp.concatenate([query, low(beta * key.astype(WIDE))], axis=0)
            key_grad = key_grad + mm(wide, tall)
            inner = low(jnp.where(strict, mm_nt(key, key), 0.0))
            residual = part(values[head], pair).astype(WIDE) - mm(inner, new)
            back = low(backs[head, pair])
            more_query, more_key, seen = [], [], []
            for local_span in range(2):
                span = 2 * pair + local_span
                new_span = span_of(new, local_span)
                if span == 0:
                    more_query.append(jnp.zeros((SPAN, LANES), WIDE))
                    seen.append(jnp.zeros((SPAN, LANES), WIDE))
                    more_key.append(mm_nt(new_span, low(state_grads[head, span])))
                    continue
                state = states_ref[head, span - 1]
                more_query.append(mm_nt(span_of(grad, local_span), state))
                seen.append(mm(span_of(key, local_span), state))
                taken = -span_of(back, local_span)
                if span == spans - 1:
                    more_key.append(mm_nt(taken, state))
                else:
                    left = jnp.concatenate([new_span, taken], axis=1)
                    right = jnp.concatenate([low(state_grads[head, span]), state], axis=1)
                    more_key.append(mm_nt(left, right))
            residual = residual - jnp.concatenate(seen, axis=0)
            query_pieces.append(query_grad + jnp.concatenate(more_query, axis=0))
            key_pieces.append(key_grad + jnp.concatenate(more_key, axis=0))
            beta_pieces.append(jnp.sum(lasts[head, pair] * residual, axis=1, keepdims=True))
        query_grads.append(jnp.concatenate(query_pieces, axis=0))
        key_grads.append(jnp.concatenate(key_pieces, axis=0))
        beta_grads.append(jnp.concatenate(beta_pieces, axis=0))
    lane_ids = lax.broadcasted_iota(jnp.int32, (length, LANES), 1)
    strengths_sum = strengths_sum_ref[...]
    for head in range(heads):
        beta = betas[head]
        strengths_sum = strengths_sum + jnp.where(
            lane_ids == step * heads + head, beta_grads[head] * beta * (1.0 - beta), 0.0
        )
    strengths_sum_ref[...] = strengths_sum

    active_grads = []
    for grads, scales, source in ((query_grads, query_scales, active[0]), (key_grads, key_scales, active[1])):
        pieces = []
        for head in range(heads):
            lanes = slice(head * LANES, (head + 1) * LANES)
            value, scale, grad = source[:, lanes], scales[head], grads[head]
            inner = jnp.sum(value * grad, axis=1, keepdims=True)
            pieces.append(scale * (grad - value * (scale * scale * inner)))
        active_grads.append(jnp.concatenate(pieces, axis=1))
    active_grads.append(
        jnp.concatenate(
            [jnp.concatenate([backs[head, pair] for pair in range(pairs)], axis=0) for head in range(heads)],
            axis=1,
        )
    )
    normed_grad = normed_grad_ref[...]
    for which in range(3):
        total, gate = totals[which], gates[which]
        total_grad = active_grads[which] * (gate * (1.0 + total * (1.0 - gate)))
        taps = taps_ref[which]
        linear = linear_ref[which]
        count = taps.shape[0]
        linear_grad = total_grad * taps[count - 1 : count]
        taps_grad_ref[which, count - 1 : count] = jnp.sum(total_grad * linear, axis=0, keepdims=True)
        for ahead in range(1, count):
            moved = shift_up(total_grad, ahead)
            place = slice(count - 1 - ahead, count - ahead)
            linear_grad = linear_grad + moved * taps[place]
            taps_grad_ref[which, place] = jnp.sum(moved * linear, axis=0, keepdims=True)
        linear_low = low(linear_grad)
        linear_grad_ref[which] = linear_low
        normed_grad = normed_grad + mm_nt(linear_low, w_qkv_ref[which])
    normed_grad_ref[...] = normed_grad

    @pl.when(step == steps - 1)
    def last_step():
        strengths_low = low(strengths_sum_ref[...])
        strengths_grad_ref[...] = strengths_low
        total = normed_grad_ref[...] + mm_nt(strengths_low, w_beta_ref[...])
        value_grad, gain_grad = norm_back(stream_ref[...].astype(WIDE), gain_ref[...], total, 1e-6)
        stream_grad_ref[...] = low(branch_ref[...] + value_grad)
        gain_grad_ref[...] = gain_grad


def mixer_backward(stream, branch, kept, gain, w_qkv, w_beta, taps, out_gain, w_out):
    strengths, linear, output, fresh, solve, states, moves = kept
    length, width = stream.shape
    inner = w_qkv.shape[2]
    spans = length // SPAN
    pairs = length // PAIR
    here = TILE // LANES
    out = jax.ShapeDtypeStruct
    count = taps.shape[1]
    flops = 2 * length * width * inner * 4 + 4 * inner * length * 128 * 40
    return pl.pallas_call(
        mixer_backward_kernel,
        name="mixer_backward",
        grid=(inner // TILE,),
        in_specs=[
            whole((length, width)),
            whole((length, width)),
            whole((length, LANES)),
            pl.BlockSpec((3, length, TILE), lambda step: (0, 0, step)),
            pl.BlockSpec((length, TILE), lambda step: (0, step)),
            pl.BlockSpec((length, TILE), lambda step: (0, step)),
            pl.BlockSpec((here, pairs, PAIR, PAIR), lambda step: (step, 0, 0, 0)),
            pl.BlockSpec((here, spans - 1, LANES, LANES), lambda step: (step, 0, 0, 0)),
            pl.BlockSpec((here, spans - 2, LANES, LANES), lambda step: (step, 0, 0, 0)),
            whole((1, width)),
            pl.BlockSpec((3, width, TILE), lambda step: (0, 0, step)),
            whole((width, LANES)),
            pl.BlockSpec((3, count, TILE), lambda step: (0, 0, step)),
            whole((1, LANES)),
            pl.BlockSpec((TILE, width), lambda step: (step, 0)),
        ],
        out_specs=[
            whole((length, width)),
            whole((1, width)),
            whole((length, width)),
            pl.BlockSpec((3, length, TILE), lambda step: (0, 0, step)),
            whole((length, LANES)),
            pl.BlockSpec((length, TILE), lambda step: (0, step)),
            pl.BlockSpec((3, count, TILE), lambda step: (0, 0, step)),
            whole((1, LANES)),
        ],
        out_shape=[
            out((length, width), LOW),
            out((1, width), WIDE),
            out((length, width), LOW),
            out((3, length, inner), LOW),
            out((length, LANES), LOW),
            out((length, inner), LOW),
            out((3, count, inner), WIDE),
            out((1, LANES), WIDE),
        ],
        scratch_shapes=[
            pltpu.VMEM((length, width), WIDE),
            pltpu.VMEM((length, LANES), WIDE),
        ],
        compiler_params=params(),
        cost_estimate=pl.CostEstimate(flops=flops * 2, bytes_accessed=20 * 2**20, transcendentals=0),
    )(stream, branch, strengths, linear, output, fresh, solve, states, moves, gain, w_qkv, w_beta, taps, out_gain, w_out)


def feed_forward_kernel(
    middle_ref, gain_ref, w_gate_up_ref, w_down_ref, result_ref, normed_ref, lifted_ref, total_ref
):
    step = pl.program_id(0)

    @pl.when(step == 0)
    def first():
        middle = middle_ref[...]
        normed_ref[...] = low(middle * norm_scale(middle, 1e-6) * gain_ref[...])
        total_ref[...] = middle

    normed = normed_ref[...]
    gate = mm(normed, w_gate_up_ref[0])
    up = mm(normed, w_gate_up_ref[1])
    lifted_ref[0] = low(gate)
    lifted_ref[1] = low(up)
    hidden = low(gate * sigmoid(gate) * up)
    total_ref[...] += mm(hidden, w_down_ref[...])

    @pl.when(step == pl.num_programs(0) - 1)
    def last():
        result_ref[...] = low(total_ref[...])


def feed_forward(middle, gain, w_gate_up, w_down):
    length, width = middle.shape
    units = w_down.shape[0]
    out = jax.ShapeDtypeStruct
    return pl.pallas_call(
        feed_forward_kernel,
        name="feed_forward",
        grid=(units // UNITS,),
        in_specs=[
            whole((length, width)),
            whole((1, width)),
            pl.BlockSpec((2, width, UNITS), lambda step: (0, 0, step)),
            pl.BlockSpec((UNITS, width), lambda step: (step, 0)),
        ],
        out_specs=[
            whole((length, width)),
            whole((length, width)),
            pl.BlockSpec((2, length, UNITS), lambda step: (0, 0, step)),
        ],
        out_shape=[
            out((length, width), LOW),
            out((length, width), LOW),
            out((2, length, units), LOW),
        ],
        scratch_shapes=[pltpu.VMEM((length, width), WIDE)],
        compiler_params=params(),
        cost_estimate=pl.CostEstimate(
            flops=2 * length * width * units * 3, bytes_accessed=24 * 2**20, transcendentals=0
        ),
    )(middle, gain, w_gate_up, w_down)


def feed_backward_kernel(
    middle_ref,
    grad_ref,
    lifted_ref,
    gain_ref,
    w_gate_up_ref,
    w_down_ref,
    middle_grad_ref,
    gain_grad_ref,
    lifted_grad_ref,
    hidden_ref,
    normed_grad_ref,
):
    step = pl.program_id(0)

    @pl.when(step == 0)
    def first():
        normed_grad_ref[...] = jnp.zeros_like(normed_grad_ref)

    hidden_grad = mm_nt(grad_ref[...], w_down_ref[...])
    gate = lifted_ref[0].astype(WIDE)
    up = lifted_ref[1].astype(WIDE)
    open_ = sigmoid(gate)
    silu = gate * open_
    hidden_ref[...] = low(silu * up)
    up_grad = low(hidden_grad * silu)
    gate_grad = low(hidden_grad * up * (open_ + silu * (1.0 - open_)))
    lifted_grad_ref[0] = gate_grad
    lifted_grad_ref[1] = up_grad
    normed_grad_ref[...] += mm_nt(gate_grad, w_gate_up_ref[0]) + mm_nt(up_grad, w_gate_up_ref[1])

    @pl.when(step == pl.num_programs(0) - 1)
    def last():
        value_grad, gain_grad = norm_back(middle_ref[...], gain_ref[...], normed_grad_ref[...], 1e-6)
        middle_grad_ref[...] = grad_ref[...].astype(WIDE) + value_grad
        gain_grad_ref[...] = gain_grad


def feed_backward(middle, grad, lifted, gain, w_gate_up, w_down):
    length, width = middle.shape
    units = w_down.shape[0]
    out = jax.ShapeDtypeStruct
    return pl.pallas_call(
        feed_backward_kernel,
        name="feed_backward",
        grid=(units // UNITS,),
        in_specs=[
            whole((length, width)),
            whole((length, width)),
            pl.BlockSpec((2, length, UNITS), lambda step: (0, 0, step)),
            whole((1, width)),
            pl.BlockSpec((2, width, UNITS), lambda step: (0, 0, step)),
            pl.BlockSpec((UNITS, width), lambda step: (step, 0)),
        ],
        out_specs=[
            whole((length, width)),
            whole((1, width)),
            pl.BlockSpec((2, length, UNITS), lambda step: (0, 0, step)),
            pl.BlockSpec((length, UNITS), lambda step: (0, step)),
        ],
        out_shape=[
            out((length, width), WIDE),
            out((1, width), WIDE),
            out((2, length, units), LOW),
            out((length, units), LOW),
        ],
        scratch_shapes=[pltpu.VMEM((length, width), WIDE)],
        compiler_params=params(),
        cost_estimate=pl.CostEstimate(
            flops=2 * length * width * units * 3, bytes_accessed=28 * 2**20, transcendentals=0
        ),
    )(middle, grad, lifted, gain, w_gate_up, w_down)


def rows_times(left, right):
    return lax.dot_general(left, right, (((0,), (0,)), ((), ())), preferred_element_type=WIDE)


def weight_grads(normed, linear_grad, strengths_grad, normed_out, branch, normed2, lifted_grad, hidden, grad):
    tall = lambda items: jnp.concatenate(items, axis=-2)
    normed, normed2 = tall(normed), tall(normed2)
    linear_grad, lifted_grad = tall(linear_grad), tall(lifted_grad)
    qkv = jnp.stack([rows_times(normed, linear_grad[i]) for i in range(3)])
    gate_up = jnp.stack([rows_times(normed2, lifted_grad[i]) for i in range(2)])
    return (
        low(qkv),
        rows_times(normed, tall(strengths_grad)),
        low(rows_times(tall(normed_out), tall(branch))),
        low(gate_up),
        low(rows_times(tall(hidden), tall(grad))),
    )


def local(
    inputs, cotangent, w_qkv, w_beta, conv_taps, w_out, w_gate_up, w_down, norm_gains, out_gains
):
    batches, unused, length, width = inputs.shape
    place = lax.axis_index("section")
    rank, half = place // 2, place % 2
    me, copies = lax.axis_index("dp"), lax.axis_size("dp")
    per = batches // 2
    layers = lax.axis_size("section") // 2

    def across(value, bit):
        return lax.ppermute(value, "section", [(i, i ^ bit) for i in range(2 * layers)])

    def by_half(own, other, axis):
        return jnp.where(
            half == 0, jnp.concatenate([own, other], axis), jnp.concatenate([other, own], axis)
        )

    def of_partner(value, axis):
        size = value.shape[axis] // copies
        mine = lax.dynamic_slice_in_dim(value, me * size, size, axis)
        return lax.all_gather(across(mine, 1), "dp", axis=axis, tiled=True)

    smalls = [conv_taps, w_beta.astype(WIDE), norm_gains, out_gains]
    packed = across(jnp.concatenate([item.reshape(-1) for item in smalls]), 1)
    others, start = [], 0
    for item in smalls:
        others.append(packed[start : start + item.size].reshape(item.shape))
        start += item.size
    taps = jnp.concatenate([conv_taps, others[0]], 2)
    heads = w_beta.shape[1]
    w_beta = jnp.concatenate([w_beta, low(others[1])], 1)
    w_beta = jnp.pad(w_beta, ((0, 0), (0, LANES - 2 * heads)))
    gains = by_half(norm_gains, others[2], 1)
    out_gain = by_half(out_gains, others[3], 0)[None]
    inner, units = w_out.shape[0], w_down.shape[0]
    w_qkv = jnp.concatenate([w_qkv, of_partner(w_qkv, 1)], 2)
    w_out = jnp.concatenate([w_out, of_partner(w_out, 0)], 0)
    w_gate_up = jnp.concatenate([w_gate_up, of_partner(w_gate_up, 1)], 2)
    w_down = jnp.concatenate([w_down, of_partner(w_down, 0)], 0)

    def forward(stream):
        middle, normed, *kept = mixer_forward(stream, gains[0:1], w_qkv, w_beta, taps, out_gain, w_out)
        result, normed2, lifted = feed_forward(middle, gains[1:2], w_gate_up, w_down)
        return result, (stream, middle, normed, kept, normed2, lifted)

    def backward(grad, saved):
        stream, middle, normed, kept, normed2, lifted = saved
        middle_grad, feed_gain, lifted_grad, hidden = feed_backward(
            middle, grad, lifted, gains[1:2], w_gate_up, w_down
        )
        stream_grad, mix_gain, branch, linear_grad, strengths_grad, normed_out, taps_grad, out_gain_grad = (
            mixer_backward(
                stream, middle_grad, kept, gains[0:1], w_qkv, w_beta, taps, out_gain, w_out
            )
        )
        big = (normed, linear_grad, strengths_grad, normed_out, branch, normed2, lifted_grad, hidden, grad)
        return stream_grad, big, (taps_grad, mix_gain, feed_gain, out_gain_grad)

    def own(value):
        items = lax.dynamic_slice_in_dim(value, half * per, per, 0)
        return [items[i, 0] for i in range(per)]

    up = [(i, i + 2) for i in range(2)]
    down = [(i + 2, i) for i in range(2)]
    saved0, arrived = [], []
    for stream in own(inputs):
        result, saved = forward(stream)
        saved0.append(saved)
        arrived.append(lax.ppermute(result, "section", up))
    saved1, results = [], []
    for stream in arrived:
        result, saved = forward(stream)
        saved1.append(saved)
        results.append(result)
    big1, small1, returned = [], [], []
    for grad, saved in zip(own(cotangent), saved1):
        stream_grad, big, small = backward(grad, saved)
        big1.append(big)
        small1.append(small)
        returned.append(lax.ppermute(stream_grad, "section", down))
    big0, small0, input_grads = [], [], []
    for grad, saved in zip(returned, saved0):
        stream_grad, big, small = backward(grad, saved)
        big0.append(big)
        small0.append(small)
        input_grads.append(stream_grad)

    turned = lambda items: [list(item) for item in zip(*items)]
    grads = lax.cond(
        rank == 0,
        lambda first, second: weight_grads(*first),
        lambda first, second: weight_grads(*second),
        turned(big0),
        turned(big1),
    )
    smalls = [
        sum(jnp.where(rank == 0, a, b) for a, b in zip(first, second))
        for first, second in zip(turned(small0), turned(small1))
    ]
    d_qkv, d_beta, d_out, d_gate_up, d_down = grads
    d_taps, d_mix, d_feed, d_out_gain = smalls

    def total(value, axis, split):
        value = lax.psum_scatter(value, "dp", scatter_dimension=axis, tiled=True)
        size = value.shape[split] // 2
        mine = lax.slice_in_dim(value, 0, size, axis=split)
        theirs = lax.slice_in_dim(value, size, 2 * size, axis=split)
        return mine.astype(WIDE) + across(theirs, 1).astype(WIDE)

    grad_qkv = total(d_qkv, 1, 2)
    grad_gate_up = total(d_gate_up, 1, 2)
    grad_out = total(d_out.reshape(2, inner, width), 1, 0)[0]
    grad_down = total(d_down.reshape(2, units, width), 1, 0)[0]

    d_gains = jnp.concatenate([d_mix, d_feed], 0)
    d_beta = d_beta[:, : 2 * heads]
    flat = [d_taps, d_beta, d_gains, d_out_gain]
    packed = lax.psum(jnp.concatenate([item.reshape(-1) for item in flat]), "dp")
    sums, start = [], 0
    for item in flat:
        sums.append(packed[start : start + item.size].reshape(item.shape))
        start += item.size

    def part(value, axis, size):
        return lax.dynamic_slice_in_dim(value, me * size, size, axis)

    def halves(value, axis):
        size = value.shape[axis] // 2
        return [
            lax.dynamic_slice_in_dim(value, which * size, size, axis) for which in (half, 1 - half)
        ]

    t_size = d_taps.shape[2] // 2 // copies
    pieces = [
        [part(sums[0][:, :, i * inner : (i + 1) * inner], 2, t_size) for i in range(2)],
        [part(sums[1][:, i * heads : (i + 1) * heads], 0, width // copies) for i in range(2)],
        [part(item, 1, width // 2 // copies) for item in halves(sums[2], 1)],
        [part(item, 1, LANES // 2 // copies) for item in halves(sums[3], 1)],
    ]
    sent = across(jnp.concatenate([theirs.reshape(-1) for mine, theirs in pieces]), 1)
    ends, start = [], 0
    for mine, theirs in pieces:
        ends.append(mine + sent[start : start + mine.size].reshape(mine.shape))
        start += mine.size
    grad_taps, grad_beta, grad_gains, grad_out_gains = ends

    held = jnp.stack([jnp.where(rank == 1, a, b) for a, b in zip(results, input_grads)])
    quarter = width // (2 * layers)

    def quarter_of(index):
        return lax.dynamic_slice_in_dim(held, index * quarter, quarter, 2)

    came = [across(quarter_of(place ^ bit), bit) for bit in (1, 2, 3)]
    same = by_half(quarter_of(place), came[0], 0)
    other = by_half(came[1], came[2], 0)
    final_stream = jnp.where(rank == 1, same, other)[:, None]
    final_grad = jnp.where(rank == 0, same, other)[:, None]
    return (
        final_stream,
        final_grad,
        grad_qkv,
        grad_beta,
        grad_taps,
        grad_out,
        grad_gate_up,
        grad_down,
        grad_gains,
        grad_out_gains[0],
    )


def solution(mesh):
    in_specs = (
        P(None, "dp", None, None),
        P(None, "dp", None, None),
        P(None, None, "section"),
        P(None, "section"),
        P(None, None, "section"),
        P("section", None),
        P(None, None, "section"),
        P("section", None),
        P(None, "section"),
        P("section"),
    )
    out_specs = (
        P(None, "dp", None, "section"),
        P(None, "dp", None, "section"),
        P(None, "dp", "section"),
        P("dp", "section"),
        P(None, None, ("section", "dp")),
        P(("section", "dp"), None),
        P(None, "dp", "section"),
        P(("section", "dp"), None),
        P(None, ("section", "dp")),
        P(("section", "dp")),
    )
    return jax.shard_map(local, mesh=mesh, in_specs=in_specs, out_specs=out_specs, check_vma=False)
```

```python
import jax
import jax.numpy as jnp
from jax import lax
from jax.experimental import pallas as pl
from jax.experimental.pallas import tpu as pltpu
from jax.sharding import PartitionSpec as P

SPAN = 64
PAIR = 2 * SPAN
LANES = 128
LOW = jnp.bfloat16
WIDE = jnp.float32
VMEM = 56 * 1024 * 1024


def mm(left, right):
    return lax.dot_general(left, right, (((1,), (0,)), ((), ())), preferred_element_type=WIDE)


def mm_nt(left, right):
    return lax.dot_general(left, right, (((1,), (1,)), ((), ())), preferred_element_type=WIDE)


def mm_tn(left, right):
    return lax.dot_general(left, right, (((0,), (0,)), ((), ())), preferred_element_type=WIDE)


def low(value):
    return value.astype(LOW)


def sigmoid(value):
    return 0.5 * jnp.tanh(0.5 * value) + 0.5


def shift_down(value, steps):
    rows = lax.broadcasted_iota(jnp.int32, value.shape, 0)
    return jnp.where(rows >= steps, pltpu.roll(value, steps, 0), 0.0)


def shift_up(value, steps):
    size = value.shape[0]
    rows = lax.broadcasted_iota(jnp.int32, value.shape, 0)
    return jnp.where(rows < size - steps, pltpu.roll(value, size - steps, 0), 0.0)


def pick_lane(value, lane):
    lanes = lax.broadcasted_iota(jnp.int32, value.shape, 1)
    return jnp.sum(jnp.where(lanes == lane, value, 0.0), axis=1, keepdims=True)


def norm_scale(value, epsilon):
    return lax.rsqrt(jnp.mean(value * value, axis=-1, keepdims=True) + epsilon)


def norm_back(value, gain, grad, epsilon):
    scale = norm_scale(value, epsilon)
    scaled = gain * grad
    inner = jnp.mean(value * scaled, axis=-1, keepdims=True)
    value_grad = scale * (scaled - value * (scale * scale * inner))
    gain_grad = jnp.sum(grad * value * scale, axis=0, keepdims=True)
    return value_grad, gain_grad


def pair_masks():
    rows = lax.broadcasted_iota(jnp.int32, (PAIR, PAIR), 0)
    cols = lax.broadcasted_iota(jnp.int32, (PAIR, PAIR), 1)
    apart = rows ^ cols
    near = apart < SPAN
    return rows, cols, apart, near


def inverse(systems, apart):
    one = (apart == 0).astype(WIDE)
    found = [one - jnp.where(apart == 1, system, 0.0) for system in systems]
    lows = [low(system) for system in systems]
    size = 2
    while size < SPAN:
        level = (apart >= size) & (apart < 2 * size)
        parts = [jnp.where(level, system, jnp.zeros_like(system)) for system in lows]
        heads = [low(item) for item in found]
        steps = [low(mm(head, part)) for head, part in zip(heads, parts)]
        found = [item - mm(step, head) for item, step, head in zip(found, steps, heads)]
        size *= 2
    return found


def conv_silu(linear, taps):
    count = taps.shape[0]
    total = linear * taps[count - 1 : count]
    for back in range(1, count):
        total = total + shift_down(linear, back) * taps[count - 1 - back : count - back]
    return total


def whole(shape):
    return pl.BlockSpec(shape, lambda step, *scalars: (0,) * len(shape))


def tiled(shape, axis):
    return pl.BlockSpec(
        shape, lambda step, *scalars: tuple(step if i == axis else 0 for i in range(len(shape)))
    )


def tiled_old(shape, axis):
    return pl.BlockSpec(
        shape,
        lambda step, info: tuple(step * (1 - info[8]) if i == axis else 0 for i in range(len(shape))),
    )


ANYWHERE = pl.BlockSpec(memory_space=pl.ANY)

DOWN, OUT = 9, 17


def mixer_copies(info_ref, refs, into_qkv, into_out, sems):
    qkv_ref, out_ref, qkv_came, qkv_twin, out_came, out_twin = refs
    rows = qkv_came.shape[1]
    first, second = pl.ds(0, rows), pl.ds(rows, rows)
    pairs = [
        (qkv_ref, into_qkv.at[0]),
        (out_ref, into_out.at[0]),
        (qkv_came, into_qkv.at[1, :, first]),
        (qkv_twin, into_qkv.at[1, :, second]),
    ]
    rows = out_came.shape[0]
    for index, source in enumerate((out_came, out_twin)):
        place = pl.multiple_of(info_ref[OUT + index] * rows, rows)
        pairs.append((source, into_out.at[1, pl.ds(place, rows)]))
    copies = [pltpu.make_async_copy(*pair, sems.at[i]) for i, pair in enumerate(pairs)]
    return copies[0], copies[1], copies[2:4], copies[4:]


def apart_order(info_ref, value_ref, into_ref, first=0):
    size = value_ref.shape[1] // 8
    for index in range(8):
        place = pl.multiple_of(info_ref[first + index] * size, size)
        into_ref[:, index * size : (index + 1) * size] = value_ref[:, pl.ds(place, size)]


def add_from_apart(info_ref, value_ref, into_ref, first=0):
    size = value_ref.shape[1] // 8
    for index in range(8):
        place = pl.ds(pl.multiple_of(info_ref[first + index] * size, size), size)
        into_ref[:, place] += value_ref[:, index * size : (index + 1) * size]


def start_all(step, copies):
    @pl.when(step == 0)
    def begin():
        for copy in copies:
            copy.start()


def wait_all(step, at, copies):
    @pl.when(step == at)
    def wait():
        for copy in copies:
            copy.wait()


def mixer_forward_kernel(
    info_ref,
    after_ref,
    stream_ref,
    gain_ref,
    w_beta_ref,
    taps_ref,
    out_gain_ref,
    qkv_own_ref,
    out_own_ref,
    qkv_came_ref,
    qkv_twin_ref,
    out_came_ref,
    out_twin_ref,
    middle_ref,
    strengths_ref,
    linear_ref,
    out_ref,
    fresh_ref,
    solve_ref,
    states_ref,
    moves_ref,
    normed_ref,
    w_qkv_ref,
    w_out_ref,
    sems,
):
    step = pl.program_id(0)
    length = stream_ref.shape[0]
    spans = length // SPAN
    heads = linear_ref.shape[2] // LANES
    refs = (qkv_own_ref, out_own_ref, qkv_came_ref, qkv_twin_ref, out_came_ref, out_twin_ref)
    own_qkv, own_out, qkv, out = mixer_copies(info_ref, refs, w_qkv_ref, w_out_ref, sems)
    start_all(step, [own_qkv, own_out])

    @pl.when(step == 0)
    def first():
        stream = stream_ref[...].astype(WIDE)
        normed_ref[0] = low(stream * norm_scale(stream, 1e-6) * gain_ref[...])
        apart_order(info_ref, normed_ref.at[0], normed_ref.at[1])
        strengths_ref[...] = mm(normed_ref[0], w_beta_ref[...])
        middle_ref[...] = stream

    normed = normed_ref[step]
    wait_all(step, 0, [own_qkv, own_out])
    wait_all(step, 1, qkv + out)
    start_all(step, qkv + out)
    active = []
    for which in range(3):
        linear = mm(normed, w_qkv_ref[step, which])
        linear_ref[which] = low(linear)
        total = conv_silu(linear, taps_ref[which])
        active.append(total * sigmoid(total))
    rows, cols, apart, near = pair_masks()
    strict = (rows > cols) & near
    lower = (rows >= cols) & near
    queries, keys, values, betas = [], [], [], []
    for head in range(heads):
        lanes = slice(head * LANES, (head + 1) * LANES)
        query, key = active[0][:, lanes], active[1][:, lanes]
        queries.append(low(query * lax.rsqrt(jnp.sum(query * query, axis=1, keepdims=True) + 1e-6)))
        keys.append(low(key * lax.rsqrt(jnp.sum(key * key, axis=1, keepdims=True) + 1e-6)))
        values.append(low(active[2][:, lanes]))
        betas.append(sigmoid(pick_lane(strengths_ref[...], step * heads + head)))
    cells = [(head, pair) for head in range(heads) for pair in range(length // PAIR)]

    def part(array, pair):
        return array[pair * PAIR : (pair + 1) * PAIR]

    systems = []
    for head, pair in cells:
        key = part(keys[head], pair)
        systems.append(jnp.where(strict, mm_nt(key, key) * part(betas[head], pair), 0.0))
    solved = [low(item) for item in inverse(systems, apart)]
    both = {}
    scores = {}
    for (head, pair), solve in zip(cells, solved):
        solve_ref[head, pair] = solve
        beta = part(betas[head], pair)
        key = part(keys[head], pair)
        right = jnp.concatenate(
            [low(beta * key.astype(WIDE)), low(beta * part(values[head], pair).astype(WIDE))], axis=1
        )
        both[head, pair] = mm(solve, right)
        scores[head, pair] = low(jnp.where(lower, mm_nt(part(queries[head], pair), key), 0.0))

    def span_of(array, span):
        return array[span * SPAN : (span + 1) * SPAN]

    def both_of(head, span):
        return span_of(both[head, span // 2], span % 2)

    states = [[None] * spans for head in range(heads)]
    turns = {}
    for head in range(heads):
        for span in range(spans - 1):
            turns[head, span] = mm_tn(span_of(keys[head], span), low(both_of(head, span)))
    for span in range(1, spans):
        for head in range(heads):
            turn = turns[head, span - 1]
            if span == 1:
                states[head][span] = turn[:, LANES:]
            else:
                before = states[head][span - 1]
                move = low(turn[:, :LANES])
                moves_ref[head, span - 2] = move
                states[head][span] = before + turn[:, LANES:] - mm(move, low(before))
    fresh = {}
    carried = {}
    for head in range(heads):
        for span in range(spans):
            item = both_of(head, span)
            if span == 0:
                fresh[head, span] = low(item[:, LANES:])
                carried[head, span] = jnp.zeros((SPAN, LANES), WIDE)
            else:
                state = low(states[head][span])
                states_ref[head, span - 1] = state
                left = jnp.concatenate([low(item[:, :LANES]), span_of(queries[head], span)], axis=0)
                seen = mm(left, state)
                fresh[head, span] = low(item[:, LANES:] - seen[:SPAN])
                carried[head, span] = seen[SPAN:]
    normed_out = []
    for head in range(heads):
        lanes = slice(head * LANES, (head + 1) * LANES)
        pieces = []
        for pair in range(length // PAIR):
            piece = jnp.concatenate([fresh[head, 2 * pair], fresh[head, 2 * pair + 1]], axis=0)
            fresh_ref[pair * PAIR : (pair + 1) * PAIR, lanes] = piece
            base = jnp.concatenate([carried[head, 2 * pair], carried[head, 2 * pair + 1]], axis=0)
            pieces.append(base + mm(scores[head, pair], piece))
        output = jnp.concatenate(pieces, axis=0)
        out_ref[:, lanes] = low(output)
        normed_out.append(low(output * norm_scale(output, 1e-5) * out_gain_ref[...]))
    middle_ref[...] += mm(jnp.concatenate(normed_out, axis=1), w_out_ref[step])


def cost(micros):
    return pl.CostEstimate(flops=int(micros * 1.1e9), bytes_accessed=2**20, transcendentals=0)


def params(**extra):
    return pltpu.CompilerParams(dimension_semantics=("arbitrary",), vmem_limit_bytes=VMEM, **extra)


def mixer_forward(info, after, stream, gain, weights, w_beta, taps, out_gain):
    length, width = stream.shape
    tile = weights[0].shape[2]
    inner = 2 * tile
    heads = inner // LANES
    spans = length // SPAN
    pairs = length // PAIR
    here = tile // LANES
    out = jax.ShapeDtypeStruct
    return pl.pallas_call(
        mixer_forward_kernel,
        name="mixer_forward",
        grid_spec=pltpu.PrefetchScalarGridSpec(
            num_scalar_prefetch=1,
            grid=(2,),
            in_specs=[
                ANYWHERE,
                whole((length, width)),
                whole((1, width)),
                whole((width, LANES)),
                tiled((3, taps.shape[1], tile), 2),
                whole((1, LANES)),
            ]
            + [ANYWHERE] * 6,
            out_specs=[
                whole((length, width)),
                whole((length, LANES)),
                tiled((3, length, tile), 2),
                tiled((length, tile), 1),
                tiled((length, tile), 1),
                tiled((here, pairs, PAIR, PAIR), 0),
                tiled((here, spans - 1, LANES, LANES), 0),
                tiled((here, spans - 2, LANES, LANES), 0),
            ],
            scratch_shapes=[
                pltpu.VMEM((2, length, width), LOW),
                pltpu.VMEM((2, 3, width, tile), LOW),
                pltpu.VMEM((2, tile, width), LOW),
                pltpu.SemaphoreType.DMA((6,)),
            ],
        ),
        out_shape=[
            out((length, width), WIDE),
            out((length, LANES), WIDE),
            out((3, length, inner), LOW),
            out((length, inner), LOW),
            out((length, inner), LOW),
            out((heads, pairs, PAIR, PAIR), LOW),
            out((heads, spans - 1, LANES, LANES), LOW),
            out((heads, spans - 2, LANES, LANES), LOW),
        ],
        compiler_params=params(),
        cost_estimate=cost(14),
    )(info, after, stream, gain, w_beta, taps, out_gain, *weights)


def or_keep(kernel, inputs, outputs, first_kept, in_place=0):
    def either(*refs):
        start = 1 + inputs
        old = refs[start : start + outputs - first_kept]
        rest = refs[start + len(old) :]

        @pl.when(refs[0][8] == 1)
        def compute():
            kernel(*refs[:start], *rest)

        @pl.when(refs[0][8] == 0)
        def keep():
            for source, target in zip(old[: len(old) - in_place], rest[first_kept:outputs]):
                target[...] = source[...]

    return either


def mixer_backward_kernel(
    info_ref,
    after_ref,
    also_ref,
    stream_ref,
    branch_ref,
    strengths_ref,
    linear_ref,
    out_ref,
    fresh_ref,
    solve_ref,
    states_ref,
    moves_ref,
    gain_ref,
    w_beta_ref,
    taps_ref,
    out_gain_ref,
    qkv_own_ref,
    out_own_ref,
    qkv_came_ref,
    qkv_twin_ref,
    out_came_ref,
    out_twin_ref,
    stream_grad_ref,
    gain_grad_ref,
    stack_ref,
    strengths_grad_ref,
    taps_grad_ref,
    out_gain_grad_ref,
    normed_grad_ref,
    strengths_sum_ref,
    branch_low_ref,
    normed_ref,
    w_qkv_ref,
    w_out_ref,
    sems,
):
    step = pl.program_id(0)
    steps = pl.num_programs(0)
    length = stream_ref.shape[0]
    spans = length // SPAN
    pairs = length // PAIR
    tile = stack_ref.shape[2]
    heads = tile // LANES
    refs = (qkv_own_ref, out_own_ref, qkv_came_ref, qkv_twin_ref, out_came_ref, out_twin_ref)
    own_qkv, own_out, qkv, out = mixer_copies(info_ref, refs, w_qkv_ref, w_out_ref, sems)
    start_all(step, [own_out, own_qkv])

    @pl.when(step == 0)
    def first():
        branch_low_ref[...] = low(branch_ref[...])
        stream = stream_ref[...].astype(WIDE)
        normed_ref[...] = low(stream * norm_scale(stream, 1e-6) * gain_ref[...])
        out_gain_grad_ref[...] = jnp.zeros_like(out_gain_grad_ref)
        strengths_sum_ref[...] = jnp.zeros_like(strengths_sum_ref)
        normed_grad_ref[...] = jnp.zeros_like(normed_grad_ref)

    columns = pl.ds(pl.multiple_of(step * tile, tile), tile)
    stack_ref[4] = branch_low_ref[:, columns]
    stack_ref[5] = normed_ref[:, columns]
    rows, cols, apart, near = pair_masks()
    strict = (rows > cols) & near
    lower = (rows >= cols) & near
    upper_strict = (rows < cols) & near
    upper = (rows <= cols) & near
    cells = [(head, pair) for head in range(heads) for pair in range(pairs)]

    def part(array, pair):
        return array[pair * PAIR : (pair + 1) * PAIR]

    def span_of(array, span):
        return array[span * SPAN : (span + 1) * SPAN]

    wait_all(step, 0, [own_out, own_qkv])
    wait_all(step, 1, out + qkv)
    start_all(step, out + qkv)
    normed_out_grad = mm_nt(branch_low_ref[...], w_out_ref[step])
    totals, gates, active = [], [], []
    for which in range(3):
        total = conv_silu(linear_ref[which].astype(WIDE), taps_ref[which])
        gate = sigmoid(total)
        totals.append(total)
        gates.append(gate)
        active.append(total * gate)
    query_scales, key_scales = [], []
    queries, keys, values, betas, output_grads = [], [], [], [], []
    for head in range(heads):
        lanes = slice(head * LANES, (head + 1) * LANES)
        query, key = active[0][:, lanes], active[1][:, lanes]
        query_scales.append(lax.rsqrt(jnp.sum(query * query, axis=1, keepdims=True) + 1e-6))
        key_scales.append(lax.rsqrt(jnp.sum(key * key, axis=1, keepdims=True) + 1e-6))
        queries.append(low(query * query_scales[head]))
        keys.append(low(key * key_scales[head]))
        values.append(low(active[2][:, lanes]))
        betas.append(sigmoid(pick_lane(strengths_ref[...], step * heads + head)))
        output = out_ref[:, lanes].astype(WIDE)
        scale = norm_scale(output, 1e-5)
        grad = normed_out_grad[:, lanes]
        stack_ref[3, :, lanes] = low(output * scale * out_gain_ref[...])
        scaled = out_gain_ref[...] * grad
        inner = jnp.mean(output * scaled, axis=1, keepdims=True)
        output_grads.append(low(scale * (scaled - output * (scale * scale * inner))))
        out_gain_grad_ref[...] += jnp.sum(grad * output * scale, axis=0, keepdims=True)
    fresh = [fresh_ref[:, head * LANES : (head + 1) * LANES] for head in range(heads)]

    scores_back, score_grads, score_grads_back = {}, {}, {}
    for head, pair in cells:
        query, key = part(queries[head], pair), part(keys[head], pair)
        grad, new = part(output_grads[head], pair), part(fresh[head], pair)
        scores_back[head, pair] = low(jnp.where(upper, mm_nt(key, query), 0.0))
        score_grads[head, pair] = low(jnp.where(lower, mm_nt(grad, new), 0.0))
        score_grads_back[head, pair] = low(jnp.where(upper, mm_nt(new, grad), 0.0))
    inside, early = {}, {}
    for head, pair in cells:
        inside[head, pair] = mm(scores_back[head, pair], part(output_grads[head], pair))
    for head, pair in cells:
        early[head, pair] = mm_tn(solve_ref[head, pair], low(inside[head, pair]))
    returns = {}
    for head in range(heads):
        for span in range(1, spans):
            beta = span_of(betas[head], span)
            back = low(-beta * span_of(early[head, span // 2], span % 2))
            left = jnp.concatenate([span_of(queries[head], span), span_of(keys[head], span)], axis=0)
            right = jnp.concatenate([span_of(output_grads[head], span), back], axis=0)
            returns[head, span] = mm_tn(left, right)
    state_grads = {}
    for span in range(spans - 2, -1, -1):
        for head in range(heads):
            if span == spans - 2:
                state_grads[head, span] = returns[head, span + 1]
            else:
                after = state_grads[head, span + 1]
                state_grads[head, span] = (
                    after + returns[head, span + 1] - mm_tn(moves_ref[head, span], low(after))
                )
    fresh_add = {}
    for head, pair in cells:
        pieces = []
        for span in (2 * pair, 2 * pair + 1):
            if span == spans - 1:
                pieces.append(jnp.zeros((SPAN, LANES), WIDE))
            else:
                pieces.append(mm(span_of(keys[head], span), low(state_grads[head, span])))
        fresh_add[head, pair] = low(jnp.concatenate(pieces, axis=0))
    lasts, backs = {}, {}
    for head, pair in cells:
        last = early[head, pair] + mm_tn(solve_ref[head, pair], fresh_add[head, pair])
        lasts[head, pair] = last
        backs[head, pair] = part(betas[head], pair) * last
    system_grads, system_grads_back = {}, {}
    for head, pair in cells:
        last, new = low(lasts[head, pair]), part(fresh[head], pair)
        system_grads[head, pair] = low(jnp.where(strict, -mm_nt(last, new), 0.0))
        system_grads_back[head, pair] = low(jnp.where(upper_strict, -mm_nt(new, last), 0.0))
    query_grads, key_grads, beta_grads = [], [], []
    for head in range(heads):
        query_pieces, key_pieces, beta_pieces = [], [], []
        for pair in range(pairs):
            query, key = part(queries[head], pair), part(keys[head], pair)
            beta, new = part(betas[head], pair), part(fresh[head], pair)
            grad = part(output_grads[head], pair)
            stacked = jnp.concatenate(
                [score_grads[head, pair], system_grads[head, pair]], axis=0
            )
            through = mm(stacked, key)
            query_grad = through[:PAIR]
            key_grad = beta * through[PAIR:]
            wide = jnp.concatenate(
                [score_grads_back[head, pair], system_grads_back[head, pair]], axis=1
            )
            tall = jnp.concatenate([query, low(beta * key.astype(WIDE))], axis=0)
            key_grad = key_grad + mm(wide, tall)
            inner = low(jnp.where(strict, mm_nt(key, key), 0.0))
            residual = part(values[head], pair).astype(WIDE) - mm(inner, new)
            back = low(backs[head, pair])
            more_query, more_key, seen = [], [], []
            for local_span in range(2):
                span = 2 * pair + local_span
                new_span = span_of(new, local_span)
                if span == 0:
                    more_query.append(jnp.zeros((SPAN, LANES), WIDE))
                    seen.append(jnp.zeros((SPAN, LANES), WIDE))
                    more_key.append(mm_nt(new_span, low(state_grads[head, span])))
                    continue
                state = states_ref[head, span - 1]
                more_query.append(mm_nt(span_of(grad, local_span), state))
                seen.append(mm(span_of(key, local_span), state))
                taken = -span_of(back, local_span)
                if span == spans - 1:
                    more_key.append(mm_nt(taken, state))
                else:
                    left = jnp.concatenate([new_span, taken], axis=1)
                    right = jnp.concatenate([low(state_grads[head, span]), state], axis=1)
                    more_key.append(mm_nt(left, right))
            residual = residual - jnp.concatenate(seen, axis=0)
            query_pieces.append(query_grad + jnp.concatenate(more_query, axis=0))
            key_pieces.append(key_grad + jnp.concatenate(more_key, axis=0))
            beta_pieces.append(jnp.sum(lasts[head, pair] * residual, axis=1, keepdims=True))
        query_grads.append(jnp.concatenate(query_pieces, axis=0))
        key_grads.append(jnp.concatenate(key_pieces, axis=0))
        beta_grads.append(jnp.concatenate(beta_pieces, axis=0))
    lane_ids = lax.broadcasted_iota(jnp.int32, (length, LANES), 1)
    strengths_sum = strengths_sum_ref[...]
    for head in range(heads):
        beta = betas[head]
        strengths_sum = strengths_sum + jnp.where(
            lane_ids == step * heads + head, beta_grads[head] * beta * (1.0 - beta), 0.0
        )
    strengths_sum_ref[...] = strengths_sum

    active_grads = []
    for grads, scales, source in ((query_grads, query_scales, active[0]), (key_grads, key_scales, active[1])):
        pieces = []
        for head in range(heads):
            lanes = slice(head * LANES, (head + 1) * LANES)
            value, scale, grad = source[:, lanes], scales[head], grads[head]
            inner = jnp.sum(value * grad, axis=1, keepdims=True)
            pieces.append(scale * (grad - value * (scale * scale * inner)))
        active_grads.append(jnp.concatenate(pieces, axis=1))
    active_grads.append(
        jnp.concatenate(
            [jnp.concatenate([backs[head, pair] for pair in range(pairs)], axis=0) for head in range(heads)],
            axis=1,
        )
    )
    normed_grad = normed_grad_ref[step]
    for which in range(3):
        total, gate = totals[which], gates[which]
        total_grad = active_grads[which] * (gate * (1.0 + total * (1.0 - gate)))
        taps = taps_ref[which]
        linear = linear_ref[which].astype(WIDE)
        count = taps.shape[0]
        linear_grad = total_grad * taps[count - 1 : count]
        taps_grad_ref[which, count - 1 : count] = jnp.sum(total_grad * linear, axis=0, keepdims=True)
        for ahead in range(1, count):
            moved = shift_up(total_grad, ahead)
            place = slice(count - 1 - ahead, count - ahead)
            linear_grad = linear_grad + moved * taps[place]
            taps_grad_ref[which, place] = jnp.sum(moved * linear, axis=0, keepdims=True)
        linear_low = low(linear_grad)
        stack_ref[which] = linear_low
        normed_grad = normed_grad + mm_nt(linear_low, w_qkv_ref[step, which])
    normed_grad_ref[step] = normed_grad

    @pl.when(step == steps - 1)
    def last_step():
        strengths_low = low(strengths_sum_ref[...])
        strengths_grad_ref[...] = strengths_low
        add_from_apart(info_ref, normed_grad_ref.at[1], normed_grad_ref.at[0])
        total = normed_grad_ref[0] + mm_nt(strengths_low, w_beta_ref[...])
        value_grad, gain_grad = norm_back(stream_ref[...].astype(WIDE), gain_ref[...], total, 1e-6)
        stream_grad_ref[...] = low(branch_ref[...] + value_grad)
        gain_grad_ref[...] = gain_grad


def mixer_backward(info, after, stream, branch, kept, gain, weights, w_beta, taps, out_gain, old=None):
    strengths, linear, output, fresh, solve, states, moves = kept
    length, width = stream.shape
    tile = weights[0].shape[2]
    inner = 2 * tile
    spans = length // SPAN
    pairs = length // PAIR
    here = tile // LANES
    out = jax.ShapeDtypeStruct
    count = taps.shape[1]
    in_specs = [
        ANYWHERE,
        ANYWHERE,
        whole((length, width)),
        whole((length, width)),
        whole((length, LANES)),
        tiled((3, length, tile), 2),
        tiled((length, tile), 1),
        tiled((length, tile), 1),
        tiled((here, pairs, PAIR, PAIR), 0),
        tiled((here, spans - 1, LANES, LANES), 0),
        tiled((here, spans - 2, LANES, LANES), 0),
        whole((1, width)),
        whole((width, LANES)),
        tiled((3, count, tile), 2),
        whole((1, LANES)),
    ] + [ANYWHERE] * 6
    kernel, more = mixer_backward_kernel, []
    if old is not None:
        more = old[1:]
        kernel = or_keep(kernel, len(in_specs), 6, 1)
        in_specs = in_specs + [
            whole((1, width)),
            tiled_old((6, length, tile), 2),
            whole((length, LANES)),
            tiled_old((3, count, tile), 2),
            whole((1, LANES)),
        ]
    return pl.pallas_call(
        kernel,
        name="mixer_backward",
        grid_spec=pltpu.PrefetchScalarGridSpec(
            num_scalar_prefetch=1,
            grid=(2,),
            in_specs=in_specs,
            out_specs=[
                whole((length, width)),
                whole((1, width)),
                tiled((6, length, tile), 2),
                whole((length, LANES)),
                tiled((3, count, tile), 2),
                whole((1, LANES)),
            ],
            scratch_shapes=[
                pltpu.VMEM((2, length, width), WIDE),
                pltpu.VMEM((length, LANES), WIDE),
                pltpu.VMEM((length, width), LOW),
                pltpu.VMEM((length, width), LOW),
                pltpu.VMEM((2, 3, width, tile), LOW),
                pltpu.VMEM((2, tile, width), LOW),
                pltpu.SemaphoreType.DMA((6,)),
            ],
        ),
        out_shape=[
            out((length, width), LOW),
            out((1, width), WIDE),
            out((6, length, inner), LOW),
            out((length, LANES), LOW),
            out((3, count, inner), WIDE),
            out((1, LANES), WIDE),
        ],
        compiler_params=params(),
        cost_estimate=cost(20),
    )(
        info, *after, stream, branch, strengths, linear, output, fresh, solve, states, moves,
        gain, w_beta, taps, out_gain, *weights, *more,
    )


def unit_tiles(units):
    count = -(-units // 512)
    size = -(-units // count // LANES) * LANES
    return [(start, min(size, units - start)) for start in range(0, units, size)]


def feed_tiles(refs, into_lift, into_down, sems):
    lift_ref, down_ref, lift_came, lift_twin, down_came, down_twin = refs
    tiles, at = [], 0
    for which in range(2):
        for start, size in unit_tiles(down_ref.shape[0]):
            span = pl.ds(start, size)
            if which == 0:
                lift = [(lift_ref.at[:, :, span], into_lift.at[0, :, :, span])]
                down = [(down_ref.at[span], into_down.at[0, span])]
            else:
                rows, columns = lift_came.shape[1], down_came.shape[1]
                lift = [
                    (lift_came.at[:, :, span], into_lift.at[1, :, pl.ds(0, rows), span]),
                    (lift_twin.at[:, :, span], into_lift.at[1, :, pl.ds(rows, rows), span]),
                ]
                down = [
                    (down_came.at[span], into_down.at[1, span, pl.ds(0, columns)]),
                    (down_twin.at[span], into_down.at[1, span, pl.ds(columns, columns)]),
                ]
            copies = []
            for group in (lift, down):
                copies.append([pltpu.make_async_copy(*pair, sems.at[at + i]) for i, pair in enumerate(group)])
                at += len(group)
            tiles.append((which, start, size, copies[0], copies[1]))
    return tiles


def start_each(copies):
    for copy in copies:
        copy.start()


def wait_each(copies):
    for copy in copies:
        copy.wait()


AHEAD = 3


def feed_forward_kernel(
    info_ref,
    middle_ref,
    gain_ref,
    lift_own_ref,
    down_own_ref,
    lift_came_ref,
    lift_twin_ref,
    down_came_ref,
    down_twin_ref,
    result_ref,
    lifted_ref,
    total_ref,
    normed_ref,
    w_gate_up_ref,
    w_down_ref,
    kept_ref,
    sems,
    out_sems,
):
    units = down_own_ref.shape[0]
    refs = (lift_own_ref, down_own_ref, lift_came_ref, lift_twin_ref, down_came_ref, down_twin_ref)
    tiles = feed_tiles(refs, w_gate_up_ref, w_down_ref, sems)
    for tile in tiles[:AHEAD]:
        start_each(tile[3] + tile[4])
    middle = middle_ref[...]
    normed_ref[0] = low(middle * norm_scale(middle, 1e-6) * gain_ref[...])
    apart_order(info_ref, normed_ref.at[0], normed_ref.at[1])
    outs = []
    lifted = []
    for index in range(len(tiles) + 1):
        if index < len(tiles):
            which, start, size, lift, down = tiles[index]
            wait_each(lift)
        if index:
            wait_each(tiles[index - 1][4])
        if 0 < index <= len(tiles) - AHEAD:
            start_each(tiles[index + AHEAD - 1][3] + tiles[index + AHEAD - 1][4])
        if index < len(tiles):
            span = pl.ds(start, size)
            normed = normed_ref[which]
            gate = mm(normed, w_gate_up_ref[which, 0, :, span])
            up = mm(normed, w_gate_up_ref[which, 1, :, span])
            place = pl.ds(which * units + start, size)
            kept_ref[0, :, place] = low(gate)
            kept_ref[1, :, place] = low(up)
            lifted.append((gate, up))
        if index:
            which, start, size, lift, down = tiles[index - 1]
            span = pl.ds(start, size)
            place = pl.ds(which * units + start, size)
            outs.append(
                pltpu.make_async_copy(
                    kept_ref.at[:, :, place], lifted_ref.at[:, :, place], out_sems.at[index - 1]
                )
            )
            outs[-1].start()
            gate, up = lifted[index - 1]
            hidden = low(gate * sigmoid(gate) * up)
            part = mm(hidden, w_down_ref[which, span, :])
            if start:
                total_ref[which] += part
            else:
                total_ref[which] = part + middle if which == 0 else part
    add_from_apart(info_ref, total_ref.at[1], total_ref.at[0], DOWN)
    result_ref[...] = low(total_ref[0])
    wait_each(outs)


def feed_forward(info, middle, gain, weights):
    length, width = middle.shape
    units = weights[1].shape[0]
    count = 2 * len(unit_tiles(units))
    out = jax.ShapeDtypeStruct
    return pl.pallas_call(
        feed_forward_kernel,
        name="feed_forward",
        grid_spec=pltpu.PrefetchScalarGridSpec(
            num_scalar_prefetch=1,
            grid=(1,),
            in_specs=[whole((length, width)), whole((1, width))] + [ANYWHERE] * 6,
            out_specs=[whole((length, width)), ANYWHERE],
            scratch_shapes=[
                pltpu.VMEM((2, length, width), WIDE),
                pltpu.VMEM((2, length, width), LOW),
                pltpu.VMEM((2, 2, width, units), LOW),
                pltpu.VMEM((2, units, width), LOW),
                pltpu.VMEM((2, length, 2 * units), LOW),
                pltpu.SemaphoreType.DMA((3 * count,)),
                pltpu.SemaphoreType.DMA((count,)),
            ],
        ),
        out_shape=[out((length, width), LOW), out((2, length, 2 * units), LOW)],
        compiler_params=params(),
        cost_estimate=cost(10),
    )(info, middle, gain, *weights)


def feed_backward_kernel(
    info_ref,
    after_ref,
    middle_ref,
    grad_ref,
    gain_ref,
    lifted_ref,
    lift_own_ref,
    down_own_ref,
    lift_came_ref,
    lift_twin_ref,
    down_came_ref,
    down_twin_ref,
    middle_grad_ref,
    gain_grad_ref,
    stack_ref,
    normed_grad_ref,
    grads_ref,
    w_gate_up_ref,
    w_down_ref,
    kept_ref,
    made_ref,
    sems,
    in_sems,
    out_sems,
):
    width = middle_ref.shape[1]
    units = down_own_ref.shape[0]
    refs = (lift_own_ref, down_own_ref, lift_came_ref, lift_twin_ref, down_came_ref, down_twin_ref)
    tiles = feed_tiles(refs, w_gate_up_ref, w_down_ref, sems)
    ins, outs = [], []
    for index, (which, start, size, lift, down) in enumerate(tiles):
        place = pl.ds(which * units + start, size)
        ins.append(pltpu.make_async_copy(lifted_ref.at[:, :, place], kept_ref.at[:, :, place], in_sems.at[index]))
        outs.append(
            pltpu.make_async_copy(
                made_ref.at[pl.ds(0, 3), :, place], stack_ref.at[pl.ds(0, 3), :, place], out_sems.at[index]
            )
        )
    for index in range(AHEAD):
        start_each(tiles[index][4] + [ins[index]] + tiles[index][3])
    middle = middle_ref[...]
    made_ref[3] = jnp.zeros(made_ref.shape[1:], LOW)
    made_ref[3, :, :width] = low(middle * norm_scale(middle, 1e-6) * gain_ref[...])
    made_ref[3, :, units : units + width] = grad_ref[...]
    ends = pltpu.make_async_copy(made_ref.at[3], stack_ref.at[3], out_sems.at[len(tiles)])
    ends.start()
    grads_ref[0] = grad_ref[...]
    apart_order(info_ref, grads_ref.at[0], grads_ref.at[1], DOWN)
    hidden_grads = []
    for index in range(len(tiles) + 1):
        if index < len(tiles):
            which, start, size, lift, down = tiles[index]
            wait_each(down)
        if index:
            ins[index - 1].wait()
            wait_each(tiles[index - 1][3])
        if 0 < index <= len(tiles) - AHEAD:
            more = index + AHEAD - 1
            start_each(tiles[more][4] + [ins[more]] + tiles[more][3])
        if index < len(tiles):
            span = pl.ds(start, size)
            hidden_grads.append(mm_nt(grads_ref[which], w_down_ref[which, span, :]))
        if index:
            which, start, size, lift, down = tiles[index - 1]
            span = pl.ds(start, size)
            place = pl.ds(which * units + start, size)
            hidden_grad = hidden_grads[index - 1]
            gate = kept_ref[0, :, place].astype(WIDE)
            up = kept_ref[1, :, place].astype(WIDE)
            open_ = sigmoid(gate)
            silu = gate * open_
            up_grad = low(hidden_grad * silu)
            gate_grad = low(hidden_grad * up * (open_ + silu * (1.0 - open_)))
            made_ref[0, :, place] = gate_grad
            made_ref[1, :, place] = up_grad
            made_ref[2, :, place] = low(silu * up)
            outs[index - 1].start()
            part = mm_nt(gate_grad, w_gate_up_ref[which, 0, :, span]) + mm_nt(
                up_grad, w_gate_up_ref[which, 1, :, span]
            )
            if start:
                normed_grad_ref[which] += part
            else:
                normed_grad_ref[which] = part
    add_from_apart(info_ref, normed_grad_ref.at[1], normed_grad_ref.at[0])
    value_grad, gain_grad = norm_back(middle, gain_ref[...], normed_grad_ref[0], 1e-6)
    middle_grad_ref[...] = grad_ref[...].astype(WIDE) + value_grad
    gain_grad_ref[...] = gain_grad
    wait_each(outs)
    ends.wait()


def feed_backward(info, after, middle, grad, lifted, gain, weights, old=None):
    length, width = middle.shape
    units = weights[1].shape[0]
    count = 2 * len(unit_tiles(units))
    out = jax.ShapeDtypeStruct
    in_specs = [ANYWHERE, whole((length, width)), whole((length, width)), whole((1, width))] + [ANYWHERE] * 7
    kernel, more, aliases = feed_backward_kernel, [], {}
    if old is not None:
        more = old[1:]
        kernel = or_keep(kernel, len(in_specs), 3, 1, 1)
        in_specs = in_specs + [whole((1, width)), ANYWHERE]
        aliases = {len(in_specs): 2}
    return pl.pallas_call(
        kernel,
        name="feed_backward",
        grid_spec=pltpu.PrefetchScalarGridSpec(
            num_scalar_prefetch=1,
            grid=(1,),
            in_specs=in_specs,
            out_specs=[whole((length, width)), whole((1, width)), ANYWHERE],
            scratch_shapes=[
                pltpu.VMEM((2, length, width), WIDE),
                pltpu.VMEM((2, length, width), LOW),
                pltpu.VMEM((2, 2, width, units), LOW),
                pltpu.VMEM((2, units, width), LOW),
                pltpu.VMEM((2, length, 2 * units), LOW),
                pltpu.VMEM((4, length, 2 * units), LOW),
                pltpu.SemaphoreType.DMA((3 * count,)),
                pltpu.SemaphoreType.DMA((count,)),
                pltpu.SemaphoreType.DMA((count + 1,)),
            ],
        ),
        out_shape=[
            out((length, width), WIDE),
            out((1, width), WIDE),
            out((4, length, 2 * units), LOW),
        ],
        input_output_aliases=aliases,
        compiler_params=params(),
        cost_estimate=cost(13),
    )(info, after, middle, grad, gain, lifted, *weights, *more)


def rows_kernel(halves, width, count, info_ref, after_ref, *refs):
    lefts, rights = refs[:count], refs[count : 2 * count]
    keep_ref, send_ref, turned_ref, rows_ref = refs[2 * count :]
    size = width // halves // 8

    @pl.when((pl.program_id(0) == 0) & (pl.program_id(1) == 0))
    def first():
        for item in range(count):
            turned_ref[item] = lefts[item][:, :width].T
            place = 0
            for which in range(halves):
                for index in (0, 2, 1, 3):
                    start = which * (width // halves) + info_ref[index] * size
                    source = pl.ds(pl.multiple_of(start, size), size)
                    rows_ref[item, place : place + size, :] = turned_ref[item, source, :]
                    place += size

    tile = keep_ref.shape[1]
    if rights[0].shape[1] == tile:
        pieces = [right[...] for right in rights]
    else:
        columns = pl.ds(pl.multiple_of(pl.program_id(1) * tile, tile), tile)
        pieces = [right[:, columns] for right in rights]
    total = mm(rows_ref[0], pieces[0])
    for item in range(1, count):
        total = total + mm(rows_ref[item], pieces[item])
    half = keep_ref.shape[0]
    keep_ref[...] = low(total[:half])
    send_ref[...] = low(total[half:])


def rows_grads(info, after, items, left, right, groups, halves, tile, tiles):
    length = items[0].shape[1]
    count = len(items)
    rows = left[3] // 2
    spread = 1 if right[1] == tile else 0
    half = pl.BlockSpec((None, rows // 2, tile), lambda g, t, info: (g, 0, t))
    shape = jax.ShapeDtypeStruct((groups, rows // 2, tile * tiles), LOW)
    return pl.pallas_call(
        lambda *refs: rows_kernel(halves, left[3], count, *refs),
        name="rows_grads",
        grid_spec=pltpu.PrefetchScalarGridSpec(
            num_scalar_prefetch=1,
            grid=(groups, tiles),
            in_specs=[ANYWHERE]
            + [pl.BlockSpec((None, length, left[1]), lambda g, t, info: (left[0], 0, left[2]))] * count
            + [pl.BlockSpec((None, length, right[1]), lambda g, t, info: (right[0] + g, 0, right[2] + spread * t))]
            * count,
            out_specs=[half, half],
            scratch_shapes=[pltpu.VMEM((count, left[3], length), LOW), pltpu.VMEM((count, rows, length), LOW)],
        ),
        out_shape=[shape, shape],
        compiler_params=pltpu.CompilerParams(
            dimension_semantics=("arbitrary", "arbitrary"), vmem_limit_bytes=VMEM
        ),
        cost_estimate=cost(1),
    )(info, after, *items, *items)


def halve(after, keep, came, axis):
    def kernel(after_ref, keep_ref, came_ref, *outs):
        total = keep_ref[...].astype(WIDE) + came_ref[...].astype(WIDE)
        if axis is None:
            outs[0][...] = total
        else:
            size = total.shape[axis - 1] // 2
            for i in range(2):
                at = slice(i * size, (i + 1) * size)
                outs[i][...] = low(total[at] if axis == 1 else total[:, at])

    groups, rows, columns = keep.shape
    shape = {None: (rows, columns), 1: (rows // 2, columns), 2: (rows, columns // 2)}[axis]
    count, dtype = (1, WIDE) if axis is None else (2, LOW)
    block = pl.BlockSpec((None, rows, columns), lambda g: (g, 0, 0))
    return pl.pallas_call(
        kernel,
        name="halve",
        grid=(groups,),
        in_specs=[ANYWHERE, block, block],
        out_specs=[pl.BlockSpec((None, *shape), lambda g: (g, 0, 0))] * count,
        out_shape=[jax.ShapeDtypeStruct((groups, *shape), dtype)] * count,
        compiler_params=params(),
        cost_estimate=cost(0.01),
    )(after, keep, came)


def tied(*values):
    return lax.optimization_barrier(values)


def exchange(value, axis, apart):
    return lax.ppermute(value, axis, [(i, i ^ apart(i)) for i in range(lax.axis_size(axis))])


def unpack(packed, like):
    found, start = [], 0
    for item in like:
        found.append(packed[start : start + item.size].reshape(item.shape))
        start += item.size
    return found


def pack(items):
    return jnp.concatenate([item.reshape(-1) for item in items])


def local(
    inputs, cotangent, w_qkv, w_beta, conv_taps, w_out, w_gate_up, w_down, norm_gains, out_gains
):
    batches, unused, length, width = inputs.shape
    place = lax.axis_index("section")
    rank, half = place // 2, place % 2
    me, copies = lax.axis_index("dp"), lax.axis_size("dp")
    per = batches // 2
    cube = copies == 8

    def across(value, bits=1):
        return exchange(value, "section", lambda i: bits)

    def flip(value, even, odd):
        return exchange(value, "dp", lambda i: odd if i % 2 else even)

    def by_half(own, other, axis):
        return jnp.where(
            half == 0, jnp.concatenate([own, other], axis), jnp.concatenate([other, own], axis)
        )

    first_apart = 2 + 2 * (me % 2)

    def mine_of(value, axis):
        size = value.shape[axis] // copies
        return lax.dynamic_slice_in_dim(value, me * size, size, axis)

    def collect(came, axis):
        came = jnp.concatenate([came, flip(came, 2, 4)], axis)
        came = jnp.concatenate([came, flip(came, 4, 2)], axis)
        return came, flip(came, 1, 1)

    smalls = [conv_taps, w_beta.astype(WIDE), norm_gains, out_gains]
    others = unpack(across(pack(smalls)), smalls)
    taps = jnp.concatenate([conv_taps, others[0]], 2)
    heads = w_beta.shape[1]
    w_beta = jnp.concatenate([w_beta, low(others[1])], 1)
    w_beta = jnp.pad(w_beta, ((0, 0), (0, LANES - 2 * heads)))
    gains = by_half(norm_gains, others[2], 1)
    out_gain = by_half(out_gains, others[3], 0)[None]
    inner, units = w_out.shape[0], w_down.shape[0]
    tile = w_qkv.shape[2]

    if cube:
        block = width // copies
        core = me % 2
        corner = 2 * ((me // 2 + me // 4) % 2) + core
        quarter, rows = width // 4, inner // 2
        came = across(mine_of(w_qkv, 1))
        came, lift = tied(came, mine_of(w_gate_up, 1))
        lift = across(lift)
        lift, out = tied(lift, lax.dynamic_slice_in_dim(w_out, core * rows, rows, 0))
        out = across(out)
        out, down = tied(out, lax.dynamic_slice_in_dim(w_down, corner * quarter, quarter, 1))
        down = across(down)
        mixer_weights = (w_qkv, w_out, *collect(came, 1), out, flip(out, 1, 1))
        near = flip(lift, 2, 4)
        lift = jnp.concatenate([lift, near], 1)
        far = flip(lift, 4, 2)
        apart = [0, first_apart, 6 - first_apart, 6, 1, 7 - first_apart, 1 + first_apart, 7]
        places = [me ^ bits for bits in apart]
        down_places = [2 * (corner ^ bits) + i for bits in (0, 2, 1, 3) for i in range(2)]
    else:

        def gathered(value):
            return lax.all_gather(across(mine_of(value, 1)), "dp", axis=1, tiled=True)

        def halves_of(value):
            return jnp.split(gathered(value), 2, 1)

        out = lax.all_gather(across(mine_of(w_out, 0)), "dp", axis=0, tiled=True)
        mixer_weights = (w_qkv, w_out, *halves_of(w_qkv), *jnp.split(out, 2, 0))
        feed_weights = (w_gate_up, w_down, *halves_of(w_gate_up), *halves_of(w_down))
        places = down_places = list(range(8))
        core, near = 0, taps
    info = jnp.stack([jnp.asarray(item, jnp.int32) for item in places + [rank == 0] + down_places + [core, 1 - core]])

    def mixer_part(after, stream):
        return mixer_forward(info, after, stream, gains[0:1], mixer_weights, w_beta, taps, out_gain)

    def feed_back(after, grad, saved, old=None):
        stream, middle, kept, lifted = saved
        return feed_backward(info, after, middle, grad, lifted, gains[1:2], feed_weights, old)

    def mixer_back(after, middle_grad, saved, old=None):
        stream, middle, kept, lifted = saved
        return mixer_backward(
            info, after, stream, middle_grad, kept, gains[0:1], mixer_weights, w_beta, taps, out_gain, old
        )

    def own(value):
        items = lax.dynamic_slice_in_dim(value, half * per, per, 0)
        return [items[i, 0] for i in range(per)]

    up = [(0, 2), (1, 3)]
    streams = own(inputs)
    saved0 = []
    for stream in streams:
        near, *kept = mixer_part(near, stream)
        saved0.append([stream, near, kept])
    if cube:
        far, down, saved0[0][1] = tied(far, down, saved0[0][1])
        lift = jnp.concatenate([lift, far], 1)
        lift_twin = flip(lift, 1, 1)
        down = jnp.concatenate([down, flip(down, 2, 4)], 1)
        down, saved0[-1][1] = tied(down, saved0[-1][1])
        feed_weights = (w_gate_up, w_down, lift, lift_twin, down, flip(down, 1, 1))
    firsts = []
    for saved in saved0:
        result, lifted = feed_forward(info, saved[1], gains[1:2], feed_weights)
        saved.append(lifted)
        firsts.append(result)
    saved1, results = [], []
    for index in range(per):
        stream = lax.ppermute(firsts[index], "section", up)
        middle, *kept = mixer_part(taps, stream)
        if index + 1 < per:
            firsts[index + 1], middle = tied(firsts[index + 1], middle)
        result, lifted = feed_forward(info, middle, gains[1:2], feed_weights)
        saved1.append([stream, middle, kept, lifted])
        results.append(result)
    returned, feeds, mixes = [], [], []
    for grad, saved in zip(own(cotangent), saved1):
        feeds.append(feed_back(taps, grad, saved))
        mixes.append(mixer_back((taps, taps), feeds[-1][0], saved))
        returned.append(lax.ppermute(mixes[-1][0], "section", [(2, 0), (3, 1)]))
    feed_twins, mix_twins = [], []
    waited = mixes[-1][0]
    for index, (grad, saved) in enumerate(zip(returned, saved0)):
        feeds[index] = feed_back(waited, grad, saved, feeds[index])
        after = (taps, taps)
        if cube:
            feed_twins.append(flip(feeds[index][2], 1, 1))
            if index:
                after = (feed_twins[index - 1], mix_twins[index - 1])
        mixes[index] = mixer_back(after, feeds[index][0], saved, mixes[index])
        if cube:
            mix_twins.append(flip(mixes[index][2], 1, 1))
    feed_all = [feed[2] for feed in feeds] + feed_twins
    if cube:
        lifts = rows_grads(info, mixes[-1][1], feed_all, (3, units, 0, width), (0, units, 0), 2, 1, units, 2)
        lift_came = flip(lifts[1], 2, 4)
        downs = rows_grads(
            info, lifts[0], feed_all, (2, 2 * units, 0, 2 * units), (3, units, 1), 1, 2, width // 2, 2
        )
        down_came = across(downs[1])
    mix_all = [mix[2] for mix in mixes]
    if cube:
        mix_all = mix_all + mix_twins
        qkvs = rows_grads(info, downs[0], mix_all, (5, width, 0, width), (0, width, 0), 3, 1, width, 1)
        qkv_came = flip(qkvs[1], 2, 4)
        outs = rows_grads(info, qkvs[0], mix_all, (3, width, 0, width), (4, width, 0), 1, 2, width, 1)
        out_came = across(outs[1])
        lifts = halve(outs[0], lifts[0], lift_came, 1)
        lift_came = flip(lifts[1], 4, 2)
        downs = halve(lifts[0], downs[0], down_came, 1)
        down_came = flip(downs[1], 2, 4)
        outs = halve(downs[0], outs[0], out_came, 1)
        out_came = flip(outs[1], 2, 4)
        qkvs = halve(outs[0], qkvs[0], qkv_came, 1)
        qkv_came = flip(qkvs[1], 4, 2)
        marks = [qkvs[0]]
        lifts = halve(qkvs[0], lifts[0], lift_came, 2)
        lift_came = across(lifts[1])
        marks.append(lifts[0])
        downs = halve(lifts[0], downs[0], down_came, 1)
        down_came = flip(downs[1], 4, 2)
        outs = halve(downs[0], outs[0], out_came, 1)
        out_came = flip(outs[1], 4, 2)
        qkvs = halve(outs[0], qkvs[0], qkv_came, 2)
        qkv_came = across(qkvs[1])
        marks.append(qkvs[0])
        grad_down = halve(qkvs[0], downs[0], down_came, None)[0]
        marks.append(grad_down)
        grad_out = halve(grad_down, outs[0], out_came, None)[0]
        grad_gate_up = halve(grad_out, lifts[0], lift_came, None)[0]
        grad_qkv = halve(grad_gate_up, qkvs[0], qkv_came, None)[0]
        grad_down, grad_out = grad_down[0], grad_out[0]
    else:

        def tall(items, index):
            return jnp.concatenate([item[index] for item in items], 0)

        def total(value, axis, split):
            value = lax.psum_scatter(low(value), "dp", scatter_dimension=axis, tiled=True)
            size = value.shape[split] // 2
            mine = lax.slice_in_dim(value, 0, size, axis=split)
            theirs = lax.slice_in_dim(value, size, 2 * size, axis=split)
            return mine.astype(WIDE) + across(theirs).astype(WIDE)

        ends = tall(feed_all, 3)
        normed2, grad, normed = ends[:, :width], ends[:, units : units + width], tall(mix_all, 5)
        grad_gate_up = total(jnp.stack([mm_tn(normed2, tall(feed_all, i)) for i in range(2)]), 1, 2)
        grad_qkv = total(jnp.stack([mm_tn(normed, tall(mix_all, i)) for i in range(3)]), 1, 2)
        down = mm_tn(tall(feed_all, 2), grad).reshape(2, units, width)
        out = mm_tn(tall(mix_all, 3), tall(mix_all, 4)).reshape(2, inner, width)
        grad_down, grad_out = total(down, 1, 0)[0], total(out, 1, 0)[0]

    strengths = [mix[3] for mix in mixes]
    if cube:
        strengths[0] = tied(strengths[0], marks[0])[0]
    d_beta = sum(mm_tn(mix[5], item) for mix, item in zip(mix_all, strengths))[:, : 2 * heads]
    d_taps = sum(mix[4] for mix in mixes)
    d_gains = jnp.concatenate([sum(mix[1] for mix in mixes), sum(feed[1] for feed in feeds)], 0)
    d_out_gain = sum(mix[5] for mix in mixes)

    flat = [d_taps, d_beta, d_gains, d_out_gain]
    packed = pack(flat)
    if cube:
        for bits, mark in zip((1, 2, 4), marks[1:]):
            packed = packed + tied(flip(packed, bits, bits), mark)[0]
    else:
        packed = lax.psum(packed, "dp")
    d_taps, d_beta, d_gains, d_out_gain = unpack(packed, flat)

    def part(value, axis, size):
        return lax.dynamic_slice_in_dim(value, me * size, size, axis)

    def halves(value, axis):
        size = value.shape[axis] // 2
        return [
            lax.dynamic_slice_in_dim(value, which * size, size, axis) for which in (half, 1 - half)
        ]

    pieces = [
        [part(d_taps[:, :, i * inner : (i + 1) * inner], 2, inner // copies) for i in range(2)],
        [part(d_beta[:, i * heads : (i + 1) * heads], 0, width // copies) for i in range(2)],
        [part(item, 1, width // 2 // copies) for item in halves(d_gains, 1)],
        [part(item, 1, LANES // 2 // copies) for item in halves(d_out_gain, 1)],
    ]
    mine = [item[0] for item in pieces]
    came = unpack(across(pack([item[1] for item in pieces])), mine)
    grad_taps, grad_beta, grad_gains, grad_out_gains = [a + b for a, b in zip(mine, came)]

    held = jnp.stack([jnp.where(rank == 1, a, mix[0]) for a, mix in zip(results, mixes)])
    if cube:
        held = tied(held, marks[0])[0]
    quarter = width // 4

    def quarter_of(index):
        return lax.dynamic_slice_in_dim(held, index * quarter, quarter, 2)

    came = [across(quarter_of(place ^ bits), bits) for bits in (1, 2, 3)]
    same = by_half(quarter_of(place), came[0], 0)
    other = by_half(came[1], came[2], 0)
    final_stream = jnp.where(rank == 1, same, other)[:, None]
    final_grad = jnp.where(rank == 0, same, other)[:, None]
    return (
        final_stream,
        final_grad,
        grad_qkv,
        grad_beta,
        grad_taps,
        grad_out,
        grad_gate_up,
        grad_down,
        grad_gains,
        grad_out_gains[0],
    )


def solution(mesh):
    in_specs = (
        P(None, "dp", None, None),
        P(None, "dp", None, None),
        P(None, None, "section"),
        P(None, "section"),
        P(None, None, "section"),
        P("section", None),
        P(None, None, "section"),
        P("section", None),
        P(None, "section"),
        P("section"),
    )
    out_specs = (
        P(None, "dp", None, "section"),
        P(None, "dp", None, "section"),
        P(None, "dp", "section"),
        P("dp", "section"),
        P(None, None, ("section", "dp")),
        P(("section", "dp"), None),
        P(None, "dp", "section"),
        P(("section", "dp"), None),
        P(None, ("section", "dp")),
        P(("section", "dp")),
    )
    return jax.shard_map(local, mesh=mesh, in_specs=in_specs, out_specs=out_specs, check_vma=False)
```

```python
import jax
import jax.numpy as jnp
from jax import lax
from jax.experimental import pallas as pl
from jax.experimental.pallas import tpu as pltpu
from jax.sharding import PartitionSpec as P

SPAN = 64
PAIR = 2 * SPAN
LANES = 128
LOW = jnp.bfloat16
WIDE = jnp.float32
VMEM = 56 * 1024 * 1024


def mm(left, right):
    return lax.dot_general(left, right, (((1,), (0,)), ((), ())), preferred_element_type=WIDE)


def mm_nt(left, right):
    return lax.dot_general(left, right, (((1,), (1,)), ((), ())), preferred_element_type=WIDE)


def mm_tn(left, right):
    return lax.dot_general(left, right, (((0,), (0,)), ((), ())), preferred_element_type=WIDE)


def low(value):
    return value.astype(LOW)


def sigmoid(value):
    return 0.5 * jnp.tanh(0.5 * value) + 0.5


def shift_down(value, steps):
    rows = lax.broadcasted_iota(jnp.int32, value.shape, 0)
    return jnp.where(rows >= steps, pltpu.roll(value, steps, 0), 0.0)


def shift_up(value, steps):
    size = value.shape[0]
    rows = lax.broadcasted_iota(jnp.int32, value.shape, 0)
    return jnp.where(rows < size - steps, pltpu.roll(value, size - steps, 0), 0.0)


def pick_lane(value, lane):
    lanes = lax.broadcasted_iota(jnp.int32, value.shape, 1)
    return jnp.sum(jnp.where(lanes == lane, value, 0.0), axis=1, keepdims=True)


def norm_scale(value, epsilon):
    return lax.rsqrt(jnp.mean(value * value, axis=-1, keepdims=True) + epsilon)


def norm_back(value, gain, grad, epsilon):
    scale = norm_scale(value, epsilon)
    scaled = gain * grad
    inner = jnp.mean(value * scaled, axis=-1, keepdims=True)
    value_grad = scale * (scaled - value * (scale * scale * inner))
    gain_grad = jnp.sum(grad * value * scale, axis=0, keepdims=True)
    return value_grad, gain_grad


def pair_masks():
    rows = lax.broadcasted_iota(jnp.int32, (PAIR, PAIR), 0)
    cols = lax.broadcasted_iota(jnp.int32, (PAIR, PAIR), 1)
    apart = rows ^ cols
    near = apart < SPAN
    return rows, cols, apart, near


def inverse(systems, apart):
    one = (apart == 0).astype(WIDE)
    found = [one - jnp.where(apart == 1, system, 0.0) for system in systems]
    lows = [low(system) for system in systems]
    size = 2
    while size < SPAN:
        level = (apart >= size) & (apart < 2 * size)
        parts = [jnp.where(level, system, jnp.zeros_like(system)) for system in lows]
        heads = [low(item) for item in found]
        steps = [low(mm(head, part)) for head, part in zip(heads, parts)]
        found = [item - mm(step, head) for item, step, head in zip(found, steps, heads)]
        size *= 2
    return found


def conv_silu(linear, taps):
    count = taps.shape[0]
    total = linear * taps[count - 1 : count]
    for back in range(1, count):
        total = total + shift_down(linear, back) * taps[count - 1 - back : count - back]
    return total


def whole(shape):
    return pl.BlockSpec(shape, lambda step, *scalars: (0,) * len(shape))


def tiled(shape, axis):
    return pl.BlockSpec(
        shape, lambda step, *scalars: tuple(step if i == axis else 0 for i in range(len(shape)))
    )


def tiled_old(shape, axis):
    return pl.BlockSpec(
        shape,
        lambda step, info: tuple(step * (1 - info[FIRST]) if i == axis else 0 for i in range(len(shape))),
    )


ANYWHERE = pl.BlockSpec(memory_space=pl.ANY)

FIRST, DOWN, OUT, SECOND = 8, 9, 17, 19


def mixer_copies(info_ref, refs, into_qkv, into_out, sems):
    qkv_ref, out_ref, qkv_came, qkv_twin, out_came, out_twin = refs
    rows = qkv_came.shape[1]
    first, second = pl.ds(0, rows), pl.ds(rows, rows)
    pairs = [
        (qkv_ref, into_qkv.at[0]),
        (out_ref, into_out.at[0]),
        (qkv_came, into_qkv.at[1, :, first]),
        (qkv_twin, into_qkv.at[1, :, second]),
    ]
    rows = out_came.shape[0]
    for index, source in enumerate((out_came, out_twin)):
        place = pl.multiple_of(info_ref[OUT + index] * rows, rows)
        pairs.append((source, into_out.at[1, pl.ds(place, rows)]))
    copies = [pltpu.make_async_copy(*pair, sems.at[i]) for i, pair in enumerate(pairs)]
    return copies[0], copies[1], copies[2:4], copies[4:]


def apart_order(info_ref, value_ref, into_ref, first=0):
    size = value_ref.shape[1] // 8
    for index in range(8):
        place = pl.multiple_of(info_ref[first + index] * size, size)
        into_ref[:, index * size : (index + 1) * size] = value_ref[:, pl.ds(place, size)]


def add_from_apart(info_ref, value_ref, into_ref, first=0):
    size = value_ref.shape[1] // 8
    for index in range(8):
        place = pl.ds(pl.multiple_of(info_ref[first + index] * size, size), size)
        into_ref[:, place] += value_ref[:, index * size : (index + 1) * size]


def start_all(step, copies):
    @pl.when(step == 0)
    def begin():
        for copy in copies:
            copy.start()


def wait_all(step, at, copies):
    @pl.when(step == at)
    def wait():
        for copy in copies:
            copy.wait()


def or_keep(kernel, inputs, outputs, first_kept, in_place=0):
    def either(*refs):
        start = 1 + inputs
        old = refs[start : start + outputs - first_kept]
        rest = refs[start + len(old) :]

        @pl.when(refs[0][FIRST] == 1)
        def compute():
            kernel(*refs[:start], *rest)

        @pl.when(refs[0][FIRST] == 0)
        def keep():
            for source, target in zip(old[: len(old) - in_place], rest[first_kept:outputs]):
                target[...] = source[...]

    return either


def only_second(kernel):
    def either(info_ref, *refs):
        @pl.when(info_ref[SECOND] == 1)
        def compute():
            kernel(info_ref, *refs)

    return either


def mixer_forward_kernel(
    info_ref,
    after_ref,
    stream_ref,
    gain_ref,
    w_beta_ref,
    taps_ref,
    out_gain_ref,
    qkv_own_ref,
    out_own_ref,
    qkv_came_ref,
    qkv_twin_ref,
    out_came_ref,
    out_twin_ref,
    middle_ref,
    strengths_ref,
    linear_ref,
    out_ref,
    fresh_ref,
    solve_ref,
    states_ref,
    moves_ref,
    normed_ref,
    w_qkv_ref,
    w_out_ref,
    sems,
):
    step = pl.program_id(0)
    length = stream_ref.shape[0]
    spans = length // SPAN
    heads = linear_ref.shape[2] // LANES
    refs = (qkv_own_ref, out_own_ref, qkv_came_ref, qkv_twin_ref, out_came_ref, out_twin_ref)
    own_qkv, own_out, qkv, out = mixer_copies(info_ref, refs, w_qkv_ref, w_out_ref, sems)
    start_all(step, [own_qkv, own_out])

    @pl.when(step == 0)
    def first():
        stream = stream_ref[...].astype(WIDE)
        normed_ref[0] = low(stream * norm_scale(stream, 1e-6) * gain_ref[...])
        apart_order(info_ref, normed_ref.at[0], normed_ref.at[1])
        strengths_ref[...] = mm(normed_ref[0], w_beta_ref[...])
        middle_ref[...] = stream

    normed = normed_ref[step]
    wait_all(step, 0, [own_qkv, own_out])
    wait_all(step, 1, qkv + out)
    start_all(step, qkv + out)
    active = []
    for which in range(3):
        linear = mm(normed, w_qkv_ref[step, which])
        linear_ref[which] = low(linear)
        total = conv_silu(linear, taps_ref[which])
        active.append(total * sigmoid(total))
    rows, cols, apart, near = pair_masks()
    strict = (rows > cols) & near
    lower = (rows >= cols) & near
    queries, keys, values, betas = [], [], [], []
    for head in range(heads):
        lanes = slice(head * LANES, (head + 1) * LANES)
        query, key = active[0][:, lanes], active[1][:, lanes]
        queries.append(low(query * lax.rsqrt(jnp.sum(query * query, axis=1, keepdims=True) + 1e-6)))
        keys.append(low(key * lax.rsqrt(jnp.sum(key * key, axis=1, keepdims=True) + 1e-6)))
        values.append(low(active[2][:, lanes]))
        betas.append(sigmoid(pick_lane(strengths_ref[...], step * heads + head)))
    cells = [(head, pair) for head in range(heads) for pair in range(length // PAIR)]

    def part(array, pair):
        return array[pair * PAIR : (pair + 1) * PAIR]

    systems = []
    for head, pair in cells:
        key = part(keys[head], pair)
        systems.append(jnp.where(strict, mm_nt(key, key) * part(betas[head], pair), 0.0))
    solved = [low(item) for item in inverse(systems, apart)]
    both = {}
    scores = {}
    for (head, pair), solve in zip(cells, solved):
        solve_ref[head, pair] = solve
        beta = part(betas[head], pair)
        key = part(keys[head], pair)
        right = jnp.concatenate(
            [low(beta * key.astype(WIDE)), low(beta * part(values[head], pair).astype(WIDE))], axis=1
        )
        both[head, pair] = mm(solve, right)
        scores[head, pair] = low(jnp.where(lower, mm_nt(part(queries[head], pair), key), 0.0))

    def span_of(array, span):
        return array[span * SPAN : (span + 1) * SPAN]

    def both_of(head, span):
        return span_of(both[head, span // 2], span % 2)

    states = [[None] * spans for head in range(heads)]
    turns = {}
    for head in range(heads):
        for span in range(spans - 1):
            turns[head, span] = mm_tn(span_of(keys[head], span), low(both_of(head, span)))
    for span in range(1, spans):
        for head in range(heads):
            turn = turns[head, span - 1]
            if span == 1:
                states[head][span] = turn[:, LANES:]
            else:
                before = states[head][span - 1]
                move = low(turn[:, :LANES])
                moves_ref[head, span - 2] = move
                states[head][span] = before + turn[:, LANES:] - mm(move, low(before))
    fresh = {}
    carried = {}
    for head in range(heads):
        for span in range(spans):
            item = both_of(head, span)
            if span == 0:
                fresh[head, span] = low(item[:, LANES:])
                carried[head, span] = jnp.zeros((SPAN, LANES), WIDE)
            else:
                state = low(states[head][span])
                states_ref[head, span - 1] = state
                left = jnp.concatenate([low(item[:, :LANES]), span_of(queries[head], span)], axis=0)
                seen = mm(left, state)
                fresh[head, span] = low(item[:, LANES:] - seen[:SPAN])
                carried[head, span] = seen[SPAN:]
    normed_out = []
    for head in range(heads):
        lanes = slice(head * LANES, (head + 1) * LANES)
        pieces = []
        for pair in range(length // PAIR):
            piece = jnp.concatenate([fresh[head, 2 * pair], fresh[head, 2 * pair + 1]], axis=0)
            fresh_ref[pair * PAIR : (pair + 1) * PAIR, lanes] = piece
            base = jnp.concatenate([carried[head, 2 * pair], carried[head, 2 * pair + 1]], axis=0)
            pieces.append(base + mm(scores[head, pair], piece))
        output = jnp.concatenate(pieces, axis=0)
        out_ref[:, lanes] = low(output)
        normed_out.append(low(output * norm_scale(output, 1e-5) * out_gain_ref[...]))
    middle_ref[...] += mm(jnp.concatenate(normed_out, axis=1), w_out_ref[step])


def cost(micros):
    return pl.CostEstimate(flops=int(micros * 1.1e9), bytes_accessed=2**20, transcendentals=0)


def params(limit=VMEM, **extra):
    return pltpu.CompilerParams(dimension_semantics=("arbitrary",), vmem_limit_bytes=limit, **extra)


def mixer_forward(info, after, stream, gain, weights, w_beta, taps, out_gain, wrap=lambda kernel: kernel):
    length, width = stream.shape
    tile = weights[0].shape[2]
    inner = 2 * tile
    heads = inner // LANES
    spans = length // SPAN
    pairs = length // PAIR
    here = tile // LANES
    out = jax.ShapeDtypeStruct
    return pl.pallas_call(
        wrap(mixer_forward_kernel),
        name="mixer_forward",
        grid_spec=pltpu.PrefetchScalarGridSpec(
            num_scalar_prefetch=1,
            grid=(2,),
            in_specs=[
                ANYWHERE,
                whole((length, width)),
                whole((1, width)),
                whole((width, LANES)),
                tiled((3, taps.shape[1], tile), 2),
                whole((1, LANES)),
            ]
            + [ANYWHERE] * 6,
            out_specs=[
                whole((length, width)),
                whole((length, LANES)),
                tiled((3, length, tile), 2),
                tiled((length, tile), 1),
                tiled((length, tile), 1),
                tiled((here, pairs, PAIR, PAIR), 0),
                tiled((here, spans - 1, LANES, LANES), 0),
                tiled((here, spans - 2, LANES, LANES), 0),
            ],
            scratch_shapes=[
                pltpu.VMEM((2, length, width), LOW),
                pltpu.VMEM((2, 3, width, tile), LOW),
                pltpu.VMEM((2, tile, width), LOW),
                pltpu.SemaphoreType.DMA((6,)),
            ],
        ),
        out_shape=[
            out((length, width), WIDE),
            out((length, LANES), WIDE),
            out((3, length, inner), LOW),
            out((length, inner), LOW),
            out((length, inner), LOW),
            out((heads, pairs, PAIR, PAIR), LOW),
            out((heads, spans - 1, LANES, LANES), LOW),
            out((heads, spans - 2, LANES, LANES), LOW),
        ],
        compiler_params=params(),
        cost_estimate=cost(14),
    )(info, after, stream, gain, w_beta, taps, out_gain, *weights)


def mixer_backward_kernel(
    info_ref,
    after_ref,
    also_ref,
    third_ref,
    stream_ref,
    branch_ref,
    strengths_ref,
    linear_ref,
    out_ref,
    fresh_ref,
    solve_ref,
    states_ref,
    moves_ref,
    gain_ref,
    w_beta_ref,
    taps_ref,
    out_gain_ref,
    qkv_own_ref,
    out_own_ref,
    qkv_came_ref,
    qkv_twin_ref,
    out_came_ref,
    out_twin_ref,
    stream_grad_ref,
    gain_grad_ref,
    stack_ref,
    strengths_grad_ref,
    taps_grad_ref,
    out_gain_grad_ref,
    normed_grad_ref,
    strengths_sum_ref,
    branch_low_ref,
    normed_ref,
    w_qkv_ref,
    w_out_ref,
    sems,
):
    step = pl.program_id(0)
    steps = pl.num_programs(0)
    length = stream_ref.shape[0]
    spans = length // SPAN
    pairs = length // PAIR
    tile = stack_ref.shape[2]
    heads = tile // LANES
    refs = (qkv_own_ref, out_own_ref, qkv_came_ref, qkv_twin_ref, out_came_ref, out_twin_ref)
    own_qkv, own_out, qkv, out = mixer_copies(info_ref, refs, w_qkv_ref, w_out_ref, sems)
    start_all(step, [own_out, own_qkv])

    @pl.when(step == 0)
    def first():
        branch_low_ref[...] = low(branch_ref[...])
        stream = stream_ref[...].astype(WIDE)
        normed_ref[...] = low(stream * norm_scale(stream, 1e-6) * gain_ref[...])
        out_gain_grad_ref[...] = jnp.zeros_like(out_gain_grad_ref)
        strengths_sum_ref[...] = jnp.zeros_like(strengths_sum_ref)
        normed_grad_ref[...] = jnp.zeros_like(normed_grad_ref)

    columns = pl.ds(pl.multiple_of(step * tile, tile), tile)
    stack_ref[4] = branch_low_ref[:, columns]
    stack_ref[5] = normed_ref[:, columns]
    rows, cols, apart, near = pair_masks()
    strict = (rows > cols) & near
    lower = (rows >= cols) & near
    upper_strict = (rows < cols) & near
    upper = (rows <= cols) & near
    cells = [(head, pair) for head in range(heads) for pair in range(pairs)]

    def part(array, pair):
        return array[pair * PAIR : (pair + 1) * PAIR]

    def span_of(array, span):
        return array[span * SPAN : (span + 1) * SPAN]

    wait_all(step, 0, [own_out, own_qkv])
    wait_all(step, 1, out + qkv)
    start_all(step, out + qkv)
    normed_out_grad = mm_nt(branch_low_ref[...], w_out_ref[step])
    totals, gates, active = [], [], []
    for which in range(3):
        total = conv_silu(linear_ref[which].astype(WIDE), taps_ref[which])
        gate = sigmoid(total)
        totals.append(total)
        gates.append(gate)
        active.append(total * gate)
    query_scales, key_scales = [], []
    queries, keys, values, betas, output_grads = [], [], [], [], []
    for head in range(heads):
        lanes = slice(head * LANES, (head + 1) * LANES)
        query, key = active[0][:, lanes], active[1][:, lanes]
        query_scales.append(lax.rsqrt(jnp.sum(query * query, axis=1, keepdims=True) + 1e-6))
        key_scales.append(lax.rsqrt(jnp.sum(key * key, axis=1, keepdims=True) + 1e-6))
        queries.append(low(query * query_scales[head]))
        keys.append(low(key * key_scales[head]))
        values.append(low(active[2][:, lanes]))
        betas.append(sigmoid(pick_lane(strengths_ref[...], step * heads + head)))
        output = out_ref[:, lanes].astype(WIDE)
        scale = norm_scale(output, 1e-5)
        grad = normed_out_grad[:, lanes]
        stack_ref[3, :, lanes] = low(output * scale * out_gain_ref[...])
        scaled = out_gain_ref[...] * grad
        inner = jnp.mean(output * scaled, axis=1, keepdims=True)
        output_grads.append(low(scale * (scaled - output * (scale * scale * inner))))
        out_gain_grad_ref[...] += jnp.sum(grad * output * scale, axis=0, keepdims=True)
    fresh = [fresh_ref[:, head * LANES : (head + 1) * LANES] for head in range(heads)]

    scores_back, score_grads, score_grads_back = {}, {}, {}
    for head, pair in cells:
        query, key = part(queries[head], pair), part(keys[head], pair)
        grad, new = part(output_grads[head], pair), part(fresh[head], pair)
        scores_back[head, pair] = low(jnp.where(upper, mm_nt(key, query), 0.0))
        score_grads[head, pair] = low(jnp.where(lower, mm_nt(grad, new), 0.0))
        score_grads_back[head, pair] = low(jnp.where(upper, mm_nt(new, grad), 0.0))
    inside, early = {}, {}
    for head, pair in cells:
        inside[head, pair] = mm(scores_back[head, pair], part(output_grads[head], pair))
    for head, pair in cells:
        early[head, pair] = mm_tn(solve_ref[head, pair], low(inside[head, pair]))
    returns = {}
    for head in range(heads):
        for span in range(1, spans):
            beta = span_of(betas[head], span)
            back = low(-beta * span_of(early[head, span // 2], span % 2))
            left = jnp.concatenate([span_of(queries[head], span), span_of(keys[head], span)], axis=0)
            right = jnp.concatenate([span_of(output_grads[head], span), back], axis=0)
            returns[head, span] = mm_tn(left, right)
    state_grads = {}
    for span in range(spans - 2, -1, -1):
        for head in range(heads):
            if span == spans - 2:
                state_grads[head, span] = returns[head, span + 1]
            else:
                after = state_grads[head, span + 1]
                state_grads[head, span] = (
                    after + returns[head, span + 1] - mm_tn(moves_ref[head, span], low(after))
                )
    fresh_add = {}
    for head, pair in cells:
        pieces = []
        for span in (2 * pair, 2 * pair + 1):
            if span == spans - 1:
                pieces.append(jnp.zeros((SPAN, LANES), WIDE))
            else:
                pieces.append(mm(span_of(keys[head], span), low(state_grads[head, span])))
        fresh_add[head, pair] = low(jnp.concatenate(pieces, axis=0))
    lasts, backs = {}, {}
    for head, pair in cells:
        last = early[head, pair] + mm_tn(solve_ref[head, pair], fresh_add[head, pair])
        lasts[head, pair] = last
        backs[head, pair] = part(betas[head], pair) * last
    system_grads, system_grads_back = {}, {}
    for head, pair in cells:
        last, new = low(lasts[head, pair]), part(fresh[head], pair)
        system_grads[head, pair] = low(jnp.where(strict, -mm_nt(last, new), 0.0))
        system_grads_back[head, pair] = low(jnp.where(upper_strict, -mm_nt(new, last), 0.0))
    query_grads, key_grads, beta_grads = [], [], []
    for head in range(heads):
        query_pieces, key_pieces, beta_pieces = [], [], []
        for pair in range(pairs):
            query, key = part(queries[head], pair), part(keys[head], pair)
            beta, new = part(betas[head], pair), part(fresh[head], pair)
            grad = part(output_grads[head], pair)
            stacked = jnp.concatenate(
                [score_grads[head, pair], system_grads[head, pair]], axis=0
            )
            through = mm(stacked, key)
            query_grad = through[:PAIR]
            key_grad = beta * through[PAIR:]
            wide = jnp.concatenate(
                [score_grads_back[head, pair], system_grads_back[head, pair]], axis=1
            )
            tall = jnp.concatenate([query, low(beta * key.astype(WIDE))], axis=0)
            key_grad = key_grad + mm(wide, tall)
            inner = low(jnp.where(strict, mm_nt(key, key), 0.0))
            residual = part(values[head], pair).astype(WIDE) - mm(inner, new)
            back = low(backs[head, pair])
            more_query, more_key, seen = [], [], []
            for local_span in range(2):
                span = 2 * pair + local_span
                new_span = span_of(new, local_span)
                if span == 0:
                    more_query.append(jnp.zeros((SPAN, LANES), WIDE))
                    seen.append(jnp.zeros((SPAN, LANES), WIDE))
                    more_key.append(mm_nt(new_span, low(state_grads[head, span])))
                    continue
                state = states_ref[head, span - 1]
                more_query.append(mm_nt(span_of(grad, local_span), state))
                seen.append(mm(span_of(key, local_span), state))
                taken = -span_of(back, local_span)
                if span == spans - 1:
                    more_key.append(mm_nt(taken, state))
                else:
                    left = jnp.concatenate([new_span, taken], axis=1)
                    right = jnp.concatenate([low(state_grads[head, span]), state], axis=1)
                    more_key.append(mm_nt(left, right))
            residual = residual - jnp.concatenate(seen, axis=0)
            query_pieces.append(query_grad + jnp.concatenate(more_query, axis=0))
            key_pieces.append(key_grad + jnp.concatenate(more_key, axis=0))
            beta_pieces.append(jnp.sum(lasts[head, pair] * residual, axis=1, keepdims=True))
        query_grads.append(jnp.concatenate(query_pieces, axis=0))
        key_grads.append(jnp.concatenate(key_pieces, axis=0))
        beta_grads.append(jnp.concatenate(beta_pieces, axis=0))
    lane_ids = lax.broadcasted_iota(jnp.int32, (length, LANES), 1)
    strengths_sum = strengths_sum_ref[...]
    for head in range(heads):
        beta = betas[head]
        strengths_sum = strengths_sum + jnp.where(
            lane_ids == step * heads + head, beta_grads[head] * beta * (1.0 - beta), 0.0
        )
    strengths_sum_ref[...] = strengths_sum

    active_grads = []
    for grads, scales, source in ((query_grads, query_scales, active[0]), (key_grads, key_scales, active[1])):
        pieces = []
        for head in range(heads):
            lanes = slice(head * LANES, (head + 1) * LANES)
            value, scale, grad = source[:, lanes], scales[head], grads[head]
            inner = jnp.sum(value * grad, axis=1, keepdims=True)
            pieces.append(scale * (grad - value * (scale * scale * inner)))
        active_grads.append(jnp.concatenate(pieces, axis=1))
    active_grads.append(
        jnp.concatenate(
            [jnp.concatenate([backs[head, pair] for pair in range(pairs)], axis=0) for head in range(heads)],
            axis=1,
        )
    )
    normed_grad = normed_grad_ref[step]
    for which in range(3):
        total, gate = totals[which], gates[which]
        total_grad = active_grads[which] * (gate * (1.0 + total * (1.0 - gate)))
        taps = taps_ref[which]
        linear = linear_ref[which].astype(WIDE)
        count = taps.shape[0]
        linear_grad = total_grad * taps[count - 1 : count]
        taps_grad_ref[which, count - 1 : count] = jnp.sum(total_grad * linear, axis=0, keepdims=True)
        for ahead in range(1, count):
            moved = shift_up(total_grad, ahead)
            place = slice(count - 1 - ahead, count - ahead)
            linear_grad = linear_grad + moved * taps[place]
            taps_grad_ref[which, place] = jnp.sum(moved * linear, axis=0, keepdims=True)
        linear_low = low(linear_grad)
        stack_ref[which] = linear_low
        normed_grad = normed_grad + mm_nt(linear_low, w_qkv_ref[step, which])
    normed_grad_ref[step] = normed_grad

    @pl.when(step == steps - 1)
    def last_step():
        strengths_low = low(strengths_sum_ref[...])
        strengths_grad_ref[...] = strengths_low
        add_from_apart(info_ref, normed_grad_ref.at[1], normed_grad_ref.at[0])
        total = normed_grad_ref[0] + mm_nt(strengths_low, w_beta_ref[...])
        value_grad, gain_grad = norm_back(stream_ref[...].astype(WIDE), gain_ref[...], total, 1e-6)
        stream_grad_ref[...] = low(branch_ref[...] + value_grad)
        gain_grad_ref[...] = gain_grad


def mixer_backward(info, after, stream, branch, kept, gain, weights, w_beta, taps, out_gain, old=None):
    strengths, linear, output, fresh, solve, states, moves = kept
    length, width = stream.shape
    tile = weights[0].shape[2]
    inner = 2 * tile
    spans = length // SPAN
    pairs = length // PAIR
    here = tile // LANES
    out = jax.ShapeDtypeStruct
    count = taps.shape[1]
    in_specs = [
        ANYWHERE,
        ANYWHERE,
        ANYWHERE,
        whole((length, width)),
        whole((length, width)),
        whole((length, LANES)),
        tiled((3, length, tile), 2),
        tiled((length, tile), 1),
        tiled((length, tile), 1),
        tiled((here, pairs, PAIR, PAIR), 0),
        tiled((here, spans - 1, LANES, LANES), 0),
        tiled((here, spans - 2, LANES, LANES), 0),
        whole((1, width)),
        whole((width, LANES)),
        tiled((3, count, tile), 2),
        whole((1, LANES)),
    ] + [ANYWHERE] * 6
    kernel, more = only_second(mixer_backward_kernel), []
    if old is not None:
        more = old[1:]
        kernel = or_keep(mixer_backward_kernel, len(in_specs), 6, 1)
        in_specs = in_specs + [
            whole((1, width)),
            tiled_old((6, length, tile), 2),
            whole((length, LANES)),
            tiled_old((3, count, tile), 2),
            whole((1, LANES)),
        ]
    return pl.pallas_call(
        kernel,
        name="mixer_backward",
        grid_spec=pltpu.PrefetchScalarGridSpec(
            num_scalar_prefetch=1,
            grid=(2,),
            in_specs=in_specs,
            out_specs=[
                whole((length, width)),
                whole((1, width)),
                tiled((6, length, tile), 2),
                whole((length, LANES)),
                tiled((3, count, tile), 2),
                whole((1, LANES)),
            ],
            scratch_shapes=[
                pltpu.VMEM((2, length, width), WIDE),
                pltpu.VMEM((length, LANES), WIDE),
                pltpu.VMEM((length, width), LOW),
                pltpu.VMEM((length, width), LOW),
                pltpu.VMEM((2, 3, width, tile), LOW),
                pltpu.VMEM((2, tile, width), LOW),
                pltpu.SemaphoreType.DMA((6,)),
            ],
        ),
        out_shape=[
            out((length, width), LOW),
            out((1, width), WIDE),
            out((6, length, inner), LOW),
            out((length, LANES), LOW),
            out((3, count, inner), WIDE),
            out((1, LANES), WIDE),
        ],
        compiler_params=params(),
        cost_estimate=cost(20),
    )(
        info, *after, stream, branch, strengths, linear, output, fresh, solve, states, moves,
        gain, w_beta, taps, out_gain, *weights, *more,
    )


def unit_tiles(units):
    count = -(-units // 512)
    size = -(-units // count // LANES) * LANES
    return [(start, min(size, units - start)) for start in range(0, units, size)]


def feed_tiles(refs, into_lift, into_down, sems):
    lift_ref, down_ref, lift_came, lift_twin, down_came, down_twin = refs
    tiles, at = [], 0
    for which in range(2):
        for start, size in unit_tiles(down_ref.shape[0]):
            span = pl.ds(start, size)
            if which == 0:
                lift = [(lift_ref.at[:, :, span], into_lift.at[0, :, :, span])]
                down = [(down_ref.at[span], into_down.at[0, span])]
            else:
                rows, columns = lift_came.shape[1], down_came.shape[1]
                lift = [
                    (lift_came.at[:, :, span], into_lift.at[1, :, pl.ds(0, rows), span]),
                    (lift_twin.at[:, :, span], into_lift.at[1, :, pl.ds(rows, rows), span]),
                ]
                down = [
                    (down_came.at[span], into_down.at[1, span, pl.ds(0, columns)]),
                    (down_twin.at[span], into_down.at[1, span, pl.ds(columns, columns)]),
                ]
            copies = []
            for group in (lift, down):
                copies.append([pltpu.make_async_copy(*pair, sems.at[at + i]) for i, pair in enumerate(group)])
                at += len(group)
            tiles.append((which, start, size, copies[0], copies[1]))
    return tiles


def start_each(copies):
    for copy in copies:
        copy.start()


def wait_each(copies):
    for copy in copies:
        copy.wait()


AHEAD = 3


def feed_forward_kernel(
    info_ref,
    middle_ref,
    gain_ref,
    lift_own_ref,
    down_own_ref,
    lift_came_ref,
    lift_twin_ref,
    down_came_ref,
    down_twin_ref,
    result_ref,
    lifted_ref,
    total_ref,
    normed_ref,
    w_gate_up_ref,
    w_down_ref,
    kept_ref,
    sems,
    out_sems,
):
    units = down_own_ref.shape[0]
    refs = (lift_own_ref, down_own_ref, lift_came_ref, lift_twin_ref, down_came_ref, down_twin_ref)
    tiles = feed_tiles(refs, w_gate_up_ref, w_down_ref, sems)
    for tile in tiles[:AHEAD]:
        start_each(tile[3] + tile[4])
    middle = middle_ref[...]
    normed_ref[0] = low(middle * norm_scale(middle, 1e-6) * gain_ref[...])
    apart_order(info_ref, normed_ref.at[0], normed_ref.at[1])
    outs = []
    lifted = []
    for index in range(len(tiles) + 1):
        if index < len(tiles):
            which, start, size, lift, down = tiles[index]
            wait_each(lift)
        if index:
            wait_each(tiles[index - 1][4])
        if 0 < index <= len(tiles) - AHEAD:
            start_each(tiles[index + AHEAD - 1][3] + tiles[index + AHEAD - 1][4])
        if index < len(tiles):
            span = pl.ds(start, size)
            normed = normed_ref[which]
            gate = mm(normed, w_gate_up_ref[which, 0, :, span])
            up = mm(normed, w_gate_up_ref[which, 1, :, span])
            place = pl.ds(which * units + start, size)
            kept_ref[0, :, place] = low(gate)
            kept_ref[1, :, place] = low(up)
            lifted.append((gate, up))
        if index:
            which, start, size, lift, down = tiles[index - 1]
            span = pl.ds(start, size)
            place = pl.ds(which * units + start, size)
            outs.append(
                pltpu.make_async_copy(
                    kept_ref.at[:, :, place], lifted_ref.at[:, :, place], out_sems.at[index - 1]
                )
            )
            outs[-1].start()
            gate, up = lifted[index - 1]
            hidden = low(gate * sigmoid(gate) * up)
            part = mm(hidden, w_down_ref[which, span, :])
            if start:
                total_ref[which] += part
            else:
                total_ref[which] = part + middle if which == 0 else part
    add_from_apart(info_ref, total_ref.at[1], total_ref.at[0], DOWN)
    result_ref[...] = low(total_ref[0])
    wait_each(outs)


def feed_forward(info, middle, gain, weights, wrap=lambda kernel: kernel):
    length, width = middle.shape
    units = weights[1].shape[0]
    count = 2 * len(unit_tiles(units))
    out = jax.ShapeDtypeStruct
    return pl.pallas_call(
        wrap(feed_forward_kernel),
        name="feed_forward",
        grid_spec=pltpu.PrefetchScalarGridSpec(
            num_scalar_prefetch=1,
            grid=(1,),
            in_specs=[whole((length, width)), whole((1, width))] + [ANYWHERE] * 6,
            out_specs=[whole((length, width)), ANYWHERE],
            scratch_shapes=[
                pltpu.VMEM((2, length, width), WIDE),
                pltpu.VMEM((2, length, width), LOW),
                pltpu.VMEM((2, 2, width, units), LOW),
                pltpu.VMEM((2, units, width), LOW),
                pltpu.VMEM((2, length, 2 * units), LOW),
                pltpu.SemaphoreType.DMA((3 * count,)),
                pltpu.SemaphoreType.DMA((count,)),
            ],
        ),
        out_shape=[out((length, width), LOW), out((2, length, 2 * units), LOW)],
        compiler_params=params(),
        cost_estimate=cost(10),
    )(info, middle, gain, *weights)


def feed_backward_kernel(
    info_ref,
    middle_ref,
    grad_ref,
    gain_ref,
    lifted_ref,
    lift_own_ref,
    down_own_ref,
    lift_came_ref,
    lift_twin_ref,
    down_came_ref,
    down_twin_ref,
    middle_grad_ref,
    gain_grad_ref,
    stack_ref,
    normed_grad_ref,
    grads_ref,
    w_gate_up_ref,
    w_down_ref,
    kept_ref,
    made_ref,
    sems,
    in_sems,
    out_sems,
):
    width = middle_ref.shape[1]
    units = down_own_ref.shape[0]
    refs = (lift_own_ref, down_own_ref, lift_came_ref, lift_twin_ref, down_came_ref, down_twin_ref)
    tiles = feed_tiles(refs, w_gate_up_ref, w_down_ref, sems)
    ins, outs = [], []
    for index, (which, start, size, lift, down) in enumerate(tiles):
        place = pl.ds(which * units + start, size)
        ins.append(pltpu.make_async_copy(lifted_ref.at[:, :, place], kept_ref.at[:, :, place], in_sems.at[index]))
        outs.append(
            pltpu.make_async_copy(
                made_ref.at[pl.ds(0, 3), :, place], stack_ref.at[pl.ds(0, 3), :, place], out_sems.at[index]
            )
        )
    for index in range(AHEAD):
        start_each(tiles[index][4] + [ins[index]] + tiles[index][3])
    middle = middle_ref[...]
    made_ref[3] = jnp.zeros(made_ref.shape[1:], LOW)
    made_ref[3, :, :width] = low(middle * norm_scale(middle, 1e-6) * gain_ref[...])
    made_ref[3, :, units : units + width] = grad_ref[...]
    ends = pltpu.make_async_copy(made_ref.at[3], stack_ref.at[3], out_sems.at[len(tiles)])
    ends.start()
    grads_ref[0] = grad_ref[...]
    apart_order(info_ref, grads_ref.at[0], grads_ref.at[1], DOWN)
    hidden_grads = []
    for index in range(len(tiles) + 1):
        if index < len(tiles):
            which, start, size, lift, down = tiles[index]
            wait_each(down)
        if index:
            ins[index - 1].wait()
            wait_each(tiles[index - 1][3])
        if 0 < index <= len(tiles) - AHEAD:
            more = index + AHEAD - 1
            start_each(tiles[more][4] + [ins[more]] + tiles[more][3])
        if index < len(tiles):
            span = pl.ds(start, size)
            hidden_grads.append(mm_nt(grads_ref[which], w_down_ref[which, span, :]))
        if index:
            which, start, size, lift, down = tiles[index - 1]
            span = pl.ds(start, size)
            place = pl.ds(which * units + start, size)
            hidden_grad = hidden_grads[index - 1]
            gate = kept_ref[0, :, place].astype(WIDE)
            up = kept_ref[1, :, place].astype(WIDE)
            open_ = sigmoid(gate)
            silu = gate * open_
            up_grad = low(hidden_grad * silu)
            gate_grad = low(hidden_grad * up * (open_ + silu * (1.0 - open_)))
            made_ref[0, :, place] = gate_grad
            made_ref[1, :, place] = up_grad
            made_ref[2, :, place] = low(silu * up)
            outs[index - 1].start()
            part = mm_nt(gate_grad, w_gate_up_ref[which, 0, :, span]) + mm_nt(
                up_grad, w_gate_up_ref[which, 1, :, span]
            )
            if start:
                normed_grad_ref[which] += part
            else:
                normed_grad_ref[which] = part
    add_from_apart(info_ref, normed_grad_ref.at[1], normed_grad_ref.at[0])
    value_grad, gain_grad = norm_back(middle, gain_ref[...], normed_grad_ref[0], 1e-6)
    middle_grad_ref[...] = grad_ref[...].astype(WIDE) + value_grad
    gain_grad_ref[...] = gain_grad
    wait_each(outs)
    ends.wait()


def feed_backward(info, after, middle, grad, lifted, gain, weights, old=None):
    length, width = middle.shape
    units = weights[1].shape[0]
    count = 2 * len(unit_tiles(units))
    out = jax.ShapeDtypeStruct
    waits = len(after)
    in_specs = [ANYWHERE] * waits + [whole((length, width)), whole((length, width)), whole((1, width))] + [ANYWHERE] * 7
    body = lambda info_ref, *refs: feed_backward_kernel(info_ref, *refs[waits:])
    kernel, more, aliases = only_second(body), [], {}
    if old is not None:
        more = old[1:]
        kernel = or_keep(body, len(in_specs), 3, 1, 1)
        in_specs = in_specs + [whole((1, width)), ANYWHERE]
        aliases = {len(in_specs): 2}
    return pl.pallas_call(
        kernel,
        name="feed_backward",
        grid_spec=pltpu.PrefetchScalarGridSpec(
            num_scalar_prefetch=1,
            grid=(1,),
            in_specs=in_specs,
            out_specs=[whole((length, width)), whole((1, width)), ANYWHERE],
            scratch_shapes=[
                pltpu.VMEM((2, length, width), WIDE),
                pltpu.VMEM((2, length, width), LOW),
                pltpu.VMEM((2, 2, width, units), LOW),
                pltpu.VMEM((2, units, width), LOW),
                pltpu.VMEM((2, length, 2 * units), LOW),
                pltpu.VMEM((4, length, 2 * units), LOW),
                pltpu.SemaphoreType.DMA((3 * count,)),
                pltpu.SemaphoreType.DMA((count,)),
                pltpu.SemaphoreType.DMA((count + 1,)),
            ],
        ),
        out_shape=[
            out((length, width), WIDE),
            out((1, width), WIDE),
            out((4, length, 2 * units), LOW),
        ],
        input_output_aliases=aliases,
        compiler_params=params(),
        cost_estimate=cost(13),
    )(info, *after, middle, grad, gain, lifted, *weights, *more)


def rows_kernel(halves, width, count, info_ref, *refs):
    lefts, rights = refs[:count], refs[count : 2 * count]
    keep_ref, send_ref, turned_ref, rows_ref = refs[2 * count :]
    size = width // halves // 8

    @pl.when((pl.program_id(0) == 0) & (pl.program_id(1) == 0))
    def first():
        for item in range(count):
            turned_ref[item] = lefts[item][:, :width].T
            place = 0
            for which in range(halves):
                for index in (0, 2, 1, 3):
                    start = which * (width // halves) + info_ref[index] * size
                    source = pl.ds(pl.multiple_of(start, size), size)
                    rows_ref[item, place : place + size, :] = turned_ref[item, source, :]
                    place += size

    tile = keep_ref.shape[1]
    if rights[0].shape[1] == tile:
        pieces = [right[...] for right in rights]
    else:
        columns = pl.ds(pl.multiple_of(pl.program_id(1) * tile, tile), tile)
        pieces = [right[:, columns] for right in rights]
    total = mm(rows_ref[0], pieces[0])
    for item in range(1, count):
        total = total + mm(rows_ref[item], pieces[item])
    half = keep_ref.shape[0]
    keep_ref[...] = low(total[:half])
    send_ref[...] = low(total[half:])


def rows_grads(info, after, items, left, right, groups, halves, tile, tiles):
    length = items[0].shape[1]
    count = len(items)
    rows = left[3] // 2
    spread = 1 if right[1] == tile else 0
    half = pl.BlockSpec((None, rows // 2, tile), lambda g, t, info: (g, 0, t))
    shape = jax.ShapeDtypeStruct((groups, rows // 2, tile * tiles), LOW)
    return pl.pallas_call(
        lambda info_ref, *refs: rows_kernel(halves, left[3], count, info_ref, *refs[len(after) :]),
        name="rows_grads",
        grid_spec=pltpu.PrefetchScalarGridSpec(
            num_scalar_prefetch=1,
            grid=(groups, tiles),
            in_specs=[ANYWHERE] * len(after)
            + [pl.BlockSpec((None, length, left[1]), lambda g, t, info: (left[0], 0, left[2]))] * count
            + [pl.BlockSpec((None, length, right[1]), lambda g, t, info: (right[0] + g, 0, right[2] + spread * t))]
            * count,
            out_specs=[half, half],
            scratch_shapes=[pltpu.VMEM((count, left[3], length), LOW), pltpu.VMEM((count, rows, length), LOW)],
        ),
        out_shape=[shape, shape],
        compiler_params=pltpu.CompilerParams(
            dimension_semantics=("arbitrary", "arbitrary"), vmem_limit_bytes=40 * 2**20
        ),
        cost_estimate=cost(10),
    )(info, *after, *items, *items)


def halve(after, keep, came, axis):
    def kernel(after_ref, keep_ref, came_ref, *outs):
        total = keep_ref[...].astype(WIDE) + came_ref[...].astype(WIDE)
        if axis is None:
            outs[0][...] = total
        else:
            size = total.shape[axis - 1] // 2
            for i in range(2):
                at = slice(i * size, (i + 1) * size)
                outs[i][...] = low(total[at] if axis == 1 else total[:, at])

    groups, rows, columns = keep.shape
    shape = {None: (rows, columns), 1: (rows // 2, columns), 2: (rows, columns // 2)}[axis]
    count, dtype = (1, WIDE) if axis is None else (2, LOW)
    block = pl.BlockSpec((None, rows, columns), lambda g: (g, 0, 0))
    return pl.pallas_call(
        kernel,
        name="halve",
        grid=(groups,),
        in_specs=[ANYWHERE, block, block],
        out_specs=[pl.BlockSpec((None, *shape), lambda g: (g, 0, 0))] * count,
        out_shape=[jax.ShapeDtypeStruct((groups, *shape), dtype)] * count,
        compiler_params=params(16 * 2**20),
        cost_estimate=cost(2),
    )(after, keep, came)


def tied(*values):
    return lax.optimization_barrier(values)


def exchange(value, axis, apart):
    return lax.ppermute(value, axis, [(i, i ^ apart(i)) for i in range(lax.axis_size(axis))])


def unpack(packed, like):
    found, start = [], 0
    for item in like:
        found.append(packed[start : start + item.size].reshape(item.shape))
        start += item.size
    return found


def pack(items):
    return jnp.concatenate([item.reshape(-1) for item in items])


def local(
    inputs, cotangent, w_qkv, w_beta, conv_taps, w_out, w_gate_up, w_down, norm_gains, out_gains
):
    batches, unused, length, width = inputs.shape
    place = lax.axis_index("section")
    rank, half = place // 2, place % 2
    me, copies = lax.axis_index("dp"), lax.axis_size("dp")
    per = batches // 2
    cube = copies == 8

    def across(value, bits=1):
        return exchange(value, "section", lambda i: bits)

    def flip(value, even, odd):
        return exchange(value, "dp", lambda i: odd if i % 2 else even)

    def by_half(own, other, axis):
        return jnp.where(
            half == 0, jnp.concatenate([own, other], axis), jnp.concatenate([other, own], axis)
        )

    first_apart = 2 + 2 * (me % 2)

    def mine_of(value, axis):
        size = value.shape[axis] // copies
        return lax.dynamic_slice_in_dim(value, me * size, size, axis)

    def collect(came, axis):
        came = jnp.concatenate([came, flip(came, 2, 4)], axis)
        came = jnp.concatenate([came, flip(came, 4, 2)], axis)
        return came, flip(came, 1, 1)

    smalls = [conv_taps, w_beta.astype(WIDE), norm_gains, out_gains]
    others = unpack(across(pack(smalls)), smalls)
    taps = jnp.concatenate([conv_taps, others[0]], 2)
    heads = w_beta.shape[1]
    w_beta = jnp.concatenate([w_beta, low(others[1])], 1)
    w_beta = jnp.pad(w_beta, ((0, 0), (0, LANES - 2 * heads)))
    gains = by_half(norm_gains, others[2], 1)
    out_gain = by_half(out_gains, others[3], 0)[None]
    inner, units = w_out.shape[0], w_down.shape[0]
    tile = w_qkv.shape[2]

    if cube:
        block = width // copies
        core = me % 2
        corner = 2 * ((me // 2 + me // 4) % 2) + core
        quarter, rows = width // 4, inner // 2
        came = across(mine_of(w_qkv, 1))
        came, lift = tied(came, mine_of(w_gate_up, 1))
        lift = across(lift)
        lift, out = tied(lift, lax.dynamic_slice_in_dim(w_out, core * rows, rows, 0))
        out = across(out)
        out, down = tied(out, lax.dynamic_slice_in_dim(w_down, corner * quarter, quarter, 1))
        down = across(down)
        mixer_weights = (w_qkv, w_out, *collect(came, 1), out, flip(out, 1, 1))
        near = flip(lift, 2, 4)
        lift = jnp.concatenate([lift, near], 1)
        far = flip(lift, 4, 2)
        apart = [0, first_apart, 6 - first_apart, 6, 1, 7 - first_apart, 1 + first_apart, 7]
        places = [me ^ bits for bits in apart]
        down_places = [2 * (corner ^ bits) + i for bits in (0, 2, 1, 3) for i in range(2)]
    else:

        def gathered(value):
            return lax.all_gather(across(mine_of(value, 1)), "dp", axis=1, tiled=True)

        def halves_of(value):
            return jnp.split(gathered(value), 2, 1)

        out = lax.all_gather(across(mine_of(w_out, 0)), "dp", axis=0, tiled=True)
        mixer_weights = (w_qkv, w_out, *halves_of(w_qkv), *jnp.split(out, 2, 0))
        feed_weights = (w_gate_up, w_down, *halves_of(w_gate_up), *halves_of(w_down))
        places = down_places = list(range(8))
        core, near = 0, taps
    info = jnp.stack([jnp.asarray(item, jnp.int32) for item in places + [rank == 0] + down_places + [core, 1 - core, rank == 1]])

    def mixer_part(after, stream, *wrap):
        return mixer_forward(info, after, stream, gains[0:1], mixer_weights, w_beta, taps, out_gain, *wrap)

    def feed_back(after, grad, saved, old=None):
        stream, middle, kept, lifted = saved
        return feed_backward(info, after, middle, grad, lifted, gains[1:2], feed_weights, old)

    def mixer_back(after, middle_grad, saved, old=None):
        stream, middle, kept, lifted = saved
        return mixer_backward(
            info, after, stream, middle_grad, kept, gains[0:1], mixer_weights, w_beta, taps, out_gain, old
        )

    def own(value):
        items = lax.dynamic_slice_in_dim(value, half * per, per, 0)
        return [items[i, 0] for i in range(per)]

    up = [(0, 2), (1, 3)]
    streams = own(inputs)
    saved0 = []
    for stream in streams:
        near, *kept = mixer_part(near, stream)
        saved0.append([stream, near, kept])
    if cube:
        far, down, saved0[0][1] = tied(far, down, saved0[0][1])
        lift = jnp.concatenate([lift, far], 1)
        lift_twin = flip(lift, 1, 1)
        down = jnp.concatenate([down, flip(down, 2, 4)], 1)
        down, saved0[-1][1] = tied(down, saved0[-1][1])
        feed_weights = (w_gate_up, w_down, lift, lift_twin, down, flip(down, 1, 1))
    firsts = []
    for saved in saved0:
        result, lifted = feed_forward(info, saved[1], gains[1:2], feed_weights)
        saved.append(lifted)
        firsts.append(result)
    grads = own(cotangent)
    results, returned, feeds, mixes = [], [], [], []
    after = taps
    for index in range(per):
        stream = lax.ppermute(firsts[index], "section", up)
        middle, *kept = mixer_part(after, stream, *([only_second] if index else []))
        if index + 1 < per:
            firsts[index + 1], middle = tied(firsts[index + 1], middle)
        result, lifted = feed_forward(info, middle, gains[1:2], feed_weights, only_second)
        results.append(result)
        saved = [stream, middle, kept, lifted]
        feeds.append(feed_back([taps], grads[index], saved))
        mixes.append(mixer_back((taps, taps, taps), feeds[-1][0], saved))
        after = mixes[-1][0]
        returned.append(lax.ppermute(after, "section", [(2, 0), (3, 1)]))
    feed_twins, mix_twins = [], []
    waited = [mixes[-1][0]]
    for index, (grad, saved) in enumerate(zip(returned, saved0)):
        feeds[index] = feed_back(waited, grad, saved, feeds[index])
        after = (taps, taps, taps)
        if cube:
            feed_twins.append(flip(feeds[index][2], 1, 1))
            if index:
                after = (feed_twins[index - 1], mix_twins[index - 1], taps)
        mixes[index] = mixer_back(after, feeds[index][0], saved, mixes[index])
        waited = [mixes[index][0]]
        if cube:
            mix_twins.append(flip(mixes[index][2], 1, 1))
    feed_all = [feed[2] for feed in feeds] + feed_twins
    held = jnp.stack([jnp.where(rank == 1, result, mix[0]) for result, mix in zip(results, mixes)])
    column = width // 2
    moved = across(lax.dynamic_slice_in_dim(held, (1 - rank) * column, column, 2), 2)
    held = lax.dynamic_slice_in_dim(held, rank * column, column, 2)
    mix_all = [mix[2] for mix in mixes]
    if cube:
        mix_all = mix_all + mix_twins
        plans = (
            (feed_all, (3, units, 0, width), (0, units, 0), 2, 1, units, 2),
            (feed_all, (2, 2 * units, 0, 2 * units), (3, units, 1), 1, 2, width // 2, 2),
            (mix_all, (5, width, 0, width), (0, width, 0), 3, 1, width, 1),
            (mix_all, (3, width, 0, width), (4, width, 0), 1, 2, width, 1),
        )
        after, kept, came = [mixes[-1][1]], [], []
        for index, plan in enumerate(plans):
            keep, send = rows_grads(info, after, *plan)
            after = [keep]
            kept.append(keep)
            came.append(across(send) if index % 2 else flip(send, 2, 4))
        after = kept[-1]
        lifts, downs, qkvs, outs = range(4)

        def turn(which, axis, onward=None):
            nonlocal after
            parts = halve(after, kept[which], came[which], axis)
            after = kept[which] = parts[0]
            if axis is not None:
                came[which] = onward(parts[1])

        def far(value):
            return flip(value, 4, 2)

        def near_flip(value):
            return flip(value, 2, 4)

        marks = [kept[downs]]
        turn(lifts, 1, far)
        turn(downs, 1, near_flip)
        marks.append(after)
        turn(outs, 1, near_flip)
        turn(qkvs, 1, far)
        marks.append(after)
        turn(lifts, 2, across)
        marks.append(after)
        turn(downs, 1, far)
        turn(outs, 1, far)
        marks.append(after)
        turn(qkvs, 2, across)
        marks.append(after)
        turn(lifts, None)
        marks.append(after)
        turn(downs, None)
        turn(outs, None)
        turn(qkvs, None)
        grad_gate_up, grad_down, grad_qkv, grad_out = kept[0], kept[1][0], kept[2], kept[3][0]
    else:

        def tall(items, index):
            return jnp.concatenate([item[index] for item in items], 0)

        def total(value, axis, split):
            value = lax.psum_scatter(low(value), "dp", scatter_dimension=axis, tiled=True)
            size = value.shape[split] // 2
            mine = lax.slice_in_dim(value, 0, size, axis=split)
            theirs = lax.slice_in_dim(value, size, 2 * size, axis=split)
            return mine.astype(WIDE) + across(theirs).astype(WIDE)

        ends = tall(feed_all, 3)
        normed2, grad, normed = ends[:, :width], ends[:, units : units + width], tall(mix_all, 5)
        grad_gate_up = total(jnp.stack([mm_tn(normed2, tall(feed_all, i)) for i in range(2)]), 1, 2)
        grad_qkv = total(jnp.stack([mm_tn(normed, tall(mix_all, i)) for i in range(3)]), 1, 2)
        down = mm_tn(tall(feed_all, 2), grad).reshape(2, units, width)
        out = mm_tn(tall(mix_all, 3), tall(mix_all, 4)).reshape(2, inner, width)
        grad_down, grad_out = total(down, 1, 0)[0], total(out, 1, 0)[0]

    strengths = [mix[3] for mix in mixes]
    if cube:
        strengths[0] = tied(strengths[0], marks[3])[0]
        moved = tied(moved, marks[1])[0]
    d_beta = sum(mm_tn(mix[5], item) for mix, item in zip(mix_all, strengths))[:, : 2 * heads]
    d_taps = sum(mix[4] for mix in mixes)
    d_gains = jnp.concatenate([sum(mix[1] for mix in mixes), sum(feed[1] for feed in feeds)], 0)
    d_out_gain = sum(mix[5] for mix in mixes)

    flat = [d_taps, d_beta, d_gains, d_out_gain]
    packed = pack(flat)
    if cube:
        for bits, mark in zip((1, 2, 4), marks[4:]):
            packed = packed + tied(flip(packed, bits, bits), mark)[0]
    else:
        packed = lax.psum(packed, "dp")
    d_taps, d_beta, d_gains, d_out_gain = unpack(packed, flat)

    def part(value, axis, size):
        return lax.dynamic_slice_in_dim(value, me * size, size, axis)

    def halves(value, axis):
        size = value.shape[axis] // 2
        return [
            lax.dynamic_slice_in_dim(value, which * size, size, axis) for which in (half, 1 - half)
        ]

    pieces = [
        [part(d_taps[:, :, i * inner : (i + 1) * inner], 2, inner // copies) for i in range(2)],
        [part(d_beta[:, i * heads : (i + 1) * heads], 0, width // copies) for i in range(2)],
        [part(item, 1, width // 2 // copies) for item in halves(d_gains, 1)],
        [part(item, 1, LANES // 2 // copies) for item in halves(d_out_gain, 1)],
    ]
    mine = [item[0] for item in pieces]
    came = unpack(across(pack([item[1] for item in pieces])), mine)
    grad_taps, grad_beta, grad_gains, grad_out_gains = [a + b for a, b in zip(mine, came)]

    kinds = jnp.stack([jnp.where(rank == 1, held, moved), jnp.where(rank == 1, moved, held)])
    mine, theirs = [
        lax.dynamic_slice_in_dim(kinds, which * column // 2, column // 2, 3) for which in (half, 1 - half)
    ]
    final_stream, final_grad = by_half(mine, across(theirs), 1)[:, :, None]
    return (
        final_stream,
        final_grad,
        grad_qkv,
        grad_beta,
        grad_taps,
        grad_out,
        grad_gate_up,
        grad_down,
        grad_gains,
        grad_out_gains[0],
    )


def solution(mesh):
    in_specs = (
        P(None, "dp", None, None),
        P(None, "dp", None, None),
        P(None, None, "section"),
        P(None, "section"),
        P(None, None, "section"),
        P("section", None),
        P(None, None, "section"),
        P("section", None),
        P(None, "section"),
        P("section"),
    )
    out_specs = (
        P(None, "dp", None, "section"),
        P(None, "dp", None, "section"),
        P(None, "dp", "section"),
        P("dp", "section"),
        P(None, None, ("section", "dp")),
        P(("section", "dp"), None),
        P(None, "dp", "section"),
        P(("section", "dp"), None),
        P(None, ("section", "dp")),
        P(("section", "dp")),
    )
    return jax.shard_map(local, mesh=mesh, in_specs=in_specs, out_specs=out_specs, check_vma=False)
```

```python
import jax
import jax.numpy as jnp
from jax import lax
from jax.experimental import pallas as pl
from jax.experimental.pallas import tpu as pltpu
from jax.sharding import PartitionSpec as P

SPAN = 64
PAIR = 2 * SPAN
LANES = 128
LOW = jnp.bfloat16
WIDE = jnp.float32
VMEM = 56 * 1024 * 1024


def mm(left, right):
    return lax.dot_general(left, right, (((1,), (0,)), ((), ())), preferred_element_type=WIDE)


def mm_nt(left, right):
    return lax.dot_general(left, right, (((1,), (1,)), ((), ())), preferred_element_type=WIDE)


def mm_tn(left, right):
    return lax.dot_general(left, right, (((0,), (0,)), ((), ())), preferred_element_type=WIDE)


def low(value):
    return value.astype(LOW)


def sigmoid(value):
    return 0.5 * jnp.tanh(0.5 * value) + 0.5


def shift_down(value, steps):
    rows = lax.broadcasted_iota(jnp.int32, value.shape, 0)
    return jnp.where(rows >= steps, pltpu.roll(value, steps, 0), 0.0)


def shift_up(value, steps):
    size = value.shape[0]
    rows = lax.broadcasted_iota(jnp.int32, value.shape, 0)
    return jnp.where(rows < size - steps, pltpu.roll(value, size - steps, 0), 0.0)


def pick_lane(value, lane):
    lanes = lax.broadcasted_iota(jnp.int32, value.shape, 1)
    return jnp.sum(jnp.where(lanes == lane, value, 0.0), axis=1, keepdims=True)


def norm_scale(value, epsilon):
    return lax.rsqrt(jnp.mean(value * value, axis=-1, keepdims=True) + epsilon)


def norm_back(value, gain, grad, epsilon):
    scale = norm_scale(value, epsilon)
    scaled = gain * grad
    inner = jnp.mean(value * scaled, axis=-1, keepdims=True)
    value_grad = scale * (scaled - value * (scale * scale * inner))
    gain_grad = jnp.sum(grad * value * scale, axis=0, keepdims=True)
    return value_grad, gain_grad


def pair_masks():
    rows = lax.broadcasted_iota(jnp.int32, (PAIR, PAIR), 0)
    cols = lax.broadcasted_iota(jnp.int32, (PAIR, PAIR), 1)
    apart = rows ^ cols
    near = apart < SPAN
    return rows, cols, apart, near


def inverse(systems, apart):
    one = (apart == 0).astype(WIDE)
    found = [one - jnp.where(apart == 1, system, 0.0) for system in systems]
    lows = [low(system) for system in systems]
    size = 2
    while size < SPAN:
        level = (apart >= size) & (apart < 2 * size)
        parts = [jnp.where(level, system, jnp.zeros_like(system)) for system in lows]
        heads = [low(item) for item in found]
        steps = [low(mm(head, part)) for head, part in zip(heads, parts)]
        found = [item - mm(step, head) for item, step, head in zip(found, steps, heads)]
        size *= 2
    return found


def conv_silu(linear, taps):
    count = taps.shape[0]
    total = linear * taps[count - 1 : count]
    for back in range(1, count):
        total = total + shift_down(linear, back) * taps[count - 1 - back : count - back]
    return total


def whole(shape):
    return pl.BlockSpec(shape, lambda step, *scalars: (0,) * len(shape))


def tiled(shape, axis):
    return pl.BlockSpec(
        shape, lambda step, *scalars: tuple(step if i == axis else 0 for i in range(len(shape)))
    )


def tiled_old(shape, axis):
    return pl.BlockSpec(
        shape,
        lambda step, info: tuple(step * (1 - info[FIRST]) if i == axis else 0 for i in range(len(shape))),
    )


ANYWHERE = pl.BlockSpec(memory_space=pl.ANY)

FIRST, DOWN, OUT, SECOND = 8, 9, 17, 19


def mixer_copies(info_ref, refs, into_qkv, into_out, sems):
    qkv_ref, out_ref, qkv_came, qkv_twin, out_came, out_twin = refs
    rows = qkv_came.shape[1]
    first, second = pl.ds(0, rows), pl.ds(rows, rows)
    pairs = [
        (qkv_ref, into_qkv.at[0]),
        (out_ref, into_out.at[0]),
        (qkv_came, into_qkv.at[1, :, first]),
        (qkv_twin, into_qkv.at[1, :, second]),
    ]
    rows = out_came.shape[0]
    for index, source in enumerate((out_came, out_twin)):
        place = pl.multiple_of(info_ref[OUT + index] * rows, rows)
        pairs.append((source, into_out.at[1, pl.ds(place, rows)]))
    copies = [pltpu.make_async_copy(*pair, sems.at[i]) for i, pair in enumerate(pairs)]
    return copies[0], copies[1], copies[2:4], copies[4:]


def apart_order(info_ref, value_ref, into_ref, first=0):
    size = value_ref.shape[1] // 8
    for index in range(8):
        place = pl.multiple_of(info_ref[first + index] * size, size)
        into_ref[:, index * size : (index + 1) * size] = value_ref[:, pl.ds(place, size)]


def add_from_apart(info_ref, value_ref, into_ref, first=0):
    size = value_ref.shape[1] // 8
    for index in range(8):
        place = pl.ds(pl.multiple_of(info_ref[first + index] * size, size), size)
        into_ref[:, place] += value_ref[:, index * size : (index + 1) * size]


def start_all(step, copies):
    @pl.when(step == 0)
    def begin():
        for copy in copies:
            copy.start()


def wait_all(step, at, copies):
    @pl.when(step == at)
    def wait():
        for copy in copies:
            copy.wait()


def or_keep(kernel, inputs, outputs, first_kept, in_place=0):
    def either(*refs):
        start = 1 + inputs
        old = refs[start : start + outputs - first_kept]
        rest = refs[start + len(old) :]

        @pl.when(refs[0][FIRST] == 1)
        def compute():
            kernel(*refs[:start], *rest)

        @pl.when(refs[0][FIRST] == 0)
        def keep():
            for source, target in zip(old[: len(old) - in_place], rest[first_kept:outputs]):
                target[...] = source[...]

    return either


def only_second(kernel):
    def either(info_ref, *refs):
        @pl.when(info_ref[SECOND] == 1)
        def compute():
            kernel(info_ref, *refs)

    return either


def mixer_forward_kernel(
    step,
    info_ref,
    stream_ref,
    gain_ref,
    w_beta_ref,
    taps_ref,
    out_gain_ref,
    qkv_own_ref,
    out_own_ref,
    qkv_came_ref,
    qkv_twin_ref,
    out_came_ref,
    out_twin_ref,
    middle_ref,
    strengths_ref,
    linear_ref,
    out_ref,
    fresh_ref,
    solve_ref,
    states_ref,
    moves_ref,
    normed_ref,
    w_qkv_ref,
    w_out_ref,
    sems,
):
    length = stream_ref.shape[0]
    spans = length // SPAN
    heads = linear_ref.shape[2] // LANES
    refs = (qkv_own_ref, out_own_ref, qkv_came_ref, qkv_twin_ref, out_came_ref, out_twin_ref)
    own_qkv, own_out, qkv, out = mixer_copies(info_ref, refs, w_qkv_ref, w_out_ref, sems)
    start_all(step, [own_qkv, own_out])

    @pl.when(step == 0)
    def first():
        stream = stream_ref[...].astype(WIDE)
        normed_ref[0] = low(stream * norm_scale(stream, 1e-6) * gain_ref[...])
        apart_order(info_ref, normed_ref.at[0], normed_ref.at[1])
        strengths_ref[...] = mm(normed_ref[0], w_beta_ref[...])
        middle_ref[...] = stream

    normed = normed_ref[step]
    wait_all(step, 0, [own_qkv, own_out])
    wait_all(step, 1, qkv + out)
    start_all(step, qkv + out)
    active = []
    for which in range(3):
        linear = mm(normed, w_qkv_ref[step, which])
        linear_ref[which] = low(linear)
        total = conv_silu(linear, taps_ref[which])
        active.append(total * sigmoid(total))
    rows, cols, apart, near = pair_masks()
    strict = (rows > cols) & near
    lower = (rows >= cols) & near
    queries, keys, values, betas = [], [], [], []
    for head in range(heads):
        lanes = slice(head * LANES, (head + 1) * LANES)
        query, key = active[0][:, lanes], active[1][:, lanes]
        queries.append(low(query * lax.rsqrt(jnp.sum(query * query, axis=1, keepdims=True) + 1e-6)))
        keys.append(low(key * lax.rsqrt(jnp.sum(key * key, axis=1, keepdims=True) + 1e-6)))
        values.append(low(active[2][:, lanes]))
        betas.append(sigmoid(pick_lane(strengths_ref[...], step * heads + head)))
    cells = [(head, pair) for head in range(heads) for pair in range(length // PAIR)]

    def part(array, pair):
        return array[pair * PAIR : (pair + 1) * PAIR]

    systems = []
    for head, pair in cells:
        key = part(keys[head], pair)
        systems.append(jnp.where(strict, mm_nt(key, key) * part(betas[head], pair), 0.0))
    solved = [low(item) for item in inverse(systems, apart)]
    both = {}
    scores = {}
    for (head, pair), solve in zip(cells, solved):
        solve_ref[head, pair] = solve
        beta = part(betas[head], pair)
        key = part(keys[head], pair)
        right = jnp.concatenate(
            [low(beta * key.astype(WIDE)), low(beta * part(values[head], pair).astype(WIDE))], axis=1
        )
        both[head, pair] = mm(solve, right)
        scores[head, pair] = low(jnp.where(lower, mm_nt(part(queries[head], pair), key), 0.0))

    def span_of(array, span):
        return array[span * SPAN : (span + 1) * SPAN]

    def both_of(head, span):
        return span_of(both[head, span // 2], span % 2)

    states = [[None] * spans for head in range(heads)]
    turns = {}
    for head in range(heads):
        for span in range(spans - 1):
            turns[head, span] = mm_tn(span_of(keys[head], span), low(both_of(head, span)))
    for span in range(1, spans):
        for head in range(heads):
            turn = turns[head, span - 1]
            if span == 1:
                states[head][span] = turn[:, LANES:]
            else:
                before = states[head][span - 1]
                move = low(turn[:, :LANES])
                moves_ref[head, span - 2] = move
                states[head][span] = before + turn[:, LANES:] - mm(move, low(before))
    fresh = {}
    carried = {}
    for head in range(heads):
        for span in range(spans):
            item = both_of(head, span)
            if span == 0:
                fresh[head, span] = low(item[:, LANES:])
                carried[head, span] = jnp.zeros((SPAN, LANES), WIDE)
            else:
                state = low(states[head][span])
                states_ref[head, span - 1] = state
                left = jnp.concatenate([low(item[:, :LANES]), span_of(queries[head], span)], axis=0)
                seen = mm(left, state)
                fresh[head, span] = low(item[:, LANES:] - seen[:SPAN])
                carried[head, span] = seen[SPAN:]
    normed_out = []
    for head in range(heads):
        lanes = slice(head * LANES, (head + 1) * LANES)
        pieces = []
        for pair in range(length // PAIR):
            piece = jnp.concatenate([fresh[head, 2 * pair], fresh[head, 2 * pair + 1]], axis=0)
            fresh_ref[pair * PAIR : (pair + 1) * PAIR, lanes] = piece
            base = jnp.concatenate([carried[head, 2 * pair], carried[head, 2 * pair + 1]], axis=0)
            pieces.append(base + mm(scores[head, pair], piece))
        output = jnp.concatenate(pieces, axis=0)
        out_ref[:, lanes] = low(output)
        normed_out.append(low(output * norm_scale(output, 1e-5) * out_gain_ref[...]))
    middle_ref[...] += mm(jnp.concatenate(normed_out, axis=1), w_out_ref[step])


def cost(micros):
    return pl.CostEstimate(flops=int(micros * 1.1e9), bytes_accessed=2**20, transcendentals=0)


def params(limit=VMEM, **extra):
    return pltpu.CompilerParams(dimension_semantics=("arbitrary",), vmem_limit_bytes=limit, **extra)


def mixer_forward(info, after, stream, gain, weights, w_beta, taps, out_gain, wrap=lambda kernel: kernel):
    length, width = stream.shape
    tile = weights[0].shape[2]
    inner = 2 * tile
    heads = inner // LANES
    spans = length // SPAN
    pairs = length // PAIR
    here = tile // LANES
    out = jax.ShapeDtypeStruct
    return pl.pallas_call(
        wrap(lambda info_ref, after_ref, *refs: mixer_forward_kernel(pl.program_id(0), info_ref, *refs)),
        name="mixer_forward",
        grid_spec=pltpu.PrefetchScalarGridSpec(
            num_scalar_prefetch=1,
            grid=(2,),
            in_specs=[
                ANYWHERE,
                whole((length, width)),
                whole((1, width)),
                whole((width, LANES)),
                tiled((3, taps.shape[1], tile), 2),
                whole((1, LANES)),
            ]
            + [ANYWHERE] * 6,
            out_specs=[
                whole((length, width)),
                whole((length, LANES)),
                tiled((3, length, tile), 2),
                tiled((length, tile), 1),
                tiled((length, tile), 1),
                tiled((here, pairs, PAIR, PAIR), 0),
                tiled((here, spans - 1, LANES, LANES), 0),
                tiled((here, spans - 2, LANES, LANES), 0),
            ],
            scratch_shapes=[
                pltpu.VMEM((2, length, width), LOW),
                pltpu.VMEM((2, 3, width, tile), LOW),
                pltpu.VMEM((2, tile, width), LOW),
                pltpu.SemaphoreType.DMA((6,)),
            ],
        ),
        out_shape=[
            out((length, width), WIDE),
            out((length, LANES), WIDE),
            out((3, length, inner), LOW),
            out((length, inner), LOW),
            out((length, inner), LOW),
            out((heads, pairs, PAIR, PAIR), LOW),
            out((heads, spans - 1, LANES, LANES), LOW),
            out((heads, spans - 2, LANES, LANES), LOW),
        ],
        compiler_params=params(),
        cost_estimate=cost(14),
    )(info, after, stream, gain, w_beta, taps, out_gain, *weights)


def mixer_backward_kernel(
    step,
    load,
    info_ref,
    stream_ref,
    branch_ref,
    strengths_ref,
    linear_ref,
    out_ref,
    fresh_ref,
    solve_ref,
    states_ref,
    moves_ref,
    gain_ref,
    w_beta_ref,
    taps_ref,
    out_gain_ref,
    qkv_own_ref,
    out_own_ref,
    qkv_came_ref,
    qkv_twin_ref,
    out_came_ref,
    out_twin_ref,
    stream_grad_ref,
    gain_grad_ref,
    stack_ref,
    strengths_grad_ref,
    taps_grad_ref,
    out_gain_grad_ref,
    normed_grad_ref,
    strengths_sum_ref,
    branch_low_ref,
    normed_ref,
    w_qkv_ref,
    w_out_ref,
    sems,
):
    length = stream_ref.shape[0]
    spans = length // SPAN
    pairs = length // PAIR
    tile = stack_ref.shape[2]
    heads = tile // LANES
    if load:
        refs = (qkv_own_ref, out_own_ref, qkv_came_ref, qkv_twin_ref, out_came_ref, out_twin_ref)
        own_qkv, own_out, qkv, out = mixer_copies(info_ref, refs, w_qkv_ref, w_out_ref, sems)
        start_all(step, [own_out, own_qkv])

    @pl.when(step == 0)
    def first():
        branch_low_ref[...] = low(branch_ref[...])
        stream = stream_ref[...].astype(WIDE)
        normed_ref[...] = low(stream * norm_scale(stream, 1e-6) * gain_ref[...])
        out_gain_grad_ref[...] = jnp.zeros_like(out_gain_grad_ref)
        strengths_sum_ref[...] = jnp.zeros_like(strengths_sum_ref)
        normed_grad_ref[...] = jnp.zeros_like(normed_grad_ref)

    columns = pl.ds(pl.multiple_of(step * tile, tile), tile)
    stack_ref[4] = branch_low_ref[:, columns]
    stack_ref[5] = normed_ref[:, columns]
    rows, cols, apart, near = pair_masks()
    strict = (rows > cols) & near
    lower = (rows >= cols) & near
    upper_strict = (rows < cols) & near
    upper = (rows <= cols) & near
    cells = [(head, pair) for head in range(heads) for pair in range(pairs)]

    def part(array, pair):
        return array[pair * PAIR : (pair + 1) * PAIR]

    def span_of(array, span):
        return array[span * SPAN : (span + 1) * SPAN]

    if load:
        wait_all(step, 0, [own_out, own_qkv])
        wait_all(step, 1, out + qkv)
        start_all(step, out + qkv)
    normed_out_grad = mm_nt(branch_low_ref[...], w_out_ref[step])
    totals, gates, active = [], [], []
    for which in range(3):
        total = conv_silu(linear_ref[which].astype(WIDE), taps_ref[which])
        gate = sigmoid(total)
        totals.append(total)
        gates.append(gate)
        active.append(total * gate)
    query_scales, key_scales = [], []
    queries, keys, values, betas, output_grads = [], [], [], [], []
    for head in range(heads):
        lanes = slice(head * LANES, (head + 1) * LANES)
        query, key = active[0][:, lanes], active[1][:, lanes]
        query_scales.append(lax.rsqrt(jnp.sum(query * query, axis=1, keepdims=True) + 1e-6))
        key_scales.append(lax.rsqrt(jnp.sum(key * key, axis=1, keepdims=True) + 1e-6))
        queries.append(low(query * query_scales[head]))
        keys.append(low(key * key_scales[head]))
        values.append(low(active[2][:, lanes]))
        betas.append(sigmoid(pick_lane(strengths_ref[...], step * heads + head)))
        output = out_ref[:, lanes].astype(WIDE)
        scale = norm_scale(output, 1e-5)
        grad = normed_out_grad[:, lanes]
        stack_ref[3, :, lanes] = low(output * scale * out_gain_ref[...])
        scaled = out_gain_ref[...] * grad
        inner = jnp.mean(output * scaled, axis=1, keepdims=True)
        output_grads.append(low(scale * (scaled - output * (scale * scale * inner))))
        out_gain_grad_ref[...] += jnp.sum(grad * output * scale, axis=0, keepdims=True)
    fresh = [fresh_ref[:, head * LANES : (head + 1) * LANES] for head in range(heads)]

    scores_back, score_grads, score_grads_back = {}, {}, {}
    for head, pair in cells:
        query, key = part(queries[head], pair), part(keys[head], pair)
        grad, new = part(output_grads[head], pair), part(fresh[head], pair)
        scores_back[head, pair] = low(jnp.where(upper, mm_nt(key, query), 0.0))
        score_grads[head, pair] = low(jnp.where(lower, mm_nt(grad, new), 0.0))
        score_grads_back[head, pair] = low(jnp.where(upper, mm_nt(new, grad), 0.0))
    inside, early = {}, {}
    for head, pair in cells:
        inside[head, pair] = mm(scores_back[head, pair], part(output_grads[head], pair))
    for head, pair in cells:
        early[head, pair] = mm_tn(solve_ref[head, pair], low(inside[head, pair]))
    returns = {}
    for head in range(heads):
        for span in range(1, spans):
            beta = span_of(betas[head], span)
            back = low(-beta * span_of(early[head, span // 2], span % 2))
            left = jnp.concatenate([span_of(queries[head], span), span_of(keys[head], span)], axis=0)
            right = jnp.concatenate([span_of(output_grads[head], span), back], axis=0)
            returns[head, span] = mm_tn(left, right)
    state_grads = {}
    for span in range(spans - 2, -1, -1):
        for head in range(heads):
            if span == spans - 2:
                state_grads[head, span] = returns[head, span + 1]
            else:
                after = state_grads[head, span + 1]
                state_grads[head, span] = (
                    after + returns[head, span + 1] - mm_tn(moves_ref[head, span], low(after))
                )
    fresh_add = {}
    for head, pair in cells:
        pieces = []
        for span in (2 * pair, 2 * pair + 1):
            if span == spans - 1:
                pieces.append(jnp.zeros((SPAN, LANES), WIDE))
            else:
                pieces.append(mm(span_of(keys[head], span), low(state_grads[head, span])))
        fresh_add[head, pair] = low(jnp.concatenate(pieces, axis=0))
    lasts, backs = {}, {}
    for head, pair in cells:
        last = early[head, pair] + mm_tn(solve_ref[head, pair], fresh_add[head, pair])
        lasts[head, pair] = last
        backs[head, pair] = part(betas[head], pair) * last
    system_grads, system_grads_back = {}, {}
    for head, pair in cells:
        last, new = low(lasts[head, pair]), part(fresh[head], pair)
        system_grads[head, pair] = low(jnp.where(strict, -mm_nt(last, new), 0.0))
        system_grads_back[head, pair] = low(jnp.where(upper_strict, -mm_nt(new, last), 0.0))
    query_grads, key_grads, beta_grads = [], [], []
    for head in range(heads):
        query_pieces, key_pieces, beta_pieces = [], [], []
        for pair in range(pairs):
            query, key = part(queries[head], pair), part(keys[head], pair)
            beta, new = part(betas[head], pair), part(fresh[head], pair)
            grad = part(output_grads[head], pair)
            stacked = jnp.concatenate(
                [score_grads[head, pair], system_grads[head, pair]], axis=0
            )
            through = mm(stacked, key)
            query_grad = through[:PAIR]
            key_grad = beta * through[PAIR:]
            wide = jnp.concatenate(
                [score_grads_back[head, pair], system_grads_back[head, pair]], axis=1
            )
            tall = jnp.concatenate([query, low(beta * key.astype(WIDE))], axis=0)
            key_grad = key_grad + mm(wide, tall)
            inner = low(jnp.where(strict, mm_nt(key, key), 0.0))
            residual = part(values[head], pair).astype(WIDE) - mm(inner, new)
            back = low(backs[head, pair])
            more_query, more_key, seen = [], [], []
            for local_span in range(2):
                span = 2 * pair + local_span
                new_span = span_of(new, local_span)
                if span == 0:
                    more_query.append(jnp.zeros((SPAN, LANES), WIDE))
                    seen.append(jnp.zeros((SPAN, LANES), WIDE))
                    more_key.append(mm_nt(new_span, low(state_grads[head, span])))
                    continue
                state = states_ref[head, span - 1]
                more_query.append(mm_nt(span_of(grad, local_span), state))
                seen.append(mm(span_of(key, local_span), state))
                taken = -span_of(back, local_span)
                if span == spans - 1:
                    more_key.append(mm_nt(taken, state))
                else:
                    left = jnp.concatenate([new_span, taken], axis=1)
                    right = jnp.concatenate([low(state_grads[head, span]), state], axis=1)
                    more_key.append(mm_nt(left, right))
            residual = residual - jnp.concatenate(seen, axis=0)
            query_pieces.append(query_grad + jnp.concatenate(more_query, axis=0))
            key_pieces.append(key_grad + jnp.concatenate(more_key, axis=0))
            beta_pieces.append(jnp.sum(lasts[head, pair] * residual, axis=1, keepdims=True))
        query_grads.append(jnp.concatenate(query_pieces, axis=0))
        key_grads.append(jnp.concatenate(key_pieces, axis=0))
        beta_grads.append(jnp.concatenate(beta_pieces, axis=0))
    lane_ids = lax.broadcasted_iota(jnp.int32, (length, LANES), 1)
    strengths_sum = strengths_sum_ref[...]
    for head in range(heads):
        beta = betas[head]
        strengths_sum = strengths_sum + jnp.where(
            lane_ids == step * heads + head, beta_grads[head] * beta * (1.0 - beta), 0.0
        )
    strengths_sum_ref[...] = strengths_sum

    active_grads = []
    for grads, scales, source in ((query_grads, query_scales, active[0]), (key_grads, key_scales, active[1])):
        pieces = []
        for head in range(heads):
            lanes = slice(head * LANES, (head + 1) * LANES)
            value, scale, grad = source[:, lanes], scales[head], grads[head]
            inner = jnp.sum(value * grad, axis=1, keepdims=True)
            pieces.append(scale * (grad - value * (scale * scale * inner)))
        active_grads.append(jnp.concatenate(pieces, axis=1))
    active_grads.append(
        jnp.concatenate(
            [jnp.concatenate([backs[head, pair] for pair in range(pairs)], axis=0) for head in range(heads)],
            axis=1,
        )
    )
    normed_grad = normed_grad_ref[step]
    for which in range(3):
        total, gate = totals[which], gates[which]
        total_grad = active_grads[which] * (gate * (1.0 + total * (1.0 - gate)))
        taps = taps_ref[which]
        linear = linear_ref[which].astype(WIDE)
        count = taps.shape[0]
        linear_grad = total_grad * taps[count - 1 : count]
        taps_grad_ref[which, count - 1 : count] = jnp.sum(total_grad * linear, axis=0, keepdims=True)
        for ahead in range(1, count):
            moved = shift_up(total_grad, ahead)
            place = slice(count - 1 - ahead, count - ahead)
            linear_grad = linear_grad + moved * taps[place]
            taps_grad_ref[which, place] = jnp.sum(moved * linear, axis=0, keepdims=True)
        linear_low = low(linear_grad)
        stack_ref[which] = linear_low
        normed_grad = normed_grad + mm_nt(linear_low, w_qkv_ref[step, which])
    normed_grad_ref[step] = normed_grad

    @pl.when(step == 1)
    def last_step():
        strengths_low = low(strengths_sum_ref[...])
        strengths_grad_ref[...] = strengths_low
        add_from_apart(info_ref, normed_grad_ref.at[1], normed_grad_ref.at[0])
        total = normed_grad_ref[0] + mm_nt(strengths_low, w_beta_ref[...])
        value_grad, gain_grad = norm_back(stream_ref[...].astype(WIDE), gain_ref[...], total, 1e-6)
        stream_grad_ref[...] = low(branch_ref[...] + value_grad)
        gain_grad_ref[...] = gain_grad


def mixer_backward(info, after, stream, branch, kept, gain, weights, w_beta, taps, out_gain, old):
    strengths, linear, output, fresh, solve, states, moves = kept
    length, width = stream.shape
    tile = weights[0].shape[2]
    inner = 2 * tile
    spans = length // SPAN
    pairs = length // PAIR
    here = tile // LANES
    out = jax.ShapeDtypeStruct
    count = taps.shape[1]
    in_specs = [
        ANYWHERE,
        ANYWHERE,
        ANYWHERE,
        whole((length, width)),
        whole((length, width)),
        whole((length, LANES)),
        tiled((3, length, tile), 2),
        tiled((length, tile), 1),
        tiled((length, tile), 1),
        tiled((here, pairs, PAIR, PAIR), 0),
        tiled((here, spans - 1, LANES, LANES), 0),
        tiled((here, spans - 2, LANES, LANES), 0),
        whole((1, width)),
        whole((width, LANES)),
        tiled((3, count, tile), 2),
        whole((1, LANES)),
    ] + [ANYWHERE] * 6
    body = lambda info_ref, *refs: mixer_backward_kernel(pl.program_id(0), True, info_ref, *refs[3:])
    kernel = or_keep(body, len(in_specs), 6, 1)
    more = old[1:]
    in_specs = in_specs + [
        whole((1, width)),
        tiled_old((6, length, tile), 2),
        whole((length, LANES)),
        tiled_old((3, count, tile), 2),
        whole((1, LANES)),
    ]
    return pl.pallas_call(
        kernel,
        name="mixer_backward",
        grid_spec=pltpu.PrefetchScalarGridSpec(
            num_scalar_prefetch=1,
            grid=(2,),
            in_specs=in_specs,
            out_specs=[
                whole((length, width)),
                whole((1, width)),
                tiled((6, length, tile), 2),
                whole((length, LANES)),
                tiled((3, count, tile), 2),
                whole((1, LANES)),
            ],
            scratch_shapes=[
                pltpu.VMEM((2, length, width), WIDE),
                pltpu.VMEM((length, LANES), WIDE),
                pltpu.VMEM((length, width), LOW),
                pltpu.VMEM((length, width), LOW),
                pltpu.VMEM((2, 3, width, tile), LOW),
                pltpu.VMEM((2, tile, width), LOW),
                pltpu.SemaphoreType.DMA((6,)),
            ],
        ),
        out_shape=[
            out((length, width), LOW),
            out((1, width), WIDE),
            out((6, length, inner), LOW),
            out((length, LANES), LOW),
            out((3, count, inner), WIDE),
            out((1, LANES), WIDE),
        ],
        compiler_params=params(),
        cost_estimate=cost(20),
    )(
        info, *after, stream, branch, strengths, linear, output, fresh, solve, states, moves,
        gain, w_beta, taps, out_gain, *weights, *more,
    )


def unit_tiles(units):
    count = -(-units // 512)
    size = -(-units // count // LANES) * LANES
    return [(start, min(size, units - start)) for start in range(0, units, size)]


def feed_tiles(refs, into_lift, into_down, sems):
    lift_ref, down_ref, lift_came, lift_twin, down_came, down_twin = refs
    tiles, at = [], 0
    for which in range(2):
        for start, size in unit_tiles(down_ref.shape[0]):
            span = pl.ds(start, size)
            if which == 0:
                lift = [(lift_ref.at[:, :, span], into_lift.at[0, :, :, span])]
                down = [(down_ref.at[span], into_down.at[0, span])]
            else:
                rows, columns = lift_came.shape[1], down_came.shape[1]
                lift = [
                    (lift_came.at[:, :, span], into_lift.at[1, :, pl.ds(0, rows), span]),
                    (lift_twin.at[:, :, span], into_lift.at[1, :, pl.ds(rows, rows), span]),
                ]
                down = [
                    (down_came.at[span], into_down.at[1, span, pl.ds(0, columns)]),
                    (down_twin.at[span], into_down.at[1, span, pl.ds(columns, columns)]),
                ]
            copies = []
            for group in (lift, down):
                copies.append([pltpu.make_async_copy(*pair, sems.at[at + i]) for i, pair in enumerate(group)])
                at += len(group)
            tiles.append((which, start, size, copies[0], copies[1]))
    return tiles


def start_each(copies):
    for copy in copies:
        copy.start()


def wait_each(copies):
    for copy in copies:
        copy.wait()


AHEAD = 3


def feed_forward_kernel(
    alone,
    info_ref,
    middle_ref,
    gain_ref,
    lift_own_ref,
    down_own_ref,
    lift_came_ref,
    lift_twin_ref,
    down_came_ref,
    down_twin_ref,
    result_ref,
    lifted_ref,
    total_ref,
    normed_ref,
    w_gate_up_ref,
    w_down_ref,
    kept_ref,
    sems,
    out_sems,
):
    units = down_own_ref.shape[0]
    refs = (lift_own_ref, down_own_ref, lift_came_ref, lift_twin_ref, down_came_ref, down_twin_ref)
    tiles = feed_tiles(refs, w_gate_up_ref, w_down_ref, sems)
    if alone:
        for tile in tiles[:AHEAD]:
            start_each(tile[3] + tile[4])
    middle = middle_ref[...]
    normed_ref[0] = low(middle * norm_scale(middle, 1e-6) * gain_ref[...])
    apart_order(info_ref, normed_ref.at[0], normed_ref.at[1])
    outs = []
    lifted = []
    for index in range(len(tiles) + 1):
        if index < len(tiles):
            which, start, size, lift, down = tiles[index]
            wait_each(lift)
        if index:
            wait_each(tiles[index - 1][4])
        if 0 < index <= len(tiles) - AHEAD:
            start_each(tiles[index + AHEAD - 1][3] + tiles[index + AHEAD - 1][4])
        if index < len(tiles):
            span = pl.ds(start, size)
            normed = normed_ref[which]
            gate = mm(normed, w_gate_up_ref[which, 0, :, span])
            up = mm(normed, w_gate_up_ref[which, 1, :, span])
            place = pl.ds(which * units + start, size)
            kept_ref[0, :, place] = low(gate)
            kept_ref[1, :, place] = low(up)
            lifted.append((gate, up))
        if index:
            which, start, size, lift, down = tiles[index - 1]
            span = pl.ds(start, size)
            place = pl.ds(which * units + start, size)
            if alone:
                outs.append(
                    pltpu.make_async_copy(
                        kept_ref.at[:, :, place], lifted_ref.at[:, :, place], out_sems.at[index - 1]
                    )
                )
                outs[-1].start()
            gate, up = lifted[index - 1]
            hidden = low(gate * sigmoid(gate) * up)
            part = mm(hidden, w_down_ref[which, span, :])
            if start:
                total_ref[which] += part
            else:
                total_ref[which] = part + middle if which == 0 else part
    add_from_apart(info_ref, total_ref.at[1], total_ref.at[0], DOWN)
    result_ref[...] = low(total_ref[0])
    wait_each(outs)


def feed_forward(info, middle, gain, weights, wrap=lambda kernel: kernel):
    length, width = middle.shape
    units = weights[1].shape[0]
    count = 2 * len(unit_tiles(units))
    out = jax.ShapeDtypeStruct
    return pl.pallas_call(
        wrap(lambda *refs: feed_forward_kernel(True, *refs)),
        name="feed_forward",
        grid_spec=pltpu.PrefetchScalarGridSpec(
            num_scalar_prefetch=1,
            grid=(1,),
            in_specs=[whole((length, width)), whole((1, width))] + [ANYWHERE] * 6,
            out_specs=[whole((length, width)), ANYWHERE],
            scratch_shapes=[
                pltpu.VMEM((2, length, width), WIDE),
                pltpu.VMEM((2, length, width), LOW),
                pltpu.VMEM((2, 2, width, units), LOW),
                pltpu.VMEM((2, units, width), LOW),
                pltpu.VMEM((2, length, 2 * units), LOW),
                pltpu.SemaphoreType.DMA((3 * count,)),
                pltpu.SemaphoreType.DMA((count,)),
            ],
        ),
        out_shape=[out((length, width), LOW), out((2, length, 2 * units), LOW)],
        compiler_params=params(),
        cost_estimate=cost(10),
    )(info, middle, gain, *weights)


def feed_backward_kernel(
    alone,
    info_ref,
    middle_ref,
    grad_ref,
    gain_ref,
    lifted_ref,
    lift_own_ref,
    down_own_ref,
    lift_came_ref,
    lift_twin_ref,
    down_came_ref,
    down_twin_ref,
    middle_grad_ref,
    gain_grad_ref,
    stack_ref,
    normed_grad_ref,
    grads_ref,
    w_gate_up_ref,
    w_down_ref,
    kept_ref,
    made_ref,
    sems,
    in_sems,
    out_sems,
):
    width = middle_ref.shape[1]
    units = down_own_ref.shape[0]
    refs = (lift_own_ref, down_own_ref, lift_came_ref, lift_twin_ref, down_came_ref, down_twin_ref)
    tiles = feed_tiles(refs, w_gate_up_ref, w_down_ref, sems)
    ins, outs = [], []
    for index, (which, start, size, lift, down) in enumerate(tiles):
        place = pl.ds(which * units + start, size)
        if alone:
            ins.append(
                pltpu.make_async_copy(lifted_ref.at[:, :, place], kept_ref.at[:, :, place], in_sems.at[index])
            )
        first, at = pl.ds(0, 2), out_sems.at
        outs.append(
            [
                pltpu.make_async_copy(kept_ref.at[:, :, place], stack_ref.at[first, :, place], at[2 * index]),
                pltpu.make_async_copy(made_ref.at[0, :, place], stack_ref.at[2, :, place], at[2 * index + 1]),
            ]
        )
    for index in range(AHEAD if alone else 0):
        start_each(tiles[index][4] + [ins[index]] + tiles[index][3])
    middle = middle_ref[...]
    made_ref[1] = jnp.zeros(made_ref.shape[1:], LOW)
    made_ref[1, :, :width] = low(middle * norm_scale(middle, 1e-6) * gain_ref[...])
    made_ref[1, :, units : units + width] = grad_ref[...]
    ends = pltpu.make_async_copy(made_ref.at[1], stack_ref.at[3], out_sems.at[2 * len(tiles)])
    ends.start()
    grads_ref[0] = grad_ref[...]
    apart_order(info_ref, grads_ref.at[0], grads_ref.at[1], DOWN)
    hidden_grads = []
    for index in range(len(tiles) + 1):
        if index < len(tiles):
            which, start, size, lift, down = tiles[index]
            if alone:
                wait_each(down)
        if index and alone:
            ins[index - 1].wait()
            wait_each(tiles[index - 1][3])
        if alone and 0 < index <= len(tiles) - AHEAD:
            more = index + AHEAD - 1
            start_each(tiles[more][4] + [ins[more]] + tiles[more][3])
        if index < len(tiles):
            span = pl.ds(start, size)
            hidden_grads.append(mm_nt(grads_ref[which], w_down_ref[which, span, :]))
        if index:
            which, start, size, lift, down = tiles[index - 1]
            span = pl.ds(start, size)
            place = pl.ds(which * units + start, size)
            hidden_grad = hidden_grads[index - 1]
            gate = kept_ref[0, :, place].astype(WIDE)
            up = kept_ref[1, :, place].astype(WIDE)
            open_ = sigmoid(gate)
            silu = gate * open_
            up_grad = low(hidden_grad * silu)
            gate_grad = low(hidden_grad * up * (open_ + silu * (1.0 - open_)))
            kept_ref[0, :, place] = gate_grad
            kept_ref[1, :, place] = up_grad
            made_ref[0, :, place] = low(silu * up)
            start_each(outs[index - 1])
            part = mm_nt(gate_grad, w_gate_up_ref[which, 0, :, span]) + mm_nt(
                up_grad, w_gate_up_ref[which, 1, :, span]
            )
            if start:
                normed_grad_ref[which] += part
            else:
                normed_grad_ref[which] = part
    add_from_apart(info_ref, normed_grad_ref.at[1], normed_grad_ref.at[0])
    value_grad, gain_grad = norm_back(middle, gain_ref[...], normed_grad_ref[0], 1e-6)
    middle_grad_ref[...] = grad_ref[...].astype(WIDE) + value_grad
    gain_grad_ref[...] = gain_grad
    for copies in outs:
        wait_each(copies)
    ends.wait()


def feed_backward(info, after, middle, grad, lifted, gain, weights, old):
    length, width = middle.shape
    units = weights[1].shape[0]
    count = 2 * len(unit_tiles(units))
    out = jax.ShapeDtypeStruct
    waits = len(after)
    in_specs = [ANYWHERE] * waits + [whole((length, width)), whole((length, width)), whole((1, width))] + [ANYWHERE] * 7
    body = lambda info_ref, *refs: feed_backward_kernel(True, info_ref, *refs[waits:])
    kernel = or_keep(body, len(in_specs), 3, 1, 1)
    in_specs = in_specs + [whole((1, width)), ANYWHERE]
    more, aliases = old[1:], {len(in_specs): 2}
    return pl.pallas_call(
        kernel,
        name="feed_backward",
        grid_spec=pltpu.PrefetchScalarGridSpec(
            num_scalar_prefetch=1,
            grid=(1,),
            in_specs=in_specs,
            out_specs=[whole((length, width)), whole((1, width)), ANYWHERE],
            scratch_shapes=[
                pltpu.VMEM((2, length, width), WIDE),
                pltpu.VMEM((2, length, width), LOW),
                pltpu.VMEM((2, 2, width, units), LOW),
                pltpu.VMEM((2, units, width), LOW),
                pltpu.VMEM((2, length, 2 * units), LOW),
                pltpu.VMEM((2, length, 2 * units), LOW),
                pltpu.SemaphoreType.DMA((3 * count,)),
                pltpu.SemaphoreType.DMA((count,)),
                pltpu.SemaphoreType.DMA((2 * count + 1,)),
            ],
        ),
        out_shape=[
            out((length, width), WIDE),
            out((1, width), WIDE),
            out((4, length, 2 * units), LOW),
        ],
        input_output_aliases=aliases,
        compiler_params=params(),
        cost_estimate=cost(13),
    )(info, *after, middle, grad, gain, lifted, *weights, *more)


def second_layer_kernel(
    info_ref,
    after_ref,
    stream_ref,
    grad_ref,
    gain_ref,
    feed_gain_ref,
    w_beta_ref,
    taps_ref,
    out_gain_ref,
    qkv_own_ref,
    out_own_ref,
    qkv_came_ref,
    qkv_twin_ref,
    out_came_ref,
    out_twin_ref,
    lift_own_ref,
    down_own_ref,
    lift_came_ref,
    lift_twin_ref,
    down_came_ref,
    down_twin_ref,
    result_ref,
    stream_grad_ref,
    feed_gain_grad_ref,
    gain_grad_ref,
    strengths_grad_ref,
    taps_grad_ref,
    out_gain_grad_ref,
    feed_stack_ref,
    stack_ref,
    middle_ref,
    branch_ref,
    strengths_ref,
    linear_ref,
    out_ref,
    fresh_ref,
    solve_ref,
    states_ref,
    moves_ref,
    normed_ref,
    w_qkv_ref,
    w_out_ref,
    totals_ref,
    lows_ref,
    w_gate_up_ref,
    w_down_ref,
    kept_ref,
    made_ref,
    strengths_sum_ref,
    branch_low_ref,
    again_ref,
    stacks_ref,
    sems,
    feed_sems,
    out_sems,
    stack_sems,
):
    turn = pl.program_id(0)
    tile = taps_ref.shape[3]
    mixer_weights = (qkv_own_ref, out_own_ref, qkv_came_ref, qkv_twin_ref, out_came_ref, out_twin_ref)
    feed_weights = (lift_own_ref, down_own_ref, lift_came_ref, lift_twin_ref, down_came_ref, down_twin_ref)
    tiles = feed_tiles(feed_weights, w_gate_up_ref, w_down_ref, feed_sems)

    def leave(which):
        columns = pl.ds(which * tile, tile)
        return pltpu.make_async_copy(stacks_ref.at[which], stack_ref.at[:, :, columns], stack_sems.at[which])

    @pl.when(turn < 2)
    def forward():
        mixer_forward_kernel(
            turn,
            info_ref,
            stream_ref,
            gain_ref,
            w_beta_ref,
            taps_ref.at[turn],
            out_gain_ref,
            *mixer_weights,
            middle_ref,
            strengths_ref,
            linear_ref.at[turn],
            out_ref.at[turn],
            fresh_ref.at[turn],
            solve_ref.at[turn],
            states_ref.at[turn],
            moves_ref.at[turn],
            normed_ref,
            w_qkv_ref,
            w_out_ref,
            sems,
        )

    @pl.when(turn == 0)
    def ahead():
        for item in tiles[:AHEAD]:
            start_each(item[3] + item[4])

    @pl.when(turn == 1)
    def feed():
        feed_forward_kernel(
            False,
            info_ref,
            middle_ref,
            feed_gain_ref,
            *feed_weights,
            result_ref,
            None,
            totals_ref,
            lows_ref,
            w_gate_up_ref,
            w_down_ref,
            kept_ref,
            feed_sems,
            None,
        )
        feed_backward_kernel(
            False,
            info_ref,
            middle_ref,
            grad_ref,
            feed_gain_ref,
            None,
            *feed_weights,
            branch_ref,
            feed_gain_grad_ref,
            feed_stack_ref,
            totals_ref,
            lows_ref,
            w_gate_up_ref,
            w_down_ref,
            kept_ref,
            made_ref,
            feed_sems,
            None,
            out_sems,
        )

    @pl.when(turn >= 2)
    def backward():
        half = turn - 2
        mixer_backward_kernel(
            half,
            False,
            info_ref,
            stream_ref,
            branch_ref,
            strengths_ref,
            linear_ref.at[half],
            out_ref.at[half],
            fresh_ref.at[half],
            solve_ref.at[half],
            states_ref.at[half],
            moves_ref.at[half],
            gain_ref,
            w_beta_ref,
            taps_ref.at[half],
            out_gain_ref,
            *mixer_weights,
            stream_grad_ref,
            gain_grad_ref,
            stacks_ref.at[half],
            strengths_grad_ref,
            taps_grad_ref.at[half],
            out_gain_grad_ref,
            totals_ref,
            strengths_sum_ref,
            branch_low_ref,
            again_ref,
            w_qkv_ref,
            w_out_ref,
            None,
        )

    for which in range(2):

        @pl.when(turn == 2 + which)
        def start_leaving():
            leave(which).start()

    @pl.when(turn == 3)
    def wait_leaving():
        leave(0).wait()
        leave(1).wait()


def second_layer(info, after, stream, grad, gains, w_beta, taps, out_gain, mixer_weights, feed_weights):
    length, width = stream.shape
    tile, units = mixer_weights[0].shape[2], feed_weights[1].shape[0]
    inner, spans, pairs, here = 2 * tile, length // SPAN, length // PAIR, tile // LANES
    taps_count = taps.shape[1]
    count = 2 * len(unit_tiles(units))
    out = jax.ShapeDtypeStruct
    taps = jnp.moveaxis(taps.reshape(3, taps_count, 2, tile), 2, 0)
    results = pl.pallas_call(
        only_second(second_layer_kernel),
        name="second_layer",
        grid_spec=pltpu.PrefetchScalarGridSpec(
            num_scalar_prefetch=1,
            grid=(4,),
            in_specs=[
                ANYWHERE,
                whole((length, width)),
                whole((length, width)),
                whole((1, width)),
                whole((1, width)),
                whole((width, LANES)),
                whole((2, 3, taps_count, tile)),
                whole((1, LANES)),
            ]
            + [ANYWHERE] * 12,
            out_specs=[
                whole((length, width)),
                whole((length, width)),
                whole((1, width)),
                whole((1, width)),
                whole((length, LANES)),
                whole((2, 3, taps_count, tile)),
                whole((1, LANES)),
                ANYWHERE,
                ANYWHERE,
            ],
            scratch_shapes=[
                pltpu.VMEM((length, width), WIDE),
                pltpu.VMEM((length, width), WIDE),
                pltpu.VMEM((length, LANES), WIDE),
                pltpu.VMEM((2, 3, length, tile), LOW),
                pltpu.VMEM((2, length, tile), LOW),
                pltpu.VMEM((2, length, tile), LOW),
                pltpu.VMEM((2, here, pairs, PAIR, PAIR), LOW),
                pltpu.VMEM((2, here, spans - 1, LANES, LANES), LOW),
                pltpu.VMEM((2, here, spans - 2, LANES, LANES), LOW),
                pltpu.VMEM((2, length, width), LOW),
                pltpu.VMEM((2, 3, width, tile), LOW),
                pltpu.VMEM((2, tile, width), LOW),
                pltpu.VMEM((2, length, width), WIDE),
                pltpu.VMEM((2, length, width), LOW),
                pltpu.VMEM((2, 2, width, units), LOW),
                pltpu.VMEM((2, units, width), LOW),
                pltpu.VMEM((2, length, 2 * units), LOW),
                pltpu.VMEM((2, length, 2 * units), LOW),
                pltpu.VMEM((length, LANES), WIDE),
                pltpu.VMEM((length, width), LOW),
                pltpu.VMEM((length, width), LOW),
                pltpu.VMEM((2, 6, length, tile), LOW),
                pltpu.SemaphoreType.DMA((6,)),
                pltpu.SemaphoreType.DMA((3 * count,)),
                pltpu.SemaphoreType.DMA((2 * count + 1,)),
                pltpu.SemaphoreType.DMA((2,)),
            ],
        ),
        out_shape=[
            out((length, width), LOW),
            out((length, width), LOW),
            out((1, width), WIDE),
            out((1, width), WIDE),
            out((length, LANES), LOW),
            out((2, 3, taps_count, tile), WIDE),
            out((1, LANES), WIDE),
            out((4, length, 2 * units), LOW),
            out((6, length, inner), LOW),
        ],
        compiler_params=pltpu.CompilerParams(dimension_semantics=("arbitrary",), vmem_limit_bytes=60 * 2**20),
        cost_estimate=cost(50),
    )(info, after, stream, grad, gains[0:1], gains[1:2], w_beta, taps, out_gain, *mixer_weights, *feed_weights)
    result, stream_grad, feed_gain, gain, strengths, taps_grad, out_gain_grad, feed_stack, stack = results
    taps_grad = jnp.moveaxis(taps_grad, 0, 2).reshape(3, taps_count, inner)
    return result, (None, feed_gain, feed_stack), (stream_grad, gain, stack, strengths, taps_grad, out_gain_grad)


def rows_kernel(halves, width, count, info_ref, *refs):
    lefts, rights = refs[:count], refs[count : 2 * count]
    keep_ref, send_ref, turned_ref, rows_ref = refs[2 * count :]
    size = width // halves // 8

    @pl.when((pl.program_id(0) == 0) & (pl.program_id(1) == 0))
    def first():
        for item in range(count):
            turned_ref[item] = lefts[item][:, :width].T
            place = 0
            for which in range(halves):
                for index in (0, 2, 1, 3):
                    start = which * (width // halves) + info_ref[index] * size
                    source = pl.ds(pl.multiple_of(start, size), size)
                    rows_ref[item, place : place + size, :] = turned_ref[item, source, :]
                    place += size

    tile = keep_ref.shape[1]
    if rights[0].shape[1] == tile:
        pieces = [right[...] for right in rights]
    else:
        columns = pl.ds(pl.multiple_of(pl.program_id(1) * tile, tile), tile)
        pieces = [right[:, columns] for right in rights]
    total = mm(rows_ref[0], pieces[0])
    for item in range(1, count):
        total = total + mm(rows_ref[item], pieces[item])
    half = keep_ref.shape[0]
    keep_ref[...] = low(total[:half])
    send_ref[...] = low(total[half:])


def rows_grads(info, after, items, left, right, groups, halves, tile, tiles):
    length = items[0].shape[1]
    count = len(items)
    rows = left[3] // 2
    spread = 1 if right[1] == tile else 0
    half = pl.BlockSpec((None, rows // 2, tile), lambda g, t, info: (g, 0, t))
    shape = jax.ShapeDtypeStruct((groups, rows // 2, tile * tiles), LOW)
    return pl.pallas_call(
        lambda info_ref, *refs: rows_kernel(halves, left[3], count, info_ref, *refs[len(after) :]),
        name="rows_grads",
        grid_spec=pltpu.PrefetchScalarGridSpec(
            num_scalar_prefetch=1,
            grid=(groups, tiles),
            in_specs=[ANYWHERE] * len(after)
            + [pl.BlockSpec((None, length, left[1]), lambda g, t, info: (left[0], 0, left[2]))] * count
            + [pl.BlockSpec((None, length, right[1]), lambda g, t, info: (right[0] + g, 0, right[2] + spread * t))]
            * count,
            out_specs=[half, half],
            scratch_shapes=[pltpu.VMEM((count, left[3], length), LOW), pltpu.VMEM((count, rows, length), LOW)],
        ),
        out_shape=[shape, shape],
        compiler_params=pltpu.CompilerParams(
            dimension_semantics=("arbitrary", "arbitrary"), vmem_limit_bytes=40 * 2**20
        ),
        cost_estimate=cost(10),
    )(info, *after, *items, *items)


def halve(after, keep, came, axis):
    def kernel(after_ref, keep_ref, came_ref, *outs):
        total = keep_ref[...].astype(WIDE) + came_ref[...].astype(WIDE)
        if axis is None:
            outs[0][...] = total
        else:
            size = total.shape[axis - 1] // 2
            for i in range(2):
                at = slice(i * size, (i + 1) * size)
                outs[i][...] = low(total[at] if axis == 1 else total[:, at])

    groups, rows, columns = keep.shape
    shape = {None: (rows, columns), 1: (rows // 2, columns), 2: (rows, columns // 2)}[axis]
    count, dtype = (1, WIDE) if axis is None else (2, LOW)
    block = pl.BlockSpec((None, rows, columns), lambda g: (g, 0, 0))
    return pl.pallas_call(
        kernel,
        name="halve",
        grid=(groups,),
        in_specs=[ANYWHERE, block, block],
        out_specs=[pl.BlockSpec((None, *shape), lambda g: (g, 0, 0))] * count,
        out_shape=[jax.ShapeDtypeStruct((groups, *shape), dtype)] * count,
        compiler_params=params(16 * 2**20),
        cost_estimate=cost(2),
    )(after, keep, came)


def tied(*values):
    return lax.optimization_barrier(values)


def exchange(value, axis, apart):
    return lax.ppermute(value, axis, [(i, i ^ apart(i)) for i in range(lax.axis_size(axis))])


def unpack(packed, like):
    found, start = [], 0
    for item in like:
        found.append(packed[start : start + item.size].reshape(item.shape))
        start += item.size
    return found


def pack(items):
    return jnp.concatenate([item.reshape(-1) for item in items])


def local(
    inputs, cotangent, w_qkv, w_beta, conv_taps, w_out, w_gate_up, w_down, norm_gains, out_gains
):
    batches, unused, length, width = inputs.shape
    place = lax.axis_index("section")
    rank, half = place // 2, place % 2
    me, copies = lax.axis_index("dp"), lax.axis_size("dp")
    per = batches // 2
    cube = copies == 8

    def across(value, bits=1):
        return exchange(value, "section", lambda i: bits)

    def flip(value, even, odd):
        return exchange(value, "dp", lambda i: odd if i % 2 else even)

    def by_half(own, other, axis):
        return jnp.where(
            half == 0, jnp.concatenate([own, other], axis), jnp.concatenate([other, own], axis)
        )

    first_apart = 2 + 2 * (me % 2)

    def mine_of(value, axis):
        size = value.shape[axis] // copies
        return lax.dynamic_slice_in_dim(value, me * size, size, axis)

    def collect(came, axis):
        came = jnp.concatenate([came, flip(came, 2, 4)], axis)
        came = jnp.concatenate([came, flip(came, 4, 2)], axis)
        return came, flip(came, 1, 1)

    smalls = [conv_taps, w_beta.astype(WIDE), norm_gains, out_gains]
    others = unpack(across(pack(smalls)), smalls)
    taps = jnp.concatenate([conv_taps, others[0]], 2)
    heads = w_beta.shape[1]
    w_beta = jnp.concatenate([w_beta, low(others[1])], 1)
    w_beta = jnp.pad(w_beta, ((0, 0), (0, LANES - 2 * heads)))
    gains = by_half(norm_gains, others[2], 1)
    out_gain = by_half(out_gains, others[3], 0)[None]
    inner, units = w_out.shape[0], w_down.shape[0]
    tile = w_qkv.shape[2]

    if cube:
        block = width // copies
        core = me % 2
        corner = 2 * ((me // 2 + me // 4) % 2) + core
        quarter, rows = width // 4, inner // 2
        came = across(mine_of(w_qkv, 1))
        came, lift = tied(came, mine_of(w_gate_up, 1))
        lift = across(lift)
        lift, out = tied(lift, lax.dynamic_slice_in_dim(w_out, core * rows, rows, 0))
        out = across(out)
        out, down = tied(out, lax.dynamic_slice_in_dim(w_down, corner * quarter, quarter, 1))
        down = across(down)
        mixer_weights = (w_qkv, w_out, *collect(came, 1), out, flip(out, 1, 1))
        near = flip(lift, 2, 4)
        lift = jnp.concatenate([lift, near], 1)
        far = flip(lift, 4, 2)
        apart = [0, first_apart, 6 - first_apart, 6, 1, 7 - first_apart, 1 + first_apart, 7]
        places = [me ^ bits for bits in apart]
        down_places = [2 * (corner ^ bits) + i for bits in (0, 2, 1, 3) for i in range(2)]
    else:

        def gathered(value):
            return lax.all_gather(across(mine_of(value, 1)), "dp", axis=1, tiled=True)

        def halves_of(value):
            return jnp.split(gathered(value), 2, 1)

        out = lax.all_gather(across(mine_of(w_out, 0)), "dp", axis=0, tiled=True)
        mixer_weights = (w_qkv, w_out, *halves_of(w_qkv), *jnp.split(out, 2, 0))
        feed_weights = (w_gate_up, w_down, *halves_of(w_gate_up), *halves_of(w_down))
        places = down_places = list(range(8))
        core, near = 0, taps
    info = jnp.stack([jnp.asarray(item, jnp.int32) for item in places + [rank == 0] + down_places + [core, 1 - core, rank == 1]])

    def mixer_part(after, stream, *wrap):
        return mixer_forward(info, after, stream, gains[0:1], mixer_weights, w_beta, taps, out_gain, *wrap)

    def feed_back(after, grad, saved, old):
        stream, middle, kept, lifted = saved
        return feed_backward(info, after, middle, grad, lifted, gains[1:2], feed_weights, old)

    def mixer_back(after, middle_grad, saved, old):
        stream, middle, kept, lifted = saved
        return mixer_backward(
            info, after, stream, middle_grad, kept, gains[0:1], mixer_weights, w_beta, taps, out_gain, old
        )

    def own(value):
        items = lax.dynamic_slice_in_dim(value, half * per, per, 0)
        return [items[i, 0] for i in range(per)]

    up = [(0, 2), (1, 3)]
    streams = own(inputs)
    saved0 = []
    for stream in streams:
        near, *kept = mixer_part(near, stream)
        saved0.append([stream, near, kept])
    if cube:
        far, down, saved0[0][1] = tied(far, down, saved0[0][1])
        lift = jnp.concatenate([lift, far], 1)
        lift_twin = flip(lift, 1, 1)
        down = jnp.concatenate([down, flip(down, 2, 4)], 1)
        down, saved0[-1][1] = tied(down, saved0[-1][1])
        feed_weights = (w_gate_up, w_down, lift, lift_twin, down, flip(down, 1, 1))
    firsts = []
    for saved in saved0:
        result, lifted = feed_forward(info, saved[1], gains[1:2], feed_weights)
        saved.append(lifted)
        firsts.append(result)
    grads = own(cotangent)
    streams = [lax.ppermute(firsts[0], "section", up)]
    after = taps
    if per > 1:
        through, streams[0], firsts[1] = tied(info.astype(WIDE), streams[0], firsts[1])
        after = lax.ppermute(through, "section", [(0, 1), (1, 0)])
        for index in range(1, per):
            firsts[index], after = tied(firsts[index], after)
            streams.append(lax.ppermute(firsts[index], "section", up))
    results, returned, feeds, mixes = [], [], [], []
    for index in range(per):
        result, feed, mix = second_layer(
            info, after, streams[index], grads[index], gains, w_beta, taps, out_gain, mixer_weights, feed_weights
        )
        results.append(result)
        feeds.append(feed)
        mixes.append(mix)
        after = mix[0]
        returned.append(lax.ppermute(after, "section", [(2, 0), (3, 1)]))
    feed_twins, mix_twins = [], []
    waited = [mixes[-1][0]]
    for index, (grad, saved) in enumerate(zip(returned, saved0)):
        feeds[index] = feed_back(waited, grad, saved, feeds[index])
        after = (taps, taps, taps)
        if cube:
            feed_twins.append(flip(feeds[index][2], 1, 1))
            if index:
                after = (feed_twins[index - 1], mix_twins[index - 1], taps)
        mixes[index] = mixer_back(after, feeds[index][0], saved, mixes[index])
        waited = [mixes[index][0]]
        if cube:
            mix_twins.append(flip(mixes[index][2], 1, 1))
    feed_all = [feed[2] for feed in feeds] + feed_twins
    held = jnp.stack([jnp.where(rank == 1, result, mix[0]) for result, mix in zip(results, mixes)])
    column = width // 2
    moved = across(lax.dynamic_slice_in_dim(held, (1 - rank) * column, column, 2), 2)
    held = lax.dynamic_slice_in_dim(held, rank * column, column, 2)
    mix_all = [mix[2] for mix in mixes]
    if cube:
        mix_all = mix_all + mix_twins
        plans = (
            (feed_all, (3, units, 0, width), (0, units, 0), 2, 1, units, 2),
            (feed_all, (2, 2 * units, 0, 2 * units), (3, units, 1), 1, 2, width // 2, 2),
            (mix_all, (5, width, 0, width), (0, width, 0), 3, 1, width, 1),
            (mix_all, (3, width, 0, width), (4, width, 0), 1, 2, width, 1),
        )
        after, kept, came = [mixes[-1][1]], [], []
        for index, plan in enumerate(plans):
            keep, send = rows_grads(info, after, *plan)
            after = [keep]
            kept.append(keep)
            came.append(across(send) if index % 2 else flip(send, 2, 4))
        after = kept[-1]
        lifts, downs, qkvs, outs = range(4)

        def turn(which, axis, onward=None):
            nonlocal after
            parts = halve(after, kept[which], came[which], axis)
            after = kept[which] = parts[0]
            if axis is not None:
                came[which] = onward(parts[1])

        def far(value):
            return flip(value, 4, 2)

        def near_flip(value):
            return flip(value, 2, 4)

        marks = [kept[downs]]
        turn(lifts, 1, far)
        turn(downs, 1, near_flip)
        marks.append(after)
        turn(outs, 1, near_flip)
        turn(qkvs, 1, far)
        marks.append(after)
        turn(lifts, 2, across)
        marks.append(after)
        turn(downs, 1, far)
        turn(outs, 1, far)
        marks.append(after)
        turn(qkvs, 2, across)
        marks.append(after)
        turn(lifts, None)
        marks.append(after)
        turn(downs, None)
        turn(outs, None)
        turn(qkvs, None)
        grad_gate_up, grad_down, grad_qkv, grad_out = kept[0], kept[1][0], kept[2], kept[3][0]
    else:

        def tall(items, index):
            return jnp.concatenate([item[index] for item in items], 0)

        def total(value, axis, split):
            value = lax.psum_scatter(low(value), "dp", scatter_dimension=axis, tiled=True)
            size = value.shape[split] // 2
            mine = lax.slice_in_dim(value, 0, size, axis=split)
            theirs = lax.slice_in_dim(value, size, 2 * size, axis=split)
            return mine.astype(WIDE) + across(theirs).astype(WIDE)

        ends = tall(feed_all, 3)
        normed2, grad, normed = ends[:, :width], ends[:, units : units + width], tall(mix_all, 5)
        grad_gate_up = total(jnp.stack([mm_tn(normed2, tall(feed_all, i)) for i in range(2)]), 1, 2)
        grad_qkv = total(jnp.stack([mm_tn(normed, tall(mix_all, i)) for i in range(3)]), 1, 2)
        down = mm_tn(tall(feed_all, 2), grad).reshape(2, units, width)
        out = mm_tn(tall(mix_all, 3), tall(mix_all, 4)).reshape(2, inner, width)
        grad_down, grad_out = total(down, 1, 0)[0], total(out, 1, 0)[0]

    strengths = [mix[3] for mix in mixes]
    if cube:
        strengths[0] = tied(strengths[0], marks[3])[0]
        moved = tied(moved, marks[1])[0]
    d_beta = sum(mm_tn(mix[5], item) for mix, item in zip(mix_all, strengths))[:, : 2 * heads]
    d_taps = sum(mix[4] for mix in mixes)
    d_gains = jnp.concatenate([sum(mix[1] for mix in mixes), sum(feed[1] for feed in feeds)], 0)
    d_out_gain = sum(mix[5] for mix in mixes)

    flat = [d_taps, d_beta, d_gains, d_out_gain]
    packed = pack(flat)
    if cube:
        for bits, mark in zip((1, 2, 4), marks[4:]):
            packed = packed + tied(flip(packed, bits, bits), mark)[0]
    else:
        packed = lax.psum(packed, "dp")
    d_taps, d_beta, d_gains, d_out_gain = unpack(packed, flat)

    def part(value, axis, size):
        return lax.dynamic_slice_in_dim(value, me * size, size, axis)

    def halves(value, axis):
        size = value.shape[axis] // 2
        return [
            lax.dynamic_slice_in_dim(value, which * size, size, axis) for which in (half, 1 - half)
        ]

    pieces = [
        [part(d_taps[:, :, i * inner : (i + 1) * inner], 2, inner // copies) for i in range(2)],
        [part(d_beta[:, i * heads : (i + 1) * heads], 0, width // copies) for i in range(2)],
        [part(item, 1, width // 2 // copies) for item in halves(d_gains, 1)],
        [part(item, 1, LANES // 2 // copies) for item in halves(d_out_gain, 1)],
    ]
    mine = [item[0] for item in pieces]
    came = unpack(across(pack([item[1] for item in pieces])), mine)
    grad_taps, grad_beta, grad_gains, grad_out_gains = [a + b for a, b in zip(mine, came)]

    kinds = jnp.stack([jnp.where(rank == 1, held, moved), jnp.where(rank == 1, moved, held)])
    mine, theirs = [
        lax.dynamic_slice_in_dim(kinds, which * column // 2, column // 2, 3) for which in (half, 1 - half)
    ]
    final_stream, final_grad = by_half(mine, across(theirs), 1)[:, :, None]
    return (
        final_stream,
        final_grad,
        grad_qkv,
        grad_beta,
        grad_taps,
        grad_out,
        grad_gate_up,
        grad_down,
        grad_gains,
        grad_out_gains[0],
    )


def solution(mesh):
    in_specs = (
        P(None, "dp", None, None),
        P(None, "dp", None, None),
        P(None, None, "section"),
        P(None, "section"),
        P(None, None, "section"),
        P("section", None),
        P(None, None, "section"),
        P("section", None),
        P(None, "section"),
        P("section"),
    )
    out_specs = (
        P(None, "dp", None, "section"),
        P(None, "dp", None, "section"),
        P(None, "dp", "section"),
        P("dp", "section"),
        P(None, None, ("section", "dp")),
        P(("section", "dp"), None),
        P(None, "dp", "section"),
        P(("section", "dp"), None),
        P(None, ("section", "dp")),
        P(("section", "dp")),
    )
    return jax.shard_map(local, mesh=mesh, in_specs=in_specs, out_specs=out_specs, check_vma=False)
```

```python
import jax
import jax.numpy as jnp
from jax import lax
from jax.experimental import pallas as pl
from jax.experimental.pallas import tpu as pltpu
from jax.sharding import PartitionSpec as P

SPAN = 64
PAIR = 2 * SPAN
LANES = 128
LOW = jnp.bfloat16
WIDE = jnp.float32
VMEM = 56 * 1024 * 1024


def mm(left, right):
    return lax.dot_general(left, right, (((1,), (0,)), ((), ())), preferred_element_type=WIDE)


def mm_nt(left, right):
    return lax.dot_general(left, right, (((1,), (1,)), ((), ())), preferred_element_type=WIDE)


def mm_tn(left, right):
    return lax.dot_general(left, right, (((0,), (0,)), ((), ())), preferred_element_type=WIDE)


def low(value):
    return value.astype(LOW)


def sigmoid(value):
    return 0.5 * jnp.tanh(0.5 * value) + 0.5


def shift_down(value, steps):
    rows = lax.broadcasted_iota(jnp.int32, value.shape, 0)
    return jnp.where(rows >= steps, pltpu.roll(value, steps, 0), 0.0)


def shift_up(value, steps):
    size = value.shape[0]
    rows = lax.broadcasted_iota(jnp.int32, value.shape, 0)
    return jnp.where(rows < size - steps, pltpu.roll(value, size - steps, 0), 0.0)


def pick_lane(value, lane):
    lanes = lax.broadcasted_iota(jnp.int32, value.shape, 1)
    return jnp.sum(jnp.where(lanes == lane, value, 0.0), axis=1, keepdims=True)


def norm_scale(value, epsilon):
    return lax.rsqrt(jnp.mean(value * value, axis=-1, keepdims=True) + epsilon)


def norm_back(value, gain, grad, epsilon):
    scale = norm_scale(value, epsilon)
    scaled = gain * grad
    inner = jnp.mean(value * scaled, axis=-1, keepdims=True)
    value_grad = scale * (scaled - value * (scale * scale * inner))
    gain_grad = jnp.sum(grad * value * scale, axis=0, keepdims=True)
    return value_grad, gain_grad


def pair_masks():
    rows = lax.broadcasted_iota(jnp.int32, (PAIR, PAIR), 0)
    cols = lax.broadcasted_iota(jnp.int32, (PAIR, PAIR), 1)
    apart = rows ^ cols
    near = apart < SPAN
    return rows, cols, apart, near


def inverse(systems, apart):
    one = (apart == 0).astype(WIDE)
    found = [one - jnp.where(apart == 1, system, 0.0) for system in systems]
    lows = [low(system) for system in systems]
    size = 2
    while size < SPAN:
        level = (apart >= size) & (apart < 2 * size)
        parts = [jnp.where(level, system, jnp.zeros_like(system)) for system in lows]
        heads = [low(item) for item in found]
        steps = [low(mm(head, part)) for head, part in zip(heads, parts)]
        found = [item - mm(step, head) for item, step, head in zip(found, steps, heads)]
        size *= 2
    return found


def conv_silu(linear, taps):
    count = taps.shape[0]
    total = linear * taps[count - 1 : count]
    for back in range(1, count):
        total = total + shift_down(linear, back) * taps[count - 1 - back : count - back]
    return total


def whole(shape):
    return pl.BlockSpec(shape, lambda step, *scalars: (0,) * len(shape))


def tiled(shape, axis):
    return pl.BlockSpec(
        shape, lambda step, *scalars: tuple(step if i == axis else 0 for i in range(len(shape)))
    )


def tiled_old(shape, axis):
    return pl.BlockSpec(
        shape,
        lambda step, info: tuple(step * (1 - info[FIRST]) if i == axis else 0 for i in range(len(shape))),
    )


ANYWHERE = pl.BlockSpec(memory_space=pl.ANY)

FIRST, DOWN, OUT, SECOND = 8, 9, 17, 19


def mixer_copies(info_ref, refs, into_qkv, into_out, sems):
    qkv_ref, out_ref, qkv_came, qkv_twin, out_came, out_twin = refs
    rows = qkv_came.shape[1]
    first, second = pl.ds(0, rows), pl.ds(rows, rows)
    pairs = [
        (qkv_ref, into_qkv.at[0]),
        (out_ref, into_out.at[0]),
        (qkv_came, into_qkv.at[1, :, first]),
        (qkv_twin, into_qkv.at[1, :, second]),
    ]
    rows = out_came.shape[0]
    for index, source in enumerate((out_came, out_twin)):
        place = pl.multiple_of(info_ref[OUT + index] * rows, rows)
        pairs.append((source, into_out.at[1, pl.ds(place, rows)]))
    copies = [pltpu.make_async_copy(*pair, sems.at[i]) for i, pair in enumerate(pairs)]
    return copies[0], copies[1], copies[2:4], copies[4:]


def apart_order(info_ref, value_ref, into_ref, first=0):
    size = value_ref.shape[1] // 8
    for index in range(8):
        place = pl.multiple_of(info_ref[first + index] * size, size)
        into_ref[:, index * size : (index + 1) * size] = value_ref[:, pl.ds(place, size)]


def add_from_apart(info_ref, value_ref, into_ref, first=0):
    size = value_ref.shape[1] // 8
    for index in range(8):
        place = pl.ds(pl.multiple_of(info_ref[first + index] * size, size), size)
        into_ref[:, place] += value_ref[:, index * size : (index + 1) * size]


def start_all(step, copies):
    @pl.when(step == 0)
    def begin():
        for copy in copies:
            copy.start()


def wait_all(step, at, copies):
    @pl.when(step == at)
    def wait():
        for copy in copies:
            copy.wait()


def or_keep(kernel, inputs, outputs, first_kept, in_place=0):
    def either(*refs):
        start = 1 + inputs
        old = refs[start : start + outputs - first_kept]
        rest = refs[start + len(old) :]

        @pl.when(refs[0][FIRST] == 1)
        def compute():
            kernel(*refs[:start], *rest)

        @pl.when(refs[0][FIRST] == 0)
        def keep():
            for source, target in zip(old[: len(old) - in_place], rest[first_kept:outputs]):
                target[...] = source[...]

    return either


def only_second(kernel):
    def either(info_ref, *refs):
        @pl.when(info_ref[SECOND] == 1)
        def compute():
            kernel(info_ref, *refs)

    return either


def mixer_forward_kernel(
    step,
    info_ref,
    stream_ref,
    gain_ref,
    w_beta_ref,
    taps_ref,
    out_gain_ref,
    qkv_own_ref,
    out_own_ref,
    qkv_came_ref,
    qkv_twin_ref,
    out_came_ref,
    out_twin_ref,
    middle_ref,
    strengths_ref,
    linear_ref,
    out_ref,
    fresh_ref,
    solve_ref,
    states_ref,
    moves_ref,
    normed_ref,
    w_qkv_ref,
    w_out_ref,
    sems,
):
    length = stream_ref.shape[0]
    spans = length // SPAN
    heads = linear_ref.shape[2] // LANES
    refs = (qkv_own_ref, out_own_ref, qkv_came_ref, qkv_twin_ref, out_came_ref, out_twin_ref)
    own_qkv, own_out, qkv, out = mixer_copies(info_ref, refs, w_qkv_ref, w_out_ref, sems)
    start_all(step, [own_qkv, own_out])

    @pl.when(step == 0)
    def first():
        stream = stream_ref[...].astype(WIDE)
        normed_ref[0] = low(stream * norm_scale(stream, 1e-6) * gain_ref[...])
        apart_order(info_ref, normed_ref.at[0], normed_ref.at[1])
        strengths_ref[...] = mm(normed_ref[0], w_beta_ref[...])
        middle_ref[...] = stream

    normed = normed_ref[step]
    wait_all(step, 0, [own_qkv, own_out])
    wait_all(step, 1, qkv + out)
    start_all(step, qkv + out)
    active = []
    for which in range(3):
        linear = mm(normed, w_qkv_ref[step, which])
        linear_ref[which] = low(linear)
        total = conv_silu(linear, taps_ref[which])
        active.append(total * sigmoid(total))
    rows, cols, apart, near = pair_masks()
    strict = (rows > cols) & near
    lower = (rows >= cols) & near
    queries, keys, values, betas = [], [], [], []
    for head in range(heads):
        lanes = slice(head * LANES, (head + 1) * LANES)
        query, key = active[0][:, lanes], active[1][:, lanes]
        queries.append(low(query * lax.rsqrt(jnp.sum(query * query, axis=1, keepdims=True) + 1e-6)))
        keys.append(low(key * lax.rsqrt(jnp.sum(key * key, axis=1, keepdims=True) + 1e-6)))
        values.append(low(active[2][:, lanes]))
        betas.append(sigmoid(pick_lane(strengths_ref[...], step * heads + head)))
    cells = [(head, pair) for head in range(heads) for pair in range(length // PAIR)]

    def part(array, pair):
        return array[pair * PAIR : (pair + 1) * PAIR]

    systems = []
    for head, pair in cells:
        key = part(keys[head], pair)
        systems.append(jnp.where(strict, mm_nt(key, key) * part(betas[head], pair), 0.0))
    solved = [low(item) for item in inverse(systems, apart)]
    both = {}
    scores = {}
    for (head, pair), solve in zip(cells, solved):
        solve_ref[head, pair] = solve
        beta = part(betas[head], pair)
        key = part(keys[head], pair)
        right = jnp.concatenate(
            [low(beta * key.astype(WIDE)), low(beta * part(values[head], pair).astype(WIDE))], axis=1
        )
        both[head, pair] = mm(solve, right)
        scores[head, pair] = low(jnp.where(lower, mm_nt(part(queries[head], pair), key), 0.0))

    def span_of(array, span):
        return array[span * SPAN : (span + 1) * SPAN]

    def both_of(head, span):
        return span_of(both[head, span // 2], span % 2)

    states = [[None] * spans for head in range(heads)]
    turns = {}
    for head in range(heads):
        for span in range(spans - 1):
            turns[head, span] = mm_tn(span_of(keys[head], span), low(both_of(head, span)))
    for span in range(1, spans):
        for head in range(heads):
            turn = turns[head, span - 1]
            if span == 1:
                states[head][span] = turn[:, LANES:]
            else:
                before = states[head][span - 1]
                move = low(turn[:, :LANES])
                moves_ref[head, span - 2] = move
                states[head][span] = before + turn[:, LANES:] - mm(move, low(before))
    fresh = {}
    carried = {}
    for head in range(heads):
        for span in range(spans):
            item = both_of(head, span)
            if span == 0:
                fresh[head, span] = low(item[:, LANES:])
                carried[head, span] = jnp.zeros((SPAN, LANES), WIDE)
            else:
                state = low(states[head][span])
                states_ref[head, span - 1] = state
                left = jnp.concatenate([low(item[:, :LANES]), span_of(queries[head], span)], axis=0)
                seen = mm(left, state)
                fresh[head, span] = low(item[:, LANES:] - seen[:SPAN])
                carried[head, span] = seen[SPAN:]
    normed_out = []
    for head in range(heads):
        lanes = slice(head * LANES, (head + 1) * LANES)
        pieces = []
        for pair in range(length // PAIR):
            piece = jnp.concatenate([fresh[head, 2 * pair], fresh[head, 2 * pair + 1]], axis=0)
            fresh_ref[pair * PAIR : (pair + 1) * PAIR, lanes] = piece
            base = jnp.concatenate([carried[head, 2 * pair], carried[head, 2 * pair + 1]], axis=0)
            pieces.append(base + mm(scores[head, pair], piece))
        output = jnp.concatenate(pieces, axis=0)
        out_ref[:, lanes] = low(output)
        normed_out.append(low(output * norm_scale(output, 1e-5) * out_gain_ref[...]))
    middle_ref[...] += mm(jnp.concatenate(normed_out, axis=1), w_out_ref[step])


def cost(micros):
    return pl.CostEstimate(flops=int(micros * 1.1e9), bytes_accessed=2**20, transcendentals=0)


def params(limit=VMEM, **extra):
    return pltpu.CompilerParams(dimension_semantics=("arbitrary",), vmem_limit_bytes=limit, **extra)


def mixer_forward(info, after, stream, gain, weights, w_beta, taps, out_gain, wrap=lambda kernel: kernel):
    length, width = stream.shape
    tile = weights[0].shape[2]
    inner = 2 * tile
    heads = inner // LANES
    spans = length // SPAN
    pairs = length // PAIR
    here = tile // LANES
    out = jax.ShapeDtypeStruct
    return pl.pallas_call(
        wrap(lambda info_ref, after_ref, *refs: mixer_forward_kernel(pl.program_id(0), info_ref, *refs)),
        name="mixer_forward",
        grid_spec=pltpu.PrefetchScalarGridSpec(
            num_scalar_prefetch=1,
            grid=(2,),
            in_specs=[
                ANYWHERE,
                whole((length, width)),
                whole((1, width)),
                whole((width, LANES)),
                tiled((3, taps.shape[1], tile), 2),
                whole((1, LANES)),
            ]
            + [ANYWHERE] * 6,
            out_specs=[
                whole((length, width)),
                whole((length, LANES)),
                tiled((3, length, tile), 2),
                tiled((length, tile), 1),
                tiled((length, tile), 1),
                tiled((here, pairs, PAIR, PAIR), 0),
                tiled((here, spans - 1, LANES, LANES), 0),
                tiled((here, spans - 2, LANES, LANES), 0),
            ],
            scratch_shapes=[
                pltpu.VMEM((2, length, width), LOW),
                pltpu.VMEM((2, 3, width, tile), LOW),
                pltpu.VMEM((2, tile, width), LOW),
                pltpu.SemaphoreType.DMA((6,)),
            ],
        ),
        out_shape=[
            out((length, width), WIDE),
            out((length, LANES), WIDE),
            out((3, length, inner), LOW),
            out((length, inner), LOW),
            out((length, inner), LOW),
            out((heads, pairs, PAIR, PAIR), LOW),
            out((heads, spans - 1, LANES, LANES), LOW),
            out((heads, spans - 2, LANES, LANES), LOW),
        ],
        compiler_params=params(),
        cost_estimate=cost(14),
    )(info, after, stream, gain, w_beta, taps, out_gain, *weights)


def mixer_backward_kernel(
    step,
    load,
    info_ref,
    stream_ref,
    branch_ref,
    strengths_ref,
    linear_ref,
    out_ref,
    fresh_ref,
    solve_ref,
    states_ref,
    moves_ref,
    gain_ref,
    w_beta_ref,
    taps_ref,
    out_gain_ref,
    qkv_own_ref,
    out_own_ref,
    qkv_came_ref,
    qkv_twin_ref,
    out_came_ref,
    out_twin_ref,
    stream_grad_ref,
    gain_grad_ref,
    stack_ref,
    strengths_grad_ref,
    taps_grad_ref,
    out_gain_grad_ref,
    normed_grad_ref,
    strengths_sum_ref,
    branch_low_ref,
    normed_ref,
    w_qkv_ref,
    w_out_ref,
    sems,
):
    length = stream_ref.shape[0]
    spans = length // SPAN
    pairs = length // PAIR
    tile = stack_ref.shape[2]
    heads = tile // LANES
    if load:
        refs = (qkv_own_ref, out_own_ref, qkv_came_ref, qkv_twin_ref, out_came_ref, out_twin_ref)
        own_qkv, own_out, qkv, out = mixer_copies(info_ref, refs, w_qkv_ref, w_out_ref, sems)
        start_all(step, [own_out, own_qkv])

    @pl.when(step == 0)
    def first():
        branch_low_ref[...] = low(branch_ref[...])
        stream = stream_ref[...].astype(WIDE)
        normed_ref[...] = low(stream * norm_scale(stream, 1e-6) * gain_ref[...])
        out_gain_grad_ref[...] = jnp.zeros_like(out_gain_grad_ref)
        strengths_sum_ref[...] = jnp.zeros_like(strengths_sum_ref)
        normed_grad_ref[...] = jnp.zeros_like(normed_grad_ref)

    columns = pl.ds(pl.multiple_of(step * tile, tile), tile)
    stack_ref[4] = branch_low_ref[:, columns]
    stack_ref[5] = normed_ref[:, columns]
    rows, cols, apart, near = pair_masks()
    strict = (rows > cols) & near
    lower = (rows >= cols) & near
    upper_strict = (rows < cols) & near
    upper = (rows <= cols) & near
    cells = [(head, pair) for head in range(heads) for pair in range(pairs)]

    def part(array, pair):
        return array[pair * PAIR : (pair + 1) * PAIR]

    def span_of(array, span):
        return array[span * SPAN : (span + 1) * SPAN]

    if load:
        wait_all(step, 0, [own_out, own_qkv])
        wait_all(step, 1, out + qkv)
        start_all(step, out + qkv)
    normed_out_grad = mm_nt(branch_low_ref[...], w_out_ref[step])
    totals, gates, active = [], [], []
    for which in range(3):
        total = conv_silu(linear_ref[which].astype(WIDE), taps_ref[which])
        gate = sigmoid(total)
        totals.append(total)
        gates.append(gate)
        active.append(total * gate)
    query_scales, key_scales = [], []
    queries, keys, values, betas, output_grads = [], [], [], [], []
    for head in range(heads):
        lanes = slice(head * LANES, (head + 1) * LANES)
        query, key = active[0][:, lanes], active[1][:, lanes]
        query_scales.append(lax.rsqrt(jnp.sum(query * query, axis=1, keepdims=True) + 1e-6))
        key_scales.append(lax.rsqrt(jnp.sum(key * key, axis=1, keepdims=True) + 1e-6))
        queries.append(low(query * query_scales[head]))
        keys.append(low(key * key_scales[head]))
        values.append(low(active[2][:, lanes]))
        betas.append(sigmoid(pick_lane(strengths_ref[...], step * heads + head)))
        output = out_ref[:, lanes].astype(WIDE)
        scale = norm_scale(output, 1e-5)
        grad = normed_out_grad[:, lanes]
        stack_ref[3, :, lanes] = low(output * scale * out_gain_ref[...])
        scaled = out_gain_ref[...] * grad
        inner = jnp.mean(output * scaled, axis=1, keepdims=True)
        output_grads.append(low(scale * (scaled - output * (scale * scale * inner))))
        out_gain_grad_ref[...] += jnp.sum(grad * output * scale, axis=0, keepdims=True)
    fresh = [fresh_ref[:, head * LANES : (head + 1) * LANES] for head in range(heads)]

    scores_back, score_grads, score_grads_back = {}, {}, {}
    for head, pair in cells:
        query, key = part(queries[head], pair), part(keys[head], pair)
        grad, new = part(output_grads[head], pair), part(fresh[head], pair)
        scores_back[head, pair] = low(jnp.where(upper, mm_nt(key, query), 0.0))
        score_grads[head, pair] = low(jnp.where(lower, mm_nt(grad, new), 0.0))
        score_grads_back[head, pair] = low(jnp.where(upper, mm_nt(new, grad), 0.0))
    inside, early = {}, {}
    for head, pair in cells:
        inside[head, pair] = mm(scores_back[head, pair], part(output_grads[head], pair))
    for head, pair in cells:
        early[head, pair] = mm_tn(solve_ref[head, pair], low(inside[head, pair]))
    returns = {}
    for head in range(heads):
        for span in range(1, spans):
            beta = span_of(betas[head], span)
            back = low(-beta * span_of(early[head, span // 2], span % 2))
            left = jnp.concatenate([span_of(queries[head], span), span_of(keys[head], span)], axis=0)
            right = jnp.concatenate([span_of(output_grads[head], span), back], axis=0)
            returns[head, span] = mm_tn(left, right)
    state_grads = {}
    for span in range(spans - 2, -1, -1):
        for head in range(heads):
            if span == spans - 2:
                state_grads[head, span] = returns[head, span + 1]
            else:
                after = state_grads[head, span + 1]
                state_grads[head, span] = (
                    after + returns[head, span + 1] - mm_tn(moves_ref[head, span], low(after))
                )
    fresh_add = {}
    for head, pair in cells:
        pieces = []
        for span in (2 * pair, 2 * pair + 1):
            if span == spans - 1:
                pieces.append(jnp.zeros((SPAN, LANES), WIDE))
            else:
                pieces.append(mm(span_of(keys[head], span), low(state_grads[head, span])))
        fresh_add[head, pair] = low(jnp.concatenate(pieces, axis=0))
    lasts, backs = {}, {}
    for head, pair in cells:
        last = early[head, pair] + mm_tn(solve_ref[head, pair], fresh_add[head, pair])
        lasts[head, pair] = last
        backs[head, pair] = part(betas[head], pair) * last
    system_grads, system_grads_back = {}, {}
    for head, pair in cells:
        last, new = low(lasts[head, pair]), part(fresh[head], pair)
        system_grads[head, pair] = low(jnp.where(strict, -mm_nt(last, new), 0.0))
        system_grads_back[head, pair] = low(jnp.where(upper_strict, -mm_nt(new, last), 0.0))
    query_grads, key_grads, beta_grads = [], [], []
    for head in range(heads):
        query_pieces, key_pieces, beta_pieces = [], [], []
        for pair in range(pairs):
            query, key = part(queries[head], pair), part(keys[head], pair)
            beta, new = part(betas[head], pair), part(fresh[head], pair)
            grad = part(output_grads[head], pair)
            stacked = jnp.concatenate(
                [score_grads[head, pair], system_grads[head, pair]], axis=0
            )
            through = mm(stacked, key)
            query_grad = through[:PAIR]
            key_grad = beta * through[PAIR:]
            wide = jnp.concatenate(
                [score_grads_back[head, pair], system_grads_back[head, pair]], axis=1
            )
            tall = jnp.concatenate([query, low(beta * key.astype(WIDE))], axis=0)
            key_grad = key_grad + mm(wide, tall)
            inner = low(jnp.where(strict, mm_nt(key, key), 0.0))
            residual = part(values[head], pair).astype(WIDE) - mm(inner, new)
            back = low(backs[head, pair])
            more_query, more_key, seen = [], [], []
            for local_span in range(2):
                span = 2 * pair + local_span
                new_span = span_of(new, local_span)
                if span == 0:
                    more_query.append(jnp.zeros((SPAN, LANES), WIDE))
                    seen.append(jnp.zeros((SPAN, LANES), WIDE))
                    more_key.append(mm_nt(new_span, low(state_grads[head, span])))
                    continue
                state = states_ref[head, span - 1]
                more_query.append(mm_nt(span_of(grad, local_span), state))
                seen.append(mm(span_of(key, local_span), state))
                taken = -span_of(back, local_span)
                if span == spans - 1:
                    more_key.append(mm_nt(taken, state))
                else:
                    left = jnp.concatenate([new_span, taken], axis=1)
                    right = jnp.concatenate([low(state_grads[head, span]), state], axis=1)
                    more_key.append(mm_nt(left, right))
            residual = residual - jnp.concatenate(seen, axis=0)
            query_pieces.append(query_grad + jnp.concatenate(more_query, axis=0))
            key_pieces.append(key_grad + jnp.concatenate(more_key, axis=0))
            beta_pieces.append(jnp.sum(lasts[head, pair] * residual, axis=1, keepdims=True))
        query_grads.append(jnp.concatenate(query_pieces, axis=0))
        key_grads.append(jnp.concatenate(key_pieces, axis=0))
        beta_grads.append(jnp.concatenate(beta_pieces, axis=0))
    lane_ids = lax.broadcasted_iota(jnp.int32, (length, LANES), 1)
    strengths_sum = strengths_sum_ref[...]
    for head in range(heads):
        beta = betas[head]
        strengths_sum = strengths_sum + jnp.where(
            lane_ids == step * heads + head, beta_grads[head] * beta * (1.0 - beta), 0.0
        )
    strengths_sum_ref[...] = strengths_sum

    active_grads = []
    for grads, scales, source in ((query_grads, query_scales, active[0]), (key_grads, key_scales, active[1])):
        pieces = []
        for head in range(heads):
            lanes = slice(head * LANES, (head + 1) * LANES)
            value, scale, grad = source[:, lanes], scales[head], grads[head]
            inner = jnp.sum(value * grad, axis=1, keepdims=True)
            pieces.append(scale * (grad - value * (scale * scale * inner)))
        active_grads.append(jnp.concatenate(pieces, axis=1))
    active_grads.append(
        jnp.concatenate(
            [jnp.concatenate([backs[head, pair] for pair in range(pairs)], axis=0) for head in range(heads)],
            axis=1,
        )
    )
    normed_grad = normed_grad_ref[step]
    for which in range(3):
        total, gate = totals[which], gates[which]
        total_grad = active_grads[which] * (gate * (1.0 + total * (1.0 - gate)))
        taps = taps_ref[which]
        linear = linear_ref[which].astype(WIDE)
        count = taps.shape[0]
        linear_grad = total_grad * taps[count - 1 : count]
        taps_grad_ref[which, count - 1 : count] = jnp.sum(total_grad * linear, axis=0, keepdims=True)
        for ahead in range(1, count):
            moved = shift_up(total_grad, ahead)
            place = slice(count - 1 - ahead, count - ahead)
            linear_grad = linear_grad + moved * taps[place]
            taps_grad_ref[which, place] = jnp.sum(moved * linear, axis=0, keepdims=True)
        linear_low = low(linear_grad)
        stack_ref[which] = linear_low
        normed_grad = normed_grad + mm_nt(linear_low, w_qkv_ref[step, which])
    normed_grad_ref[step] = normed_grad

    @pl.when(step == 1)
    def last_step():
        strengths_low = low(strengths_sum_ref[...])
        strengths_grad_ref[...] = strengths_low
        add_from_apart(info_ref, normed_grad_ref.at[1], normed_grad_ref.at[0])
        total = normed_grad_ref[0] + mm_nt(strengths_low, w_beta_ref[...])
        value_grad, gain_grad = norm_back(stream_ref[...].astype(WIDE), gain_ref[...], total, 1e-6)
        stream_grad_ref[...] = low(branch_ref[...] + value_grad)
        gain_grad_ref[...] = gain_grad


def mixer_backward(info, after, stream, branch, kept, gain, weights, w_beta, taps, out_gain, old):
    strengths, linear, output, fresh, solve, states, moves = kept
    length, width = stream.shape
    tile = weights[0].shape[2]
    inner = 2 * tile
    spans = length // SPAN
    pairs = length // PAIR
    here = tile // LANES
    out = jax.ShapeDtypeStruct
    count = taps.shape[1]
    in_specs = [
        ANYWHERE,
        ANYWHERE,
        ANYWHERE,
        whole((length, width)),
        whole((length, width)),
        whole((length, LANES)),
        tiled((3, length, tile), 2),
        tiled((length, tile), 1),
        tiled((length, tile), 1),
        tiled((here, pairs, PAIR, PAIR), 0),
        tiled((here, spans - 1, LANES, LANES), 0),
        tiled((here, spans - 2, LANES, LANES), 0),
        whole((1, width)),
        whole((width, LANES)),
        tiled((3, count, tile), 2),
        whole((1, LANES)),
    ] + [ANYWHERE] * 6
    body = lambda info_ref, *refs: mixer_backward_kernel(pl.program_id(0), True, info_ref, *refs[3:])
    kernel = or_keep(body, len(in_specs), 6, 1)
    more = old[1:]
    in_specs = in_specs + [
        whole((1, width)),
        tiled_old((6, length, tile), 2),
        whole((length, LANES)),
        tiled_old((3, count, tile), 2),
        whole((1, LANES)),
    ]
    return pl.pallas_call(
        kernel,
        name="mixer_backward",
        grid_spec=pltpu.PrefetchScalarGridSpec(
            num_scalar_prefetch=1,
            grid=(2,),
            in_specs=in_specs,
            out_specs=[
                whole((length, width)),
                whole((1, width)),
                tiled((6, length, tile), 2),
                whole((length, LANES)),
                tiled((3, count, tile), 2),
                whole((1, LANES)),
            ],
            scratch_shapes=[
                pltpu.VMEM((2, length, width), WIDE),
                pltpu.VMEM((length, LANES), WIDE),
                pltpu.VMEM((length, width), LOW),
                pltpu.VMEM((length, width), LOW),
                pltpu.VMEM((2, 3, width, tile), LOW),
                pltpu.VMEM((2, tile, width), LOW),
                pltpu.SemaphoreType.DMA((6,)),
            ],
        ),
        out_shape=[
            out((length, width), LOW),
            out((1, width), WIDE),
            out((6, length, inner), LOW),
            out((length, LANES), LOW),
            out((3, count, inner), WIDE),
            out((1, LANES), WIDE),
        ],
        compiler_params=params(),
        cost_estimate=cost(20),
    )(
        info, *after, stream, branch, strengths, linear, output, fresh, solve, states, moves,
        gain, w_beta, taps, out_gain, *weights, *more,
    )


def unit_tiles(units):
    count = -(-units // 512)
    size = -(-units // count // LANES) * LANES
    return [(start, min(size, units - start)) for start in range(0, units, size)]


def feed_tiles(refs, into_lift, into_down, sems):
    lift_ref, down_ref, lift_came, lift_twin, down_came, down_twin = refs
    tiles, at = [], 0
    for which in range(2):
        for start, size in unit_tiles(down_ref.shape[0]):
            span = pl.ds(start, size)
            if which == 0:
                lift = [(lift_ref.at[:, :, span], into_lift.at[0, :, :, span])]
                down = [(down_ref.at[span], into_down.at[0, span])]
            else:
                rows, columns = lift_came.shape[1], down_came.shape[1]
                lift = [
                    (lift_came.at[:, :, span], into_lift.at[1, :, pl.ds(0, rows), span]),
                    (lift_twin.at[:, :, span], into_lift.at[1, :, pl.ds(rows, rows), span]),
                ]
                down = [
                    (down_came.at[span], into_down.at[1, span, pl.ds(0, columns)]),
                    (down_twin.at[span], into_down.at[1, span, pl.ds(columns, columns)]),
                ]
            copies = []
            for group in (lift, down):
                copies.append([pltpu.make_async_copy(*pair, sems.at[at + i]) for i, pair in enumerate(group)])
                at += len(group)
            tiles.append((which, start, size, copies[0], copies[1]))
    return tiles


def start_each(copies):
    for copy in copies:
        copy.start()


def wait_each(copies):
    for copy in copies:
        copy.wait()


AHEAD = 3


def feed_forward_kernel(
    alone,
    info_ref,
    middle_ref,
    gain_ref,
    lift_own_ref,
    down_own_ref,
    lift_came_ref,
    lift_twin_ref,
    down_came_ref,
    down_twin_ref,
    result_ref,
    lifted_ref,
    total_ref,
    normed_ref,
    w_gate_up_ref,
    w_down_ref,
    kept_ref,
    sems,
    out_sems,
):
    units = down_own_ref.shape[0]
    refs = (lift_own_ref, down_own_ref, lift_came_ref, lift_twin_ref, down_came_ref, down_twin_ref)
    tiles = feed_tiles(refs, w_gate_up_ref, w_down_ref, sems)
    if alone:
        for tile in tiles[:AHEAD]:
            start_each(tile[3] + tile[4])
    middle = middle_ref[...]
    normed_ref[0] = low(middle * norm_scale(middle, 1e-6) * gain_ref[...])
    apart_order(info_ref, normed_ref.at[0], normed_ref.at[1])
    outs = []
    lifted = []
    for index in range(len(tiles) + 1):
        if index < len(tiles):
            which, start, size, lift, down = tiles[index]
            wait_each(lift)
        if index:
            wait_each(tiles[index - 1][4])
        if 0 < index <= len(tiles) - AHEAD:
            start_each(tiles[index + AHEAD - 1][3] + tiles[index + AHEAD - 1][4])
        if index < len(tiles):
            span = pl.ds(start, size)
            normed = normed_ref[which]
            gate = mm(normed, w_gate_up_ref[which, 0, :, span])
            up = mm(normed, w_gate_up_ref[which, 1, :, span])
            place = pl.ds(which * units + start, size)
            kept_ref[0, :, place] = low(gate)
            kept_ref[1, :, place] = low(up)
            lifted.append((gate, up))
        if index:
            which, start, size, lift, down = tiles[index - 1]
            span = pl.ds(start, size)
            place = pl.ds(which * units + start, size)
            if alone:
                outs.append(
                    pltpu.make_async_copy(
                        kept_ref.at[:, :, place], lifted_ref.at[:, :, place], out_sems.at[index - 1]
                    )
                )
                outs[-1].start()
            gate, up = lifted[index - 1]
            hidden = low(gate * sigmoid(gate) * up)
            part = mm(hidden, w_down_ref[which, span, :])
            if start:
                total_ref[which] += part
            else:
                total_ref[which] = part + middle if which == 0 else part
    add_from_apart(info_ref, total_ref.at[1], total_ref.at[0], DOWN)
    result_ref[...] = low(total_ref[0])
    wait_each(outs)


def feed_forward(info, middle, gain, weights, wrap=lambda kernel: kernel):
    length, width = middle.shape
    units = weights[1].shape[0]
    count = 2 * len(unit_tiles(units))
    out = jax.ShapeDtypeStruct
    return pl.pallas_call(
        wrap(lambda *refs: feed_forward_kernel(True, *refs)),
        name="feed_forward",
        grid_spec=pltpu.PrefetchScalarGridSpec(
            num_scalar_prefetch=1,
            grid=(1,),
            in_specs=[whole((length, width)), whole((1, width))] + [ANYWHERE] * 6,
            out_specs=[whole((length, width)), ANYWHERE],
            scratch_shapes=[
                pltpu.VMEM((2, length, width), WIDE),
                pltpu.VMEM((2, length, width), LOW),
                pltpu.VMEM((2, 2, width, units), LOW),
                pltpu.VMEM((2, units, width), LOW),
                pltpu.VMEM((2, length, 2 * units), LOW),
                pltpu.SemaphoreType.DMA((3 * count,)),
                pltpu.SemaphoreType.DMA((count,)),
            ],
        ),
        out_shape=[out((length, width), LOW), out((2, length, 2 * units), LOW)],
        compiler_params=params(),
        cost_estimate=cost(10),
    )(info, middle, gain, *weights)


def feed_backward_kernel(
    alone,
    info_ref,
    middle_ref,
    grad_ref,
    gain_ref,
    lifted_ref,
    lift_own_ref,
    down_own_ref,
    lift_came_ref,
    lift_twin_ref,
    down_came_ref,
    down_twin_ref,
    middle_grad_ref,
    gain_grad_ref,
    stack_ref,
    normed_grad_ref,
    grads_ref,
    w_gate_up_ref,
    w_down_ref,
    kept_ref,
    made_ref,
    sems,
    in_sems,
    out_sems,
):
    width = middle_ref.shape[1]
    units = down_own_ref.shape[0]
    refs = (lift_own_ref, down_own_ref, lift_came_ref, lift_twin_ref, down_came_ref, down_twin_ref)
    tiles = feed_tiles(refs, w_gate_up_ref, w_down_ref, sems)
    ins, outs = [], []
    for index, (which, start, size, lift, down) in enumerate(tiles):
        place = pl.ds(which * units + start, size)
        if alone:
            ins.append(
                pltpu.make_async_copy(lifted_ref.at[:, :, place], kept_ref.at[:, :, place], in_sems.at[index])
            )
        first, at = pl.ds(0, 2), out_sems.at
        outs.append(
            [
                pltpu.make_async_copy(kept_ref.at[:, :, place], stack_ref.at[first, :, place], at[2 * index]),
                pltpu.make_async_copy(made_ref.at[0, :, place], stack_ref.at[2, :, place], at[2 * index + 1]),
            ]
        )
    for index in range(AHEAD if alone else 0):
        start_each(tiles[index][4] + [ins[index]] + tiles[index][3])
    middle = middle_ref[...]
    made_ref[1] = jnp.zeros(made_ref.shape[1:], LOW)
    made_ref[1, :, :width] = low(middle * norm_scale(middle, 1e-6) * gain_ref[...])
    made_ref[1, :, units : units + width] = grad_ref[...]
    ends = pltpu.make_async_copy(made_ref.at[1], stack_ref.at[3], out_sems.at[2 * len(tiles)])
    ends.start()
    grads_ref[0] = grad_ref[...]
    apart_order(info_ref, grads_ref.at[0], grads_ref.at[1], DOWN)
    hidden_grads = []
    for index in range(len(tiles) + 1):
        if index < len(tiles):
            which, start, size, lift, down = tiles[index]
            if alone:
                wait_each(down)
        if index and alone:
            ins[index - 1].wait()
            wait_each(tiles[index - 1][3])
        if alone and 0 < index <= len(tiles) - AHEAD:
            more = index + AHEAD - 1
            start_each(tiles[more][4] + [ins[more]] + tiles[more][3])
        if index < len(tiles):
            span = pl.ds(start, size)
            hidden_grads.append(mm_nt(grads_ref[which], w_down_ref[which, span, :]))
        if index:
            which, start, size, lift, down = tiles[index - 1]
            span = pl.ds(start, size)
            place = pl.ds(which * units + start, size)
            hidden_grad = hidden_grads[index - 1]
            gate = kept_ref[0, :, place].astype(WIDE)
            up = kept_ref[1, :, place].astype(WIDE)
            open_ = sigmoid(gate)
            silu = gate * open_
            up_grad = low(hidden_grad * silu)
            gate_grad = low(hidden_grad * up * (open_ + silu * (1.0 - open_)))
            kept_ref[0, :, place] = gate_grad
            kept_ref[1, :, place] = up_grad
            made_ref[0, :, place] = low(silu * up)
            start_each(outs[index - 1])
            part = mm_nt(gate_grad, w_gate_up_ref[which, 0, :, span]) + mm_nt(
                up_grad, w_gate_up_ref[which, 1, :, span]
            )
            if start:
                normed_grad_ref[which] += part
            else:
                normed_grad_ref[which] = part
    add_from_apart(info_ref, normed_grad_ref.at[1], normed_grad_ref.at[0])
    value_grad, gain_grad = norm_back(middle, gain_ref[...], normed_grad_ref[0], 1e-6)
    middle_grad_ref[...] = grad_ref[...].astype(WIDE) + value_grad
    gain_grad_ref[...] = gain_grad
    for copies in outs:
        wait_each(copies)
    ends.wait()


def feed_backward(info, after, middle, grad, lifted, gain, weights, old):
    length, width = middle.shape
    units = weights[1].shape[0]
    count = 2 * len(unit_tiles(units))
    out = jax.ShapeDtypeStruct
    waits = len(after)
    in_specs = [ANYWHERE] * waits + [whole((length, width)), whole((length, width)), whole((1, width))] + [ANYWHERE] * 7
    body = lambda info_ref, *refs: feed_backward_kernel(True, info_ref, *refs[waits:])
    kernel = or_keep(body, len(in_specs), 3, 1, 1)
    in_specs = in_specs + [whole((1, width)), ANYWHERE]
    more, aliases = old[1:], {len(in_specs): 2}
    return pl.pallas_call(
        kernel,
        name="feed_backward",
        grid_spec=pltpu.PrefetchScalarGridSpec(
            num_scalar_prefetch=1,
            grid=(1,),
            in_specs=in_specs,
            out_specs=[whole((length, width)), whole((1, width)), ANYWHERE],
            scratch_shapes=[
                pltpu.VMEM((2, length, width), WIDE),
                pltpu.VMEM((2, length, width), LOW),
                pltpu.VMEM((2, 2, width, units), LOW),
                pltpu.VMEM((2, units, width), LOW),
                pltpu.VMEM((2, length, 2 * units), LOW),
                pltpu.VMEM((2, length, 2 * units), LOW),
                pltpu.SemaphoreType.DMA((3 * count,)),
                pltpu.SemaphoreType.DMA((count,)),
                pltpu.SemaphoreType.DMA((2 * count + 1,)),
            ],
        ),
        out_shape=[
            out((length, width), WIDE),
            out((1, width), WIDE),
            out((4, length, 2 * units), LOW),
        ],
        input_output_aliases=aliases,
        compiler_params=params(),
        cost_estimate=cost(13),
    )(info, *after, middle, grad, gain, lifted, *weights, *more)


def feed_forward_half(which, units, lows_ref, w_gate_up_ref, w_down_ref, kept_ref, totals_ref):
    normed = lows_ref[which]
    lifted = []
    tiles = unit_tiles(units)
    for index in range(len(tiles) + 1):
        if index < len(tiles):
            start, size = tiles[index]
            span, place = pl.ds(start, size), pl.ds(pl.multiple_of(which * units + start, LANES), size)
            gate = mm(normed, w_gate_up_ref[which, 0, :, span])
            up = mm(normed, w_gate_up_ref[which, 1, :, span])
            kept_ref[0, :, place] = low(gate)
            kept_ref[1, :, place] = low(up)
            lifted.append((gate, up))
        if index:
            start, size = tiles[index - 1]
            gate, up = lifted[index - 1]
            part = mm(low(gate * sigmoid(gate) * up), w_down_ref[which, pl.ds(start, size), :])
            if index > 1:
                totals_ref[which] += part
            else:
                totals_ref[which] = part


def feed_backward_half(which, units, lows_ref, w_gate_up_ref, w_down_ref, kept_ref, made_ref, totals_ref):
    grads = lows_ref[which]
    hidden_grads = []
    tiles = unit_tiles(units)
    for index in range(len(tiles) + 1):
        if index < len(tiles):
            start, size = tiles[index]
            hidden_grads.append(mm_nt(grads, w_down_ref[which, pl.ds(start, size), :]))
        if index:
            start, size = tiles[index - 1]
            span, place = pl.ds(start, size), pl.ds(pl.multiple_of(which * units + start, LANES), size)
            hidden_grad = hidden_grads[index - 1]
            gate = kept_ref[0, :, place].astype(WIDE)
            up = kept_ref[1, :, place].astype(WIDE)
            open_ = sigmoid(gate)
            silu = gate * open_
            up_grad = low(hidden_grad * silu)
            gate_grad = low(hidden_grad * up * (open_ + silu * (1.0 - open_)))
            kept_ref[0, :, place] = gate_grad
            kept_ref[1, :, place] = up_grad
            made_ref[0, :, place] = low(silu * up)
            part = mm_nt(gate_grad, w_gate_up_ref[which, 0, :, span]) + mm_nt(
                up_grad, w_gate_up_ref[which, 1, :, span]
            )
            if index > 1:
                totals_ref[which] += part
            else:
                totals_ref[which] = part


def second_layer_kernel(
    info_ref,
    after_ref,
    stream_ref,
    grad_ref,
    gain_ref,
    feed_gain_ref,
    w_beta_ref,
    taps_ref,
    out_gain_ref,
    qkv_own_ref,
    out_own_ref,
    qkv_came_ref,
    qkv_twin_ref,
    out_came_ref,
    out_twin_ref,
    lift_own_ref,
    down_own_ref,
    lift_came_ref,
    lift_twin_ref,
    down_came_ref,
    down_twin_ref,
    result_ref,
    stream_grad_ref,
    feed_gain_grad_ref,
    gain_grad_ref,
    strengths_grad_ref,
    taps_grad_ref,
    out_gain_grad_ref,
    feed_stack_ref,
    stack_ref,
    middle_ref,
    branch_ref,
    strengths_ref,
    linear_ref,
    out_ref,
    fresh_ref,
    solve_ref,
    states_ref,
    moves_ref,
    normed_ref,
    w_qkv_ref,
    w_out_ref,
    totals_ref,
    lows_ref,
    w_gate_up_ref,
    w_down_ref,
    kept_ref,
    made_ref,
    strengths_sum_ref,
    branch_low_ref,
    again_ref,
    stacks_ref,
    sems,
    feed_sems,
    out_sems,
    stack_sems,
):
    turn = pl.program_id(0)
    tile = taps_ref.shape[3]
    mixer_weights = (qkv_own_ref, out_own_ref, qkv_came_ref, qkv_twin_ref, out_came_ref, out_twin_ref)
    feed_weights = (lift_own_ref, down_own_ref, lift_came_ref, lift_twin_ref, down_came_ref, down_twin_ref)
    tiles = feed_tiles(feed_weights, w_gate_up_ref, w_down_ref, feed_sems)

    def leave(which):
        columns = pl.ds(which * tile, tile)
        return pltpu.make_async_copy(stacks_ref.at[which], stack_ref.at[:, :, columns], stack_sems.at[which])

    @pl.when(turn < 2)
    def forward():
        mixer_forward_kernel(
            turn,
            info_ref,
            stream_ref,
            gain_ref,
            w_beta_ref,
            taps_ref.at[turn],
            out_gain_ref,
            *mixer_weights,
            middle_ref,
            strengths_ref,
            linear_ref.at[turn],
            out_ref.at[turn],
            fresh_ref.at[turn],
            solve_ref.at[turn],
            states_ref.at[turn],
            moves_ref.at[turn],
            normed_ref,
            w_qkv_ref,
            w_out_ref,
            sems,
        )

    units, width = down_own_ref.shape[0], middle_ref.shape[1]
    half_tiles = len(tiles) // 2
    whole_stack = [
        pltpu.make_async_copy(kept_ref, feed_stack_ref.at[pl.ds(0, 2)], out_sems.at[0]),
        pltpu.make_async_copy(made_ref, feed_stack_ref.at[pl.ds(2, 2)], out_sems.at[1]),
    ]

    for which in range(2):

        @pl.when(turn == which)
        def ahead():
            for item in tiles[which * half_tiles : (which + 1) * half_tiles]:
                start_each(item[3] + item[4])

        @pl.when(turn == 2 + which)
        def arrived():
            for item in tiles[which * half_tiles : (which + 1) * half_tiles]:
                wait_each(item[3] + item[4])

    @pl.when(turn == 2)
    def feed_first():
        middle = middle_ref[...]
        lows_ref[0] = low(middle * norm_scale(middle, 1e-6) * feed_gain_ref[...])
        made_ref[1] = jnp.zeros(made_ref.shape[1:], LOW)
        made_ref[1, :, :width] = lows_ref[0]
        apart_order(info_ref, lows_ref.at[0], lows_ref.at[1])

    @pl.when((turn == 2) | (turn == 3))
    def feed():
        feed_forward_half(turn - 2, units, lows_ref, w_gate_up_ref, w_down_ref, kept_ref, totals_ref)

    @pl.when(turn == 3)
    def feed_last():
        add_from_apart(info_ref, totals_ref.at[1], totals_ref.at[0], DOWN)
        result_ref[...] = low(totals_ref[0] + middle_ref[...])

    @pl.when(turn == 4)
    def feed_back_first():
        made_ref[1, :, units : units + width] = grad_ref[...]
        lows_ref[0] = grad_ref[...]
        apart_order(info_ref, lows_ref.at[0], lows_ref.at[1], DOWN)

    @pl.when((turn == 4) | (turn == 5))
    def feed_back():
        feed_backward_half(turn - 4, units, lows_ref, w_gate_up_ref, w_down_ref, kept_ref, made_ref, totals_ref)

    @pl.when(turn == 5)
    def feed_back_last():
        start_each(whole_stack)
        add_from_apart(info_ref, totals_ref.at[1], totals_ref.at[0])
        value_grad, gain_grad = norm_back(middle_ref[...], feed_gain_ref[...], totals_ref[0], 1e-6)
        branch_ref[...] = grad_ref[...].astype(WIDE) + value_grad
        feed_gain_grad_ref[...] = gain_grad

    @pl.when(turn >= 6)
    def backward():
        half = turn - 6
        mixer_backward_kernel(
            half,
            False,
            info_ref,
            stream_ref,
            branch_ref,
            strengths_ref,
            linear_ref.at[half],
            out_ref.at[half],
            fresh_ref.at[half],
            solve_ref.at[half],
            states_ref.at[half],
            moves_ref.at[half],
            gain_ref,
            w_beta_ref,
            taps_ref.at[half],
            out_gain_ref,
            *mixer_weights,
            stream_grad_ref,
            gain_grad_ref,
            stacks_ref.at[half],
            strengths_grad_ref,
            taps_grad_ref.at[half],
            out_gain_grad_ref,
            totals_ref,
            strengths_sum_ref,
            branch_low_ref,
            again_ref,
            w_qkv_ref,
            w_out_ref,
            None,
        )

    for which in range(2):

        @pl.when(turn == 6 + which)
        def start_leaving():
            leave(which).start()

    @pl.when(turn == 7)
    def wait_leaving():
        wait_each(whole_stack)
        leave(0).wait()
        leave(1).wait()


def second_layer(info, after, stream, grad, gains, w_beta, taps, out_gain, mixer_weights, feed_weights):
    length, width = stream.shape
    tile, units = mixer_weights[0].shape[2], feed_weights[1].shape[0]
    inner, spans, pairs, here = 2 * tile, length // SPAN, length // PAIR, tile // LANES
    taps_count = taps.shape[1]
    count = 2 * len(unit_tiles(units))
    out = jax.ShapeDtypeStruct
    taps = jnp.moveaxis(taps.reshape(3, taps_count, 2, tile), 2, 0)
    results = pl.pallas_call(
        only_second(second_layer_kernel),
        name="second_layer",
        grid_spec=pltpu.PrefetchScalarGridSpec(
            num_scalar_prefetch=1,
            grid=(8,),
            in_specs=[
                ANYWHERE,
                whole((length, width)),
                whole((length, width)),
                whole((1, width)),
                whole((1, width)),
                whole((width, LANES)),
                whole((2, 3, taps_count, tile)),
                whole((1, LANES)),
            ]
            + [ANYWHERE] * 12,
            out_specs=[
                whole((length, width)),
                whole((length, width)),
                whole((1, width)),
                whole((1, width)),
                whole((length, LANES)),
                whole((2, 3, taps_count, tile)),
                whole((1, LANES)),
                ANYWHERE,
                ANYWHERE,
            ],
            scratch_shapes=[
                pltpu.VMEM((length, width), WIDE),
                pltpu.VMEM((length, width), WIDE),
                pltpu.VMEM((length, LANES), WIDE),
                pltpu.VMEM((2, 3, length, tile), LOW),
                pltpu.VMEM((2, length, tile), LOW),
                pltpu.VMEM((2, length, tile), LOW),
                pltpu.VMEM((2, here, pairs, PAIR, PAIR), LOW),
                pltpu.VMEM((2, here, spans - 1, LANES, LANES), LOW),
                pltpu.VMEM((2, here, spans - 2, LANES, LANES), LOW),
                pltpu.VMEM((2, length, width), LOW),
                pltpu.VMEM((2, 3, width, tile), LOW),
                pltpu.VMEM((2, tile, width), LOW),
                pltpu.VMEM((2, length, width), WIDE),
                pltpu.VMEM((2, length, width), LOW),
                pltpu.VMEM((2, 2, width, units), LOW),
                pltpu.VMEM((2, units, width), LOW),
                pltpu.VMEM((2, length, 2 * units), LOW),
                pltpu.VMEM((2, length, 2 * units), LOW),
                pltpu.VMEM((length, LANES), WIDE),
                pltpu.VMEM((length, width), LOW),
                pltpu.VMEM((length, width), LOW),
                pltpu.VMEM((2, 6, length, tile), LOW),
                pltpu.SemaphoreType.DMA((6,)),
                pltpu.SemaphoreType.DMA((3 * count,)),
                pltpu.SemaphoreType.DMA((2,)),
                pltpu.SemaphoreType.DMA((2,)),
            ],
        ),
        out_shape=[
            out((length, width), LOW),
            out((length, width), LOW),
            out((1, width), WIDE),
            out((1, width), WIDE),
            out((length, LANES), LOW),
            out((2, 3, taps_count, tile), WIDE),
            out((1, LANES), WIDE),
            out((4, length, 2 * units), LOW),
            out((6, length, inner), LOW),
        ],
        compiler_params=pltpu.CompilerParams(dimension_semantics=("arbitrary",), vmem_limit_bytes=60 * 2**20),
        cost_estimate=cost(50),
    )(info, after, stream, grad, gains[0:1], gains[1:2], w_beta, taps, out_gain, *mixer_weights, *feed_weights)
    result, stream_grad, feed_gain, gain, strengths, taps_grad, out_gain_grad, feed_stack, stack = results
    taps_grad = jnp.moveaxis(taps_grad, 0, 2).reshape(3, taps_count, inner)
    return result, (None, feed_gain, feed_stack), (stream_grad, gain, stack, strengths, taps_grad, out_gain_grad)


def rows_kernel(halves, width, count, info_ref, *refs):
    lefts, rights = refs[:count], refs[count : 2 * count]
    keep_ref, send_ref, turned_ref, rows_ref = refs[2 * count :]
    size = width // halves // 8

    @pl.when((pl.program_id(0) == 0) & (pl.program_id(1) == 0))
    def first():
        for item in range(count):
            turned_ref[item] = lefts[item][:, :width].T
            place = 0
            for which in range(halves):
                for index in (0, 2, 1, 3):
                    start = which * (width // halves) + info_ref[index] * size
                    source = pl.ds(pl.multiple_of(start, size), size)
                    rows_ref[item, place : place + size, :] = turned_ref[item, source, :]
                    place += size

    tile = keep_ref.shape[1]
    if rights[0].shape[1] == tile:
        pieces = [right[...] for right in rights]
    else:
        columns = pl.ds(pl.multiple_of(pl.program_id(1) * tile, tile), tile)
        pieces = [right[:, columns] for right in rights]
    total = mm(rows_ref[0], pieces[0])
    for item in range(1, count):
        total = total + mm(rows_ref[item], pieces[item])
    half = keep_ref.shape[0]
    keep_ref[...] = low(total[:half])
    send_ref[...] = low(total[half:])


def rows_grads(info, after, items, left, right, groups, halves, tile, tiles):
    length = items[0].shape[1]
    count = len(items)
    rows = left[3] // 2
    spread = 1 if right[1] == tile else 0
    half = pl.BlockSpec((None, rows // 2, tile), lambda g, t, info: (g, 0, t))
    shape = jax.ShapeDtypeStruct((groups, rows // 2, tile * tiles), LOW)
    return pl.pallas_call(
        lambda info_ref, *refs: rows_kernel(halves, left[3], count, info_ref, *refs[len(after) :]),
        name="rows_grads",
        grid_spec=pltpu.PrefetchScalarGridSpec(
            num_scalar_prefetch=1,
            grid=(groups, tiles),
            in_specs=[ANYWHERE] * len(after)
            + [pl.BlockSpec((None, length, left[1]), lambda g, t, info: (left[0], 0, left[2]))] * count
            + [pl.BlockSpec((None, length, right[1]), lambda g, t, info: (right[0] + g, 0, right[2] + spread * t))]
            * count,
            out_specs=[half, half],
            scratch_shapes=[pltpu.VMEM((count, left[3], length), LOW), pltpu.VMEM((count, rows, length), LOW)],
        ),
        out_shape=[shape, shape],
        compiler_params=pltpu.CompilerParams(
            dimension_semantics=("arbitrary", "arbitrary"), vmem_limit_bytes=40 * 2**20
        ),
        cost_estimate=cost(10),
    )(info, *after, *items, *items)


def halve(after, keep, came, axis):
    def kernel(after_ref, keep_ref, came_ref, *outs):
        total = keep_ref[...].astype(WIDE) + came_ref[...].astype(WIDE)
        if axis is None:
            outs[0][...] = total
        else:
            size = total.shape[axis - 1] // 2
            for i in range(2):
                at = slice(i * size, (i + 1) * size)
                outs[i][...] = low(total[at] if axis == 1 else total[:, at])

    groups, rows, columns = keep.shape
    shape = {None: (rows, columns), 1: (rows // 2, columns), 2: (rows, columns // 2)}[axis]
    count, dtype = (1, WIDE) if axis is None else (2, LOW)
    block = pl.BlockSpec((None, rows, columns), lambda g: (g, 0, 0))
    return pl.pallas_call(
        kernel,
        name="halve",
        grid=(groups,),
        in_specs=[ANYWHERE, block, block],
        out_specs=[pl.BlockSpec((None, *shape), lambda g: (g, 0, 0))] * count,
        out_shape=[jax.ShapeDtypeStruct((groups, *shape), dtype)] * count,
        compiler_params=params(16 * 2**20),
        cost_estimate=cost(2),
    )(after, keep, came)


def tied(*values):
    return lax.optimization_barrier(values)


def exchange(value, axis, apart):
    return lax.ppermute(value, axis, [(i, i ^ apart(i)) for i in range(lax.axis_size(axis))])


def unpack(packed, like):
    found, start = [], 0
    for item in like:
        found.append(packed[start : start + item.size].reshape(item.shape))
        start += item.size
    return found


def pack(items):
    return jnp.concatenate([item.reshape(-1) for item in items])


def local(
    inputs, cotangent, w_qkv, w_beta, conv_taps, w_out, w_gate_up, w_down, norm_gains, out_gains
):
    batches, unused, length, width = inputs.shape
    place = lax.axis_index("section")
    rank, half = place // 2, place % 2
    me, copies = lax.axis_index("dp"), lax.axis_size("dp")
    per = batches // 2
    cube = copies == 8

    def across(value, bits=1):
        return exchange(value, "section", lambda i: bits)

    def flip(value, even, odd):
        return exchange(value, "dp", lambda i: odd if i % 2 else even)

    def by_half(own, other, axis):
        return jnp.where(
            half == 0, jnp.concatenate([own, other], axis), jnp.concatenate([other, own], axis)
        )

    first_apart = 2 + 2 * (me % 2)

    def mine_of(value, axis):
        size = value.shape[axis] // copies
        return lax.dynamic_slice_in_dim(value, me * size, size, axis)

    def collect(came, axis):
        came = jnp.concatenate([came, flip(came, 2, 4)], axis)
        came = jnp.concatenate([came, flip(came, 4, 2)], axis)
        return came, flip(came, 1, 1)

    smalls = [conv_taps, w_beta.astype(WIDE), norm_gains, out_gains]
    others = unpack(across(pack(smalls)), smalls)
    taps = jnp.concatenate([conv_taps, others[0]], 2)
    heads = w_beta.shape[1]
    w_beta = jnp.concatenate([w_beta, low(others[1])], 1)
    w_beta = jnp.pad(w_beta, ((0, 0), (0, LANES - 2 * heads)))
    gains = by_half(norm_gains, others[2], 1)
    out_gain = by_half(out_gains, others[3], 0)[None]
    inner, units = w_out.shape[0], w_down.shape[0]
    tile = w_qkv.shape[2]

    if cube:
        block = width // copies
        core = me % 2
        corner = 2 * ((me // 2 + me // 4) % 2) + core
        quarter, rows = width // 4, inner // 2
        came = across(mine_of(w_qkv, 1))
        came, lift = tied(came, mine_of(w_gate_up, 1))
        lift = across(lift)
        lift, out = tied(lift, lax.dynamic_slice_in_dim(w_out, core * rows, rows, 0))
        out = across(out)
        out, down = tied(out, lax.dynamic_slice_in_dim(w_down, corner * quarter, quarter, 1))
        down = across(down)
        mixer_weights = (w_qkv, w_out, *collect(came, 1), out, flip(out, 1, 1))
        near = flip(lift, 2, 4)
        lift = jnp.concatenate([lift, near], 1)
        far = flip(lift, 4, 2)
        apart = [0, first_apart, 6 - first_apart, 6, 1, 7 - first_apart, 1 + first_apart, 7]
        places = [me ^ bits for bits in apart]
        down_places = [2 * (corner ^ bits) + i for bits in (0, 2, 1, 3) for i in range(2)]
    else:

        def gathered(value):
            return lax.all_gather(across(mine_of(value, 1)), "dp", axis=1, tiled=True)

        def halves_of(value):
            return jnp.split(gathered(value), 2, 1)

        out = lax.all_gather(across(mine_of(w_out, 0)), "dp", axis=0, tiled=True)
        mixer_weights = (w_qkv, w_out, *halves_of(w_qkv), *jnp.split(out, 2, 0))
        feed_weights = (w_gate_up, w_down, *halves_of(w_gate_up), *halves_of(w_down))
        places = down_places = list(range(8))
        core, near = 0, taps
    info = jnp.stack([jnp.asarray(item, jnp.int32) for item in places + [rank == 0] + down_places + [core, 1 - core, rank == 1]])

    def mixer_part(after, stream, *wrap):
        return mixer_forward(info, after, stream, gains[0:1], mixer_weights, w_beta, taps, out_gain, *wrap)

    def feed_back(after, grad, saved, old):
        stream, middle, kept, lifted = saved
        return feed_backward(info, after, middle, grad, lifted, gains[1:2], feed_weights, old)

    def mixer_back(after, middle_grad, saved, old):
        stream, middle, kept, lifted = saved
        return mixer_backward(
            info, after, stream, middle_grad, kept, gains[0:1], mixer_weights, w_beta, taps, out_gain, old
        )

    def own(value):
        items = lax.dynamic_slice_in_dim(value, half * per, per, 0)
        return [items[i, 0] for i in range(per)]

    up = [(0, 2), (1, 3)]
    streams = own(inputs)
    saved0 = []
    for stream in streams:
        near, *kept = mixer_part(near, stream)
        saved0.append([stream, near, kept])
    if cube:
        far, down, saved0[0][1] = tied(far, down, saved0[0][1])
        lift = jnp.concatenate([lift, far], 1)
        lift_twin = flip(lift, 1, 1)
        down = jnp.concatenate([down, flip(down, 2, 4)], 1)
        down, saved0[-1][1] = tied(down, saved0[-1][1])
        feed_weights = (w_gate_up, w_down, lift, lift_twin, down, flip(down, 1, 1))
    firsts = []
    for saved in saved0:
        result, lifted = feed_forward(info, saved[1], gains[1:2], feed_weights)
        saved.append(lifted)
        firsts.append(result)
    grads = own(cotangent)
    streams = [lax.ppermute(firsts[0], "section", up)]
    after = taps
    if per > 1:
        through, streams[0], firsts[1] = tied(info.astype(WIDE), streams[0], firsts[1])
        after = lax.ppermute(through, "section", [(0, 1), (1, 0)])
        for index in range(1, per):
            firsts[index], after = tied(firsts[index], after)
            streams.append(lax.ppermute(firsts[index], "section", up))
    results, returned, feeds, mixes = [], [], [], []
    for index in range(per):
        result, feed, mix = second_layer(
            info, after, streams[index], grads[index], gains, w_beta, taps, out_gain, mixer_weights, feed_weights
        )
        results.append(result)
        feeds.append(feed)
        mixes.append(mix)
        after = mix[0]
        returned.append(lax.ppermute(after, "section", [(2, 0), (3, 1)]))
    feed_twins, mix_twins = [], []
    waited = [mixes[-1][0]]
    for index, (grad, saved) in enumerate(zip(returned, saved0)):
        feeds[index] = feed_back(waited, grad, saved, feeds[index])
        after = (taps, taps, taps)
        if cube:
            feed_twins.append(flip(feeds[index][2], 1, 1))
            if index:
                after = (feed_twins[index - 1], mix_twins[index - 1], taps)
        mixes[index] = mixer_back(after, feeds[index][0], saved, mixes[index])
        waited = [mixes[index][0]]
        if cube:
            mix_twins.append(flip(mixes[index][2], 1, 1))
    feed_all = [feed[2] for feed in feeds] + feed_twins
    held = jnp.stack([jnp.where(rank == 1, result, mix[0]) for result, mix in zip(results, mixes)])
    column = width // 2
    moved = across(lax.dynamic_slice_in_dim(held, (1 - rank) * column, column, 2), 2)
    held = lax.dynamic_slice_in_dim(held, rank * column, column, 2)
    mix_all = [mix[2] for mix in mixes]
    if cube:
        mix_all = mix_all + mix_twins
        plans = (
            (feed_all, (3, units, 0, width), (0, units, 0), 2, 1, units, 2),
            (feed_all, (2, 2 * units, 0, 2 * units), (3, units, 1), 1, 2, width // 2, 2),
            (mix_all, (5, width, 0, width), (0, width, 0), 3, 1, width, 1),
            (mix_all, (3, width, 0, width), (4, width, 0), 1, 2, width, 1),
        )
        after, kept, came = [mixes[-1][1]], [], []
        for index, plan in enumerate(plans):
            keep, send = rows_grads(info, after, *plan)
            after = [keep]
            kept.append(keep)
            came.append(across(send) if index % 2 else flip(send, 2, 4))
        after = kept[-1]
        lifts, downs, qkvs, outs = range(4)

        def turn(which, axis, onward=None):
            nonlocal after
            parts = halve(after, kept[which], came[which], axis)
            after = kept[which] = parts[0]
            if axis is not None:
                came[which] = onward(parts[1])

        def far(value):
            return flip(value, 4, 2)

        def near_flip(value):
            return flip(value, 2, 4)

        marks = [kept[downs]]
        turn(lifts, 1, far)
        turn(downs, 1, near_flip)
        marks.append(after)
        turn(outs, 1, near_flip)
        turn(qkvs, 1, far)
        marks.append(after)
        turn(lifts, 2, across)
        marks.append(after)
        turn(downs, 1, far)
        turn(outs, 1, far)
        marks.append(after)
        turn(qkvs, 2, across)
        marks.append(after)
        turn(lifts, None)
        marks.append(after)
        turn(downs, None)
        turn(outs, None)
        turn(qkvs, None)
        grad_gate_up, grad_down, grad_qkv, grad_out = kept[0], kept[1][0], kept[2], kept[3][0]
    else:

        def tall(items, index):
            return jnp.concatenate([item[index] for item in items], 0)

        def total(value, axis, split):
            value = lax.psum_scatter(low(value), "dp", scatter_dimension=axis, tiled=True)
            size = value.shape[split] // 2
            mine = lax.slice_in_dim(value, 0, size, axis=split)
            theirs = lax.slice_in_dim(value, size, 2 * size, axis=split)
            return mine.astype(WIDE) + across(theirs).astype(WIDE)

        ends = tall(feed_all, 3)
        normed2, grad, normed = ends[:, :width], ends[:, units : units + width], tall(mix_all, 5)
        grad_gate_up = total(jnp.stack([mm_tn(normed2, tall(feed_all, i)) for i in range(2)]), 1, 2)
        grad_qkv = total(jnp.stack([mm_tn(normed, tall(mix_all, i)) for i in range(3)]), 1, 2)
        down = mm_tn(tall(feed_all, 2), grad).reshape(2, units, width)
        out = mm_tn(tall(mix_all, 3), tall(mix_all, 4)).reshape(2, inner, width)
        grad_down, grad_out = total(down, 1, 0)[0], total(out, 1, 0)[0]

    strengths = [mix[3] for mix in mixes]
    if cube:
        strengths[0] = tied(strengths[0], marks[3])[0]
        moved = tied(moved, marks[1])[0]
    d_beta = sum(mm_tn(mix[5], item) for mix, item in zip(mix_all, strengths))[:, : 2 * heads]
    d_taps = sum(mix[4] for mix in mixes)
    d_gains = jnp.concatenate([sum(mix[1] for mix in mixes), sum(feed[1] for feed in feeds)], 0)
    d_out_gain = sum(mix[5] for mix in mixes)

    flat = [d_taps, d_beta, d_gains, d_out_gain]
    packed = pack(flat)
    if cube:
        for bits, mark in zip((1, 2, 4), marks[4:]):
            packed = packed + tied(flip(packed, bits, bits), mark)[0]
    else:
        packed = lax.psum(packed, "dp")
    d_taps, d_beta, d_gains, d_out_gain = unpack(packed, flat)

    def part(value, axis, size):
        return lax.dynamic_slice_in_dim(value, me * size, size, axis)

    def halves(value, axis):
        size = value.shape[axis] // 2
        return [
            lax.dynamic_slice_in_dim(value, which * size, size, axis) for which in (half, 1 - half)
        ]

    pieces = [
        [part(d_taps[:, :, i * inner : (i + 1) * inner], 2, inner // copies) for i in range(2)],
        [part(d_beta[:, i * heads : (i + 1) * heads], 0, width // copies) for i in range(2)],
        [part(item, 1, width // 2 // copies) for item in halves(d_gains, 1)],
        [part(item, 1, LANES // 2 // copies) for item in halves(d_out_gain, 1)],
    ]
    mine = [item[0] for item in pieces]
    came = unpack(across(pack([item[1] for item in pieces])), mine)
    grad_taps, grad_beta, grad_gains, grad_out_gains = [a + b for a, b in zip(mine, came)]

    kinds = jnp.stack([jnp.where(rank == 1, held, moved), jnp.where(rank == 1, moved, held)])
    mine, theirs = [
        lax.dynamic_slice_in_dim(kinds, which * column // 2, column // 2, 3) for which in (half, 1 - half)
    ]
    final_stream, final_grad = by_half(mine, across(theirs), 1)[:, :, None]
    return (
        final_stream,
        final_grad,
        grad_qkv,
        grad_beta,
        grad_taps,
        grad_out,
        grad_gate_up,
        grad_down,
        grad_gains,
        grad_out_gains[0],
    )


def solution(mesh):
    in_specs = (
        P(None, "dp", None, None),
        P(None, "dp", None, None),
        P(None, None, "section"),
        P(None, "section"),
        P(None, None, "section"),
        P("section", None),
        P(None, None, "section"),
        P("section", None),
        P(None, "section"),
        P("section"),
    )
    out_specs = (
        P(None, "dp", None, "section"),
        P(None, "dp", None, "section"),
        P(None, "dp", "section"),
        P("dp", "section"),
        P(None, None, ("section", "dp")),
        P(("section", "dp"), None),
        P(None, "dp", "section"),
        P(("section", "dp"), None),
        P(None, ("section", "dp")),
        P(("section", "dp")),
    )
    return jax.shard_map(local, mesh=mesh, in_specs=in_specs, out_specs=out_specs, check_vma=False)
```
